128 devices in a mesh: fsdp: 4 (over x), ctx: 16 (over z_hi, y, core), tp: 2 (over z_lo).
Axes of the slice: x: 4, y: 4, z: 4 (z_hi: 2, z_lo: 2; z = z_hi * 2 + z_lo), core: 2. Of those that a mesh axis runs over, the one named last changes fastest.
Arguments:
- tokens: bfloat16 [4, 4096, 1024], P('fsdp', 'ctx'), may hold values from -12 to 12, as said below
- ln1_gain: bfloat16 [1024], P(('fsdp', 'ctx')), may hold values from 0.5 to 1.5
- ln1_bias: bfloat16 [1024], P(('fsdp', 'ctx')), may hold values from -1.5 to 1.5
- qkv_weight: bfloat16 [1024, 3, 1024], P(('fsdp', 'ctx'), None, 'tp'), may hold values from -0.1875 to 0.1875
- qv_bias: bfloat16 [2, 1024], P(None, 'tp'), may hold values from -1.5 to 1.5
- proj_weight: bfloat16 [1024, 1024], P('tp', ('fsdp', 'ctx')), may hold values from -0.75 to 0.75
- proj_bias: bfloat16 [1024], P(('fsdp', 'ctx')), may hold values from -1.5 to 1.5
- ln2_gain: bfloat16 [1024], P(('fsdp', 'ctx')), may hold values from 0.5 to 1.5
- ln2_bias: bfloat16 [1024], P(('fsdp', 'ctx')), may hold values from -1.5 to 1.5
- fc_weight: bfloat16 [1024, 4096], P(('fsdp', 'ctx'), 'tp'), may hold values from -0.1875 to 0.1875
- fc_bias: bfloat16 [4096], P('tp'), may hold values from -2.5 to 2.5
- out_weight: bfloat16 [4096, 1024], P('tp', ('fsdp', 'ctx')), may hold values from -0.09375 to 0.09375
- out_bias: bfloat16 [1024], P(('fsdp', 'ctx')), may hold values from -1.5 to 1.5
- piece_starts: int32 [4, 2], P('fsdp'), may hold values from 0 to 3840, as said below
- seq_lengths: int32 [4], replicated, may hold values from 3968 to 4096, as said below
- cotangent: bfloat16 [4, 4096, 1024], P('fsdp', 'ctx'), may hold values from -6 to 6
Outputs:
- layer_out: bfloat16 [4, 4096, 1024], P('fsdp', 'ctx')
- grad_tokens: bfloat16 [4, 4096, 1024], P('fsdp', 'ctx')
- grad_ln1_gain: float32 [1024], P(('fsdp', 'ctx'))
- grad_ln1_bias: float32 [1024], P(('fsdp', 'ctx'))
- grad_qkv: float32 [1024, 3, 1024], P(('fsdp', 'ctx'), None, 'tp')
- grad_qv_bias: float32 [2, 1024], P(None, 'tp')
- grad_proj: float32 [1024, 1024], P('tp', ('fsdp', 'ctx'))
- grad_proj_bias: float32 [1024], P(('fsdp', 'ctx'))
- grad_ln2_gain: float32 [1024], P(('fsdp', 'ctx'))
- grad_ln2_bias: float32 [1024], P(('fsdp', 'ctx'))
- grad_fc: float32 [1024, 4096], P(('fsdp', 'ctx'), 'tp')
- grad_fc_bias: float32 [4096], P('tp')
- grad_out: float32 [4096, 1024], P('tp', ('fsdp', 'ctx'))
- grad_out_bias: float32 [1024], P(('fsdp', 'ctx'))
- root_squares: float32 [4], replicated
The draws below stay inside these ranges and needn't reach their ends.
Inputs may be any that keep to these rules, and one draw needn't show every extreme that they name: `tokens`: each row is a value drawn near zero scaled by a factor that depends on the row. `piece_starts`: piece k of a sequence starts at k * (2048) or later and ends by (k + 1) * 2048; pieces never intersect. `seq_lengths`: some sequence is full in every draw.
All inputs are finite; a program needn't handle non-finite values.
Results may differ from the reference program's by a relative error of at most 0.02.
Values may be sent and summed in bfloat16 or wider, within the bound.
No kernel may reach another device: no remote copies, remote signals or barrier semaphores. Data moves between devices by JAX's collectives and lax.ppermute only.
A program may use at most 128 MiB of HBM per device.

```python
import jax
import jax.numpy as jnp
from jax import lax

D = 1024
HEADS = 16
HEAD = 64
FF = 4096
TOK_DEV = 256
PIECE = 256
PIECES = 2
SEQ_LEN = 4096
SEQS = 4
TOKENS = 16384


def draw_tokens(key, part):
    key = jax.random.fold_in(key, 11)
    base_key, jitter_key = jax.random.split(key)
    base = jnp.clip(jax.random.normal(base_key, (TOKENS, D), jnp.float32), -4.0, 4.0)
    rising = 0.6 * jnp.exp(jnp.log(3.0) * jnp.arange(TOKENS, dtype=jnp.float32) / TOKENS)
    jitter = jnp.exp(jax.random.uniform(jitter_key, (TOKENS, 1), jnp.float32, -0.5, 0.5))
    return (base * rising[:, None] * jitter).reshape(SEQS, SEQ_LEN, D).astype(jnp.bfloat16)


def draw_piece_starts(key, part):
    key = jax.random.fold_in(key, 23)
    offset_key, chosen_key = jax.random.split(key)
    region = SEQ_LEN // PIECES
    room = region - PIECE + 1
    offsets = jax.random.randint(offset_key, (SEQS, PIECES), 0, room)
    chosen = jax.random.randint(chosen_key, (), 0, SEQS)
    column = jnp.arange(PIECES, dtype=jnp.int32)
    forced = jnp.where(column == 0, 0, jnp.where(column == PIECES - 1, room - 1, offsets[chosen]))
    offsets = jnp.where((jnp.arange(SEQS) == chosen)[:, None], forced[None, :], offsets)
    return (offsets + column[None, :] * region).astype(jnp.int32)


def draw_seq_lengths(key, part):
    key = jax.random.fold_in(key, 37)
    tail_key, order_key = jax.random.split(key)
    tails = jax.random.randint(tail_key, (SEQS,), 0, TOK_DEV // 2 + 1)
    order = jax.random.permutation(order_key, SEQS)
    index_row = jnp.arange(SEQS)
    tails = jnp.where(index_row == order[0], 0, tails)
    tails = jnp.where(index_row == order[1], TOK_DEV // 2, tails)
    return (SEQ_LEN - tails).astype(jnp.int32)


def block_scale(rng, dims, cuts, smallest, high):
    def one(axis_at, parts):
        heights = jax.random.uniform(jax.random.fold_in(jax.random.fold_in(rng, 6), axis_at), (parts,), jnp.float32, smallest / len(cuts), high / len(cuts))
        return jnp.repeat(jnp.exp(heights), dims[axis_at] // parts).reshape((-1,) + (1,) * (len(dims) - axis_at - 1))

    level = one(*cuts[0])
    for cut in cuts[1:]:
        level = level * one(*cut)
    return level


def scatter_about(key, extent, scale, limit, cuts=(), held_as=jnp.bfloat16):
    loudness = block_scale(key, extent, cuts, -0.22, 0.18) if cuts else 1.0
    result = jax.random.normal(key, extent, jnp.float32) * scale * loudness
    return jnp.minimum(jnp.maximum(result, -limit), limit).astype(held_as)


def setup_inputs(seed: int = 0) -> dict:
    seeds = jax.random.split(jax.random.key(seed), 17)
    return {
        "tokens": draw_tokens(jax.random.fold_in(seeds[16], 71), 0),
        "ln1_gain": jnp.clip(1.0 + 0.1 * jax.random.normal(seeds[1], (D,), jnp.float32), 0.5, 1.5).astype(jnp.bfloat16),
        "ln1_bias": scatter_about(seeds[2], (D,), 0.3, 1.5, ((0, 64),)),
        "qkv_weight": scatter_about(seeds[3], (D, 3, D), D ** -0.5, 0.1875, ((0, 64), (2, 2))),
        "qv_bias": scatter_about(seeds[4], (2, D), 0.3, 1.5, ((1, 2),)),
        "proj_weight": scatter_about(seeds[5], (D, D), (D // 16) ** -0.5, 0.75, ((0, 2), (1, 64))),
        "proj_bias": scatter_about(seeds[6], (D,), 0.3, 1.5, ((0, 64),)),
        "ln2_gain": jnp.clip(1.0 + 0.1 * jax.random.normal(seeds[7], (D,), jnp.float32), 0.5, 1.5).astype(jnp.bfloat16),
        "ln2_bias": scatter_about(seeds[8], (D,), 0.3, 1.5, ((0, 64),)),
        "fc_weight": scatter_about(seeds[9], (D, FF), D ** -0.5, 0.1875, ((0, 64), (1, 2))),
        "fc_bias": scatter_about(seeds[10], (FF,), 0.5, 2.5, ((0, 2),)),
        "out_weight": scatter_about(seeds[11], (FF, D), FF ** -0.5, 0.09375, ((0, 2), (1, 64))),
        "out_bias": scatter_about(seeds[12], (D,), 0.3, 1.5, ((0, 64),)),
        "piece_starts": draw_piece_starts(jax.random.fold_in(seeds[16], 71), 0),
        "seq_lengths": draw_seq_lengths(jax.random.fold_in(seeds[16], 71), 0),
        "cotangent": scatter_about(seeds[15], (SEQS, SEQ_LEN, D), 1.0, 6.0, ((0, 4), (1, 16))),
    }


NORM_EPS = 1e-05
ROOT_EPS = 1e-06
MASKED = -1e+30
HIGHEST = lax.Precision.HIGHEST

@jax.custom_vjp
def low(v):
    return lax.optimization_barrier(v.astype(jnp.bfloat16)).astype(jnp.float32)

@jax.custom_vjp
def low_back(v):
    return v

def low_keep(v):
    return (low(v), None)

def low_pass(kept, grad):
    return (grad,)

def back_keep(v):
    return (v, None)

def back_low(kept, grad):
    return (low(grad),)
low.defvjp(low_keep, low_pass)
low_back.defvjp(back_keep, back_low)

def layer_norm(values, gain, shift):
    center = values - lax.optimization_barrier(jnp.mean(values, axis=-1, keepdims=True))
    spread = lax.optimization_barrier(jnp.mean(center * center, axis=-1, keepdims=True))
    return center * lax.rsqrt(spread + NORM_EPS) * gain + shift

def piece_number(positions, starts):
    inside = (positions[:, None] >= starts[None, :]) & (positions[:, None] < starts[None, :] + PIECE)
    labels = jnp.arange(1, starts.shape[0] + 1, dtype=jnp.int32)
    return lax.optimization_barrier(jnp.sum(jnp.where(inside, labels[None, :], 0), axis=1)).astype(jnp.int32)

def visible(query_pos, query_piece, key_pos, key_piece, length):
    causal = key_pos[None, :] <= query_pos[:, None]
    shared = (query_piece[:, None] == key_piece[None, :]) & (query_piece[:, None] > 0)
    return (key_pos[None, :] < length) & (causal | shared)

def attend_sequence(queries, key_rows, value_rows, starts, length):
    positions = jnp.arange(SEQ_LEN, dtype=jnp.int32)
    pieces = piece_number(positions, starts)
    block_rows = min(512, SEQ_LEN)

    def one_block(block_start):
        query_block = lax.dynamic_slice_in_dim(queries, block_start, block_rows, 0)
        query_pos = block_start + jnp.arange(block_rows, dtype=jnp.int32)
        query_piece = lax.dynamic_slice_in_dim(pieces, block_start, block_rows, 0)
        scaled = low_back(jnp.einsum('qhe,khe->hqk', query_block, key_rows, precision=HIGHEST)) * 0.125
        allowed = visible(query_pos, query_piece, positions, pieces, length)
        attn_probs = low(jax.nn.softmax(jnp.where(allowed[None], scaled, MASKED), axis=-1))
        return jnp.einsum('hqk,khe->qhe', attn_probs, value_rows, precision=HIGHEST)
    block_starts = jnp.arange(SEQ_LEN // block_rows, dtype=jnp.int32) * block_rows
    outputs = lax.map(jax.checkpoint(one_block), block_starts)
    return outputs.reshape(SEQ_LEN, HEADS, HEAD)

def by_sequence(field):
    return field.reshape(SEQS, SEQ_LEN, HEADS, HEAD)

def reference(tokens, ln1_gain, ln1_bias, qkv_weight, qv_bias, proj_weight, proj_bias, ln2_gain, ln2_bias, fc_weight, fc_bias, out_weight, out_bias, piece_starts, seq_lengths, cotangent):

    def attend_items(items):
        return attend_sequence(items[0], items[1], items[2], items[3], items[4])

    def forward(token_block, gain_one, shift_one, w_qkv, b_qv, w_proj, b_proj, gain_two, shift_two, w_fc, b_fc, w_out, b_out):
        inputs = token_block.reshape(TOKENS, D)
        normed = low(layer_norm(inputs, gain_one, shift_one))
        project = jnp.einsum('td,dcn->tcn', normed, w_qkv, precision=HIGHEST)
        queries = low_back(low(project[:, 0] + b_qv[0]))
        key_rows = low_back(low(project[:, 1]))
        value_rows = low_back(low(project[:, 2] + b_qv[1]))
        mixed = lax.map(attend_items, (by_sequence(queries), by_sequence(key_rows), by_sequence(value_rows), piece_starts, seq_lengths))
        heads_out = low_back(low(mixed.reshape(TOKENS, D)))
        attn_out = low_back(jnp.dot(heads_out, w_proj, precision=HIGHEST) + b_proj)
        middle = inputs + attn_out
        normed_two = low(layer_norm(middle, gain_two, shift_two))
        hidden = low_back(jnp.dot(normed_two, w_fc, precision=HIGHEST) + b_fc)
        activated = low(jax.nn.gelu(hidden, approximate=True))
        mlp_out = low_back(jnp.dot(activated, w_out, precision=HIGHEST) + b_out)
        return ((middle + mlp_out).reshape(SEQS, SEQ_LEN, D), (attn_out, mlp_out))
    floats = tuple((array_in.astype(jnp.float32) for array_in in (tokens, ln1_gain, ln1_bias, qkv_weight, qv_bias, proj_weight, proj_bias, ln2_gain, ln2_bias, fc_weight, fc_bias, out_weight, out_bias)))
    final, backward, (attn_out, mlp_out) = jax.vjp(forward, *floats, has_aux=True)
    positions = jnp.arange(SEQ_LEN, dtype=jnp.int32)
    valid_grid = (positions[None, :] < seq_lengths[:, None]).astype(jnp.float32)
    gradients = backward(cotangent.astype(jnp.float32) * valid_grid[:, :, None])
    valid_rows = valid_grid.reshape(TOKENS)
    valid_total = jnp.sum(valid_rows) * D

    def mean_square(field):
        return jnp.sum(valid_rows * lax.optimization_barrier(jnp.sum(field * field, axis=1))) / valid_total
    root_squares = jnp.sqrt(jnp.stack([mean_square(floats[0].reshape(TOKENS, D)), mean_square(attn_out), mean_square(mlp_out), mean_square(final.reshape(TOKENS, D))]) + ROOT_EPS)
    return (final.astype(jnp.bfloat16), gradients[0].astype(jnp.bfloat16), gradients[1], gradients[2], gradients[3], gradients[4], gradients[5], gradients[6], gradients[7], gradients[8], gradients[9], gradients[10], gradients[11], gradients[12], root_squares)
```

```python
import jax
import jax.numpy as jnp
from jax import lax
from jax.experimental import pallas as pl
from jax.experimental.pallas import tpu as pltpu
from jax.sharding import Mesh
from jax.sharding import PartitionSpec as P

f32 = jnp.float32
bf16 = jnp.bfloat16
NORM_EPS = 1e-05
ROOT_EPS = 1e-06
B=256; E=64; NB=16; MASKED=-1e30; PIECE=256

def piece_of(pos, info_ref):
    n0=(pos>=info_ref[2])&(pos<info_ref[2]+PIECE)
    n1=(pos>=info_ref[3])&(pos<info_ref[3]+PIECE)
    return jnp.where(n0,1,0)+jnp.where(n1,2,0)

def allowed_block(key_block, query_block, info_ref):
    kpos=key_block*B+lax.broadcasted_iota(jnp.int32,(B,1),0)
    qpos=query_block*B+lax.broadcasted_iota(jnp.int32,(1,B),1)
    kp=piece_of(kpos,info_ref); qp=piece_of(qpos,info_ref)
    qp=jnp.where(qp==0,-1,qp)
    kp=jnp.where(kpos<info_ref[1],kp,-2)
    kpos=jnp.where(kpos<info_ref[1],kpos,1<<20)
    return (kpos<=qpos)|(kp==qp)

def extra_blocks(p, info_ref):
    edge=(2*p+2)*B
    crosses=((info_ref[2]<edge)&(edge<info_ref[2]+PIECE))|((info_ref[3]<edge)&(edge<info_ref[3]+PIECE))
    return jnp.where((info_ref[0]==1)&(p<NB//2-1)&crosses,1,0)

def dot(a,b): return jnp.dot(a,b,preferred_element_type=f32)

def forward_kernel(info_ref, own_ref, other_ref, out_ref, low_ref, lse_ref, key_ref, value_ref):
    core=info_ref[0]
    def stage(p,_):
        key_ref[2*p+core]=own_ref[p,E:2*E,:].T
        value_ref[2*p+core]=own_ref[p,2*E:,:]
        key_ref[2*p+1-core]=other_ref[p,:E,:].T
        value_ref[2*p+1-core]=other_ref[p,E:,:]
        return 0
    lax.fori_loop(0,NB//2,stage,0)
    def one(p,_):
        query=own_ref[p,:E,:]*jnp.asarray(0.125,bf16)
        qb=2*p+core
        def step(blocks,masked,carry):
            top,total,acc=carry
            scores=[dot(key_ref[j],query) for j in blocks]
            if masked: scores=[jnp.where(allowed_block(j,qb,info_ref),s,MASKED) for j,s in zip(blocks,scores)]
            new=top
            for s in scores: new=jnp.maximum(new,jnp.max(s,axis=0,keepdims=True))
            scale=jnp.exp(top-new)
            total=total*scale; acc=acc*scale
            for j,s in zip(blocks,scores):
                e=jnp.exp(s-new)
                total=total+jnp.sum(e,axis=0,keepdims=True)
                acc=acc+dot(value_ref[j],e.astype(bf16))
            return new,total,acc
        carry=(jnp.full((1,B),MASKED,f32),jnp.zeros((1,B),f32),jnp.zeros((E,B),f32))
        carry=step((2*p,2*p+1),True,carry)
        carry=lax.fori_loop(0,p,lambda i,c: step((2*i,2*i+1),False,c),carry)
        carry=lax.fori_loop(0,extra_blocks(p,info_ref),lambda i,c: step((2*p+2,),True,c),carry)
        top,total,acc=carry
        o=acc/total
        out_ref[p]=o
        low_ref[p]=o.astype(bf16)
        lse_ref[p]=top+jnp.log(total)
        return 0
    lax.fori_loop(0,NB//2,one,0)

def backward_kernel(info_ref, own_ref, other_ref, gout_ref, out_ref, lse_ref, gq_ref, gown_ref, gother_ref,
                    key_ref, keyt_ref, value_ref, gk_ref, gv_ref):
    core=info_ref[0]
    def stage(p,_):
        a=own_ref[p,E:2*E,:]; b=other_ref[p,:E,:]
        keyt_ref[2*p+core]=a; keyt_ref[2*p+1-core]=b
        key_ref[2*p+core]=a.T; key_ref[2*p+1-core]=b.T
        value_ref[2*p+core]=own_ref[p,2*E:,:].T
        value_ref[2*p+1-core]=other_ref[p,E:,:].T
        return 0
    lax.fori_loop(0,NB//2,stage,0)
    gk_ref[...]=jnp.zeros_like(gk_ref); gv_ref[...]=jnp.zeros_like(gv_ref)
    def one(p,_):
        query=own_ref[p,:E,:]*jnp.asarray(0.125,bf16)
        rows=query.T
        gout=gout_ref[p]; gout_rows=gout.T
        lse=lse_ref[p]
        delta=jnp.sum(gout.astype(f32)*out_ref[p],axis=0,keepdims=True)
        qb=2*p+core
        def step(blocks,masked,acc):
            for j in blocks:
                s=dot(key_ref[j],query)
                if masked: s=jnp.where(allowed_block(j,qb,info_ref),s,MASKED)
                e=jnp.exp(s-lse)
                gp=dot(value_ref[j],gout)
                gs=(e*(gp-delta)).astype(bf16)
                gv_ref[j]+=dot(e.astype(bf16),gout_rows)
                gk_ref[j]+=dot(gs,rows)
                acc=acc+dot(keyt_ref[j],gs)
            return acc
        acc=step((2*p,2*p+1),True,jnp.zeros((E,B),f32))
        acc=lax.fori_loop(0,p,lambda i,c: step((2*i,2*i+1),False,c),acc)
        acc=lax.fori_loop(0,extra_blocks(p,info_ref),lambda i,c: step((2*p+2,),True,c),acc)
        gq_ref[p]=(acc*0.125).astype(bf16)
        return 0
    lax.fori_loop(0,NB//2,one,0)
    def finish(p,_):
        gown_ref[p,:E,:]=gk_ref[2*p+core].T
        gown_ref[p,E:,:]=gv_ref[2*p+core].T
        gother_ref[p,:E,:]=gk_ref[2*p+1-core].T.astype(bf16)
        gother_ref[p,E:,:]=gv_ref[2*p+1-core].T.astype(bf16)
        return 0
    lax.fori_loop(0,NB//2,finish,0)

VM=pl.BlockSpec(memory_space=pltpu.VMEM); SM=pl.BlockSpec(memory_space=pltpu.SMEM)
LIMIT=48*1024*1024
def attn_forward(info,own,other):
    H=NB//2
    return pl.pallas_call(forward_kernel,
        out_shape=(jax.ShapeDtypeStruct((H,E,B),f32),jax.ShapeDtypeStruct((H,E,B),bf16),jax.ShapeDtypeStruct((H,1,B),f32)),
        in_specs=[SM,VM,VM],out_specs=(VM,VM,VM),
        scratch_shapes=[pltpu.VMEM((NB,B,E),bf16),pltpu.VMEM((NB,E,B),bf16)],
        compiler_params=pltpu.CompilerParams(vmem_limit_bytes=LIMIT),
        cost_estimate=pl.CostEstimate(flops=2*2*B*B*E*72,bytes_accessed=3<<20,transcendentals=B*B*72),
        name="attention_forward")(info,own,other)
def attn_backward(info,own,other,gout,out,lse):
    H=NB//2
    return pl.pallas_call(backward_kernel,
        out_shape=(jax.ShapeDtypeStruct((H,E,B),bf16),jax.ShapeDtypeStruct((H,2*E,B),f32),jax.ShapeDtypeStruct((H,2*E,B),bf16)),
        in_specs=[SM]+[VM]*5,out_specs=(VM,VM,VM),
        scratch_shapes=[pltpu.VMEM((NB,B,E),bf16),pltpu.VMEM((NB,E,B),bf16),pltpu.VMEM((NB,B,E),bf16),pltpu.VMEM((NB,B,E),f32),pltpu.VMEM((NB,B,E),f32)],
        compiler_params=pltpu.CompilerParams(vmem_limit_bytes=LIMIT),
        cost_estimate=pl.CostEstimate(flops=5*2*B*B*E*72,bytes_accessed=5<<20,transcendentals=B*B*72),
        name="attention_backward")(info,own,other,gout,out,lse)


CORE = ("c",)
SPREAD = ("x", "zh", "y")
LINE = ("zh", "y")


def low(field):
    return field.astype(bf16)


def swap(field, axis):
    return lax.ppermute(field, axis, [(0, 1), (1, 0)])


def exchange(field, axes):
    return lax.all_to_all(field, axes, split_axis=0, concat_axis=0, tiled=True)


def spread_out(field):
    return exchange(jnp.broadcast_to(field[None], (32,) + field.shape), SPREAD)


def after(field, *others):
    return lax.optimization_barrier((field, *others))[0]


def contract(a, b, dim_a, dim_b):
    return lax.dot_general(a, b, (((dim_a,), (dim_b,)), ((), ())), preferred_element_type=f32)


def feature_order(core):
    place = jnp.arange(1024, dtype=jnp.int32)
    half = place // 512
    group = (place % 512) // 16
    feature = (group * 2 + jnp.where(half == 0, core, 1 - core)) * 16 + place % 16
    return low(jnp.arange(1024, dtype=jnp.int32)[:, None] == feature[None, :])


def norm_parts(values):
    center = values - jnp.mean(values, axis=-1, keepdims=True)
    inverse = lax.rsqrt(jnp.mean(center * center, axis=-1, keepdims=True) + NORM_EPS)
    return center * inverse, inverse


def norm_back(grad, gain, norm, inverse):
    scaled = grad * gain
    return inverse * (
        scaled
        - jnp.mean(scaled, axis=-1, keepdims=True)
        - norm * jnp.mean(scaled * norm, axis=-1, keepdims=True)
    )


def gelu_pair(u):
    k = 0.7978845608028654
    t = jnp.tanh(k * (u + 0.044715 * u * u * u))
    value = 0.5 * u * (1.0 + t)
    slope = 0.5 * (1.0 + t) + 0.5 * u * (1.0 - t * t) * k * (1.0 + 3 * 0.044715 * u * u)
    return value, slope


def body(
    tokens,
    ln1_gain,
    ln1_bias,
    qkv_weight,
    qv_bias,
    proj_weight,
    proj_bias,
    ln2_gain,
    ln2_bias,
    fc_weight,
    fc_bias,
    out_weight,
    out_bias,
    piece_starts,
    seq_lengths,
    cotangent,
):
    core = lax.axis_index("c")
    line = lax.axis_index(LINE)
    length = lax.dynamic_index_in_dim(seq_lengths, lax.axis_index("x"), 0, False)
    info = jnp.stack([core.astype(jnp.int32), length, piece_starts[0, 0], piece_starts[0, 1]])

    small = jnp.stack([ln1_gain, ln1_bias, proj_bias, ln2_gain, ln2_bias, out_bias], axis=1)
    small = jnp.pad(small, ((0, 0), (0, 122)))
    pay_q = jnp.concatenate([qkv_weight.reshape(16, 1536), small], axis=1)
    own_q = spread_out(pay_q).reshape(512, 1664)
    pay_r = jnp.concatenate([proj_weight.T, fc_weight, out_weight.T], axis=1)
    own_r = spread_out(after(pay_r, own_q)).reshape(512, 4608)
    all_q = jnp.concatenate([own_q, swap(own_q, "c")], axis=0)
    w_qkv = all_q[:, :1536]
    vectors = all_q[:, 1536:1544].astype(f32).T
    gain_one, shift_one, b_proj, gain_two, shift_two, b_out = [vectors[i : i + 1] for i in range(6)]

    order = feature_order(core)
    inputs = jnp.dot(tokens[0], order, preferred_element_type=f32)
    position = (line * 2 + core) * 256 + jnp.arange(256, dtype=jnp.int32)
    valid = (position < length).astype(f32)[:, None]
    grad_final = jnp.dot(cotangent[0], order, preferred_element_type=f32) * valid
    grad_mlp = low(grad_final)

    norm_one, inv_one = norm_parts(inputs)
    normed = low(norm_one * gain_one + shift_one)
    bias = qv_bias.astype(f32)
    bias3 = jnp.concatenate([bias[0], jnp.zeros((512,), f32), bias[1]])
    project = low(contract(w_qkv, normed, 0, 1) + bias3[:, None])
    heads = project.reshape(3, 8, 64, 256).transpose(1, 0, 2, 3).reshape(8, 192, 256)
    own = exchange(heads, LINE)
    other = swap(own[:, 64:], "c")
    attended, attended_low, log_sum = attn_forward(info, own, other)
    heads_out = exchange(attended_low, LINE).reshape(512, 256)

    all_r = jnp.concatenate([own_r, swap(own_r, "c")], axis=0)
    w_proj = all_r[:, :512]
    w_fc = all_r[:, 512:2560]
    w_out = all_r[:, 2560:]

    attn_part = low(contract(heads_out, w_proj, 0, 1))
    attn_out = attn_part.astype(f32) + swap(attn_part, "tp").astype(f32) + b_proj
    middle = inputs + attn_out
    norm_two, inv_two = norm_parts(middle)
    normed_two = low(norm_two * gain_two + shift_two)
    hidden = jnp.dot(normed_two, w_fc, preferred_element_type=f32) + fc_bias.astype(f32)
    value, slope = gelu_pair(hidden)
    activated = low(value)
    grad_act = jnp.dot(grad_mlp, w_out, preferred_element_type=f32)
    grad_hidden = low(grad_act * slope)
    norm_two_part = low(contract(grad_hidden, w_fc, 1, 1))
    grad_norm_two = norm_two_part.astype(f32) + swap(norm_two_part, "tp").astype(f32)
    mlp_part = low(contract(activated, w_out, 1, 1))
    mlp_out = mlp_part.astype(f32) + swap(mlp_part, "tp").astype(f32) + b_out
    final = middle + mlp_out

    grad_middle = grad_final + norm_back(grad_norm_two, gain_two, norm_two, inv_two)
    grad_attn = low(grad_middle)
    grad_heads = low(contract(w_proj, grad_attn, 0, 1)).reshape(8, 64, 256)
    grad_mine = exchange(grad_heads, LINE)
    grad_query, grad_own, grad_other = attn_backward(
        info, own, other, grad_mine, attended, log_sum
    )

    grad_proj = contract(grad_attn, heads_out, 0, 1)
    grad_fc = contract(normed_two, grad_hidden, 0, 0)
    grad_out = contract(grad_mlp, activated, 0, 0)

    def squares(field):
        return jnp.sum(valid * field * field)

    roots = jnp.stack([squares(inputs), squares(attn_out), squares(mlp_out), squares(final)])
    columns = jnp.stack(
        [
            jnp.sum(grad_attn.astype(f32), axis=0),
            jnp.sum(grad_norm_two * norm_two, axis=0),
            jnp.sum(grad_norm_two, axis=0),
            jnp.sum(grad_mlp.astype(f32), axis=0),
        ],
        axis=1,
    )
    fc_sums = jnp.sum(grad_hidden.astype(f32), axis=0).reshape(16, 128)
    shared = jnp.concatenate([fc_sums, jnp.broadcast_to(roots[None], (16, 4))], axis=1)
    shared = jnp.broadcast_to(shared[None], (64, 16, 132)).reshape(1024, 132)
    pay_g = jnp.concatenate(
        [grad_proj, grad_fc, grad_out, shared, columns, jnp.zeros((1024, 120), f32)], axis=1
    )

    def scatter(pay):
        mine, theirs = pay[:512], low(pay[512:])
        both = low(mine + swap(theirs, "c").astype(f32))
        got = exchange(both.reshape(32, 16, -1), SPREAD)
        return jnp.sum(got.astype(f32), axis=0)

    got_g = scatter(pay_g)

    grad_kv = low(grad_own + swap(grad_other, "c").astype(f32))
    grad_back = exchange(jnp.concatenate([grad_query, grad_kv], axis=1), LINE)
    grad_project = grad_back.reshape(8, 3, 64, 256).transpose(1, 0, 2, 3).reshape(1536, 256)
    norm_one_part = low(contract(grad_project, w_qkv, 0, 1))
    grad_normed = norm_one_part.astype(f32) + swap(norm_one_part, "tp").astype(f32)
    grad_inputs = grad_middle + norm_back(grad_normed, gain_one, norm_one, inv_one)

    grad_qkv = contract(normed, grad_project, 0, 1)
    part = norm_one_part.astype(f32)
    columns = jnp.stack([jnp.sum(part * norm_one, axis=0), jnp.sum(part, axis=0)], axis=1)
    sums = jnp.sum(grad_project.astype(f32), axis=1)
    sums = jnp.concatenate([sums[:512], sums[1024:]]).reshape(16, 64)
    sums = jnp.broadcast_to(sums[None], (64, 16, 64)).reshape(1024, 64)
    got_q = scatter(
        jnp.concatenate([grad_qkv, sums, columns, jnp.zeros((1024, 62), f32)], axis=1)
    )

    ln1 = got_q[:, 1600:1602]
    ln1 = ln1 + swap(ln1, "tp")
    root_sum = got_g[0, 4736:4740]
    valid_total = jnp.sum(seq_lengths).astype(f32)
    root_squares = jnp.sqrt(root_sum / (valid_total * 1024) + ROOT_EPS)
    return (
        low(contract(low(final), order, 1, 1))[None],
        low(contract(low(grad_inputs), order, 1, 1))[None],
        ln1[:, 0],
        ln1[:, 1],
        got_q[:, :1536].reshape(16, 3, 512),
        got_q[:, 1536:1600].reshape(2, 512),
        got_g[:, :512].T,
        got_g[:, 4740],
        got_g[:, 4741],
        got_g[:, 4742],
        got_g[:, 512:2560],
        got_g[:, 4608:4736].reshape(2048),
        got_g[:, 2560:4608].T,
        got_g[:, 4743],
        root_squares,
    )


def solution(mesh):
    fine = Mesh(mesh.devices.reshape(4, 2, 4, 2, 2), ("x", "zh", "y", "c", "tp"))
    ctx = ("zh", "y", "c")
    every = ("x", "zh", "y", "c")
    in_specs = (
        P("x", ctx, None),
        P(every),
        P(every),
        P(every, None, "tp"),
        P(None, "tp"),
        P("tp", every),
        P(every),
        P(every),
        P(every),
        P(every, "tp"),
        P("tp"),
        P("tp", every),
        P(every),
        P("x", None),
        P(),
        P("x", ctx, None),
    )
    out_specs = (
        P("x", ctx, None),
        P("x", ctx, None),
        P(every),
        P(every),
        P(every, None, "tp"),
        P(None, "tp"),
        P("tp", every),
        P(every),
        P(every),
        P(every),
        P(every, "tp"),
        P("tp"),
        P("tp", every),
        P(every),
        P(),
    )
    return jax.shard_map(body, mesh=fine, in_specs=in_specs, out_specs=out_specs, check_vma=False)
```

```python
from functools import partial

import jax
import jax.numpy as jnp
from jax import lax
from jax.experimental import pallas as pl
from jax.experimental.pallas import tpu as pltpu
from jax.sharding import Mesh
from jax.sharding import PartitionSpec as P

f32 = jnp.float32
bf16 = jnp.bfloat16
NORM_EPS = 1e-05
ROOT_EPS = 1e-06
B=256; E=64; NB=16; MASKED=-1e30; PIECE=256

class Facts:
    def __init__(self, lengths_ref, starts_ref):
        self.core = lax.axis_index("c")
        self.items = (self.core, lengths_ref[lax.axis_index("x")], starts_ref[0, 0], starts_ref[0, 1])

    def __getitem__(self, at):
        return self.items[at]


def piece_of(pos, info_ref):
    n0=(pos>=info_ref[2])&(pos<info_ref[2]+PIECE)
    n1=(pos>=info_ref[3])&(pos<info_ref[3]+PIECE)
    return jnp.where(n0,1,0)+jnp.where(n1,2,0)

def allowed_block(key_block, query_block, info_ref):
    kpos=key_block*B+lax.broadcasted_iota(jnp.int32,(B,1),0)
    qpos=query_block*B+lax.broadcasted_iota(jnp.int32,(1,B),1)
    kp=piece_of(kpos,info_ref); qp=piece_of(qpos,info_ref)
    qp=jnp.where(qp==0,-1,qp)
    kp=jnp.where(kpos<info_ref[1],kp,-2)
    kpos=jnp.where(kpos<info_ref[1],kpos,1<<20)
    return (kpos<=qpos)|(kp==qp)

def extra_blocks(p, info_ref):
    edge=(2*p+2)*B
    crosses=((info_ref[2]<edge)&(edge<info_ref[2]+PIECE))|((info_ref[3]<edge)&(edge<info_ref[3]+PIECE))
    return jnp.where((info_ref[0]==1)&(p<NB//2-1)&crosses,1,0)

def dot(a,b): return jnp.dot(a,b,preferred_element_type=f32)

def forward_kernel(lengths_ref, starts_ref, own_ref, other_ref, out_ref, low_ref, lse_ref, key_ref, value_ref):
    info_ref=Facts(lengths_ref,starts_ref)
    core=info_ref[0]
    def stage(p,_):
        key_ref[2*p+core]=own_ref[p,E:2*E,:].T
        value_ref[2*p+core]=own_ref[p,2*E:,:]
        key_ref[2*p+1-core]=other_ref[p,:E,:].T
        value_ref[2*p+1-core]=other_ref[p,E:,:]
        return 0
    lax.fori_loop(0,NB//2,stage,0)
    def one(p,_):
        query=own_ref[p,:E,:]*jnp.asarray(0.125,bf16)
        qb=2*p+core
        def step(blocks,masked,carry):
            top,total,acc=carry
            scores=[dot(key_ref[j],query) for j in blocks]
            if masked: scores=[jnp.where(allowed_block(j,qb,info_ref),s,MASKED) for j,s in zip(blocks,scores)]
            new=top
            for s in scores: new=jnp.maximum(new,jnp.max(s,axis=0,keepdims=True))
            scale=jnp.exp(top-new)
            total=total*scale; acc=acc*scale
            for j,s in zip(blocks,scores):
                e=jnp.exp(s-new)
                total=total+jnp.sum(e,axis=0,keepdims=True)
                acc=acc+dot(value_ref[j],e.astype(bf16))
            return new,total,acc
        carry=(jnp.full((1,B),MASKED,f32),jnp.zeros((1,B),f32),jnp.zeros((E,B),f32))
        carry=step((2*p,2*p+1),True,carry)
        carry=lax.fori_loop(0,p,lambda i,c: step((2*i,2*i+1),False,c),carry)
        carry=lax.fori_loop(0,extra_blocks(p,info_ref),lambda i,c: step((2*p+2,),True,c),carry)
        top,total,acc=carry
        o=acc/total
        out_ref[p]=o
        low_ref[p]=o.astype(bf16)
        lse_ref[p]=top+jnp.log(total)
        return 0
    lax.fori_loop(0,NB//2,one,0)

def backward_kernel(lengths_ref, starts_ref, own_ref, other_ref, gout_ref, out_ref, lse_ref, gq_ref, gown_ref, gother_ref,
                    key_ref, keyt_ref, value_ref, gk_ref, gv_ref):
    info_ref=Facts(lengths_ref,starts_ref)
    core=info_ref[0]
    def stage(p,_):
        a=own_ref[p,E:2*E,:]; b=other_ref[p,:E,:]
        keyt_ref[2*p+core]=a; keyt_ref[2*p+1-core]=b
        key_ref[2*p+core]=a.T; key_ref[2*p+1-core]=b.T
        value_ref[2*p+core]=own_ref[p,2*E:,:].T
        value_ref[2*p+1-core]=other_ref[p,E:,:].T
        return 0
    lax.fori_loop(0,NB//2,stage,0)
    gk_ref[...]=jnp.zeros_like(gk_ref); gv_ref[...]=jnp.zeros_like(gv_ref)
    def one(p,_):
        query=own_ref[p,:E,:]*jnp.asarray(0.125,bf16)
        rows=query.T
        gout=gout_ref[p]; gout_rows=gout.T
        lse=lse_ref[p]
        delta=jnp.sum(gout.astype(f32)*out_ref[p],axis=0,keepdims=True)
        qb=2*p+core
        def step(blocks,masked,acc):
            for j in blocks:
                s=dot(key_ref[j],query)
                if masked: s=jnp.where(allowed_block(j,qb,info_ref),s,MASKED)
                e=jnp.exp(s-lse)
                gp=dot(value_ref[j],gout)
                gs=(e*(gp-delta)).astype(bf16)
                gv_ref[j]+=dot(e.astype(bf16),gout_rows)
                gk_ref[j]+=dot(gs,rows)
                acc=acc+dot(keyt_ref[j],gs)
            return acc
        acc=step((2*p,2*p+1),True,jnp.zeros((E,B),f32))
        acc=lax.fori_loop(0,p,lambda i,c: step((2*i,2*i+1),False,c),acc)
        acc=lax.fori_loop(0,extra_blocks(p,info_ref),lambda i,c: step((2*p+2,),True,c),acc)
        gq_ref[p]=(acc*0.125).astype(bf16)
        return 0
    lax.fori_loop(0,NB//2,one,0)
    def finish(p,_):
        gown_ref[p,:E,:]=gk_ref[2*p+core].T
        gown_ref[p,E:,:]=gv_ref[2*p+core].T
        gother_ref[p,:E,:]=gk_ref[2*p+1-core].T.astype(bf16)
        gother_ref[p,E:,:]=gv_ref[2*p+1-core].T.astype(bf16)
        return 0
    lax.fori_loop(0,NB//2,finish,0)

VM=pl.BlockSpec(memory_space=pltpu.VMEM); SM=pl.BlockSpec(memory_space=pltpu.SMEM)
LIMIT=40*1024*1024
def attn_forward(lengths,starts,own,other):
    H=NB//2
    return pl.pallas_call(forward_kernel,
        out_shape=(jax.ShapeDtypeStruct((H,E,B),f32),jax.ShapeDtypeStruct((H,E,B),bf16),jax.ShapeDtypeStruct((H,1,B),f32)),
        in_specs=[SM,SM,VM,VM],out_specs=(VM,VM,VM),
        scratch_shapes=[pltpu.VMEM((NB,B,E),bf16),pltpu.VMEM((NB,E,B),bf16)],
        compiler_params=pltpu.CompilerParams(vmem_limit_bytes=LIMIT),
        cost_estimate=takes(4),
        name="attention_forward")(lengths,starts,own,other)
def attn_backward(lengths,starts,own,other,gout,out,lse):
    H=NB//2
    return pl.pallas_call(backward_kernel,
        out_shape=(jax.ShapeDtypeStruct((H,E,B),bf16),jax.ShapeDtypeStruct((H,2*E,B),f32),jax.ShapeDtypeStruct((H,2*E,B),bf16)),
        in_specs=[SM,SM]+[VM]*5,out_specs=(VM,VM,VM),
        scratch_shapes=[pltpu.VMEM((NB,B,E),bf16),pltpu.VMEM((NB,E,B),bf16),pltpu.VMEM((NB,B,E),bf16),pltpu.VMEM((NB,B,E),f32),pltpu.VMEM((NB,B,E),f32)],
        compiler_params=pltpu.CompilerParams(vmem_limit_bytes=LIMIT),
        cost_estimate=takes(26),
        name="attention_backward")(lengths,starts,own,other,gout,out,lse)


SPREAD = ("x", "y", "zh")
LINE = ("zh", "y")
VM = pl.BlockSpec(memory_space=pltpu.VMEM)
SM = pl.BlockSpec(memory_space=pltpu.SMEM)
ANY = pl.BlockSpec(memory_space=pl.ANY)
ROOMY = pltpu.CompilerParams(vmem_limit_bytes=40 * 1024 * 1024)
WHOLE = pltpu.CompilerParams(vmem_limit_bytes=58 * 1024 * 1024)


def takes(microseconds):
    return pl.CostEstimate(
        flops=int(microseconds * 1.15e9), bytes_accessed=1 << 20, transcendentals=0
    )


def low(field):
    return field.astype(bf16)


def swap(field, axis):
    return lax.ppermute(field, axis, [(0, 1), (1, 0)])


def exchange(field, axes):
    return lax.all_to_all(field, axes, split_axis=0, concat_axis=0, tiled=True)


def after(field, *others):
    return lax.optimization_barrier((field, *others))[0]


def contract(a, b, dim_a, dim_b):
    return lax.dot_general(a, b, (((dim_a,), (dim_b,)), ((), ())), preferred_element_type=f32)


def shape(*dims, kind=bf16):
    return jax.ShapeDtypeStruct(dims, kind)


def far(field):
    return pltpu.with_memory_space_constraint(field, pltpu.HBM)


def block_of(array):
    dims = len(array.shape)
    return pl.BlockSpec(array.shape, lambda *_: (0,) * dims)


def call(kernel, name, outs, *args, scalars=0, cost=1, scratch=()):
    return pl.pallas_call(
        kernel,
        grid=(1,),
        out_shape=outs,
        in_specs=[SM] * scalars + [block_of(a) for a in args[scalars:]],
        out_specs=jax.tree.map(block_of, outs),
        scratch_shapes=list(scratch),
        compiler_params=ROOMY,
        cost_estimate=takes(cost),
        name=name,
    )(*args)


def feature_order(order_ref):
    place = lax.broadcasted_iota(jnp.int32, (1, 1024), 1)
    group = (place & 511) >> 4
    canon = ((group >> 3) << 3) + ((group & 1) << 2) + ((group >> 1) & 3)
    feature = ((canon * 2 + (lax.axis_index("c") ^ (place >> 9))) << 4) + (place & 15)
    for at in range(0, 1024, 256):
        rows = at + lax.broadcasted_iota(jnp.int32, (256, 1024), 0)
        order_ref[at : at + 256, :] = jnp.where(rows == feature, 1.0, 0.0).astype(bf16)


def valid_rows(lengths_ref):
    ctx = (lax.axis_index("zh") * 4 + lax.axis_index("y")) * 2 + lax.axis_index("c")
    position = ctx * 256 + lax.broadcasted_iota(jnp.int32, (256, 1), 0)
    return jnp.where(position < lengths_ref[lax.axis_index("x")], 1.0, 0.0)


def norm_parts(values):
    center = values - jnp.mean(values, axis=-1, keepdims=True)
    inverse = lax.rsqrt(jnp.mean(center * center, axis=-1, keepdims=True) + NORM_EPS)
    return center * inverse, inverse


def norm_back(grad, gain, norm, inverse):
    scaled = grad * gain
    return inverse * (
        scaled
        - jnp.mean(scaled, axis=-1, keepdims=True)
        - norm * jnp.mean(scaled * norm, axis=-1, keepdims=True)
    )


def gelu_pair(u):
    k = 0.7978845608028654
    square = u * u
    t = jnp.tanh(u * (k + (k * 0.044715) * square))
    half = 0.5 + 0.5 * t
    value = u * half
    slope = half + (0.5 * u) * (1.0 - t * t) * (k + (3 * 0.044715 * k) * square)
    return value, slope


def prepare_kernel(proj_ref, qkv_ref, a_ref, b_ref, c_ref, d_ref, e_ref, g_ref, out_ref):
    rows = [r[...].astype(f32) for r in (a_ref, b_ref, c_ref, d_ref, e_ref, g_ref)]
    small = jnp.concatenate(rows + [jnp.zeros((2, 16), f32)], axis=0).T
    small = low(jnp.concatenate([small, jnp.zeros((16, 120), f32)], axis=1))

    def one(k, _):
        out_ref[k, :, :512] = proj_ref[...]
        for c in range(3):
            out_ref[k, :, 512 * (c + 1) : 512 * (c + 2)] = qkv_ref[:, c, :]
        out_ref[k, :, 2048:] = small
        return 0

    lax.fori_loop(0, 32, one, 0)


def prepare_rest_kernel(fc_ref, out_ref, rest_ref):
    rest_ref[:, :2048] = fc_ref[...]
    rest_ref[:, 2048:] = out_ref[...]


def inputs_kernel(lengths_ref, tokens_ref, cotangent_ref, inputs_ref, grad_ref, order_ref):
    feature_order(order_ref)
    inputs_ref[...] = low(dot(tokens_ref[...], order_ref[...]))
    grad = dot(cotangent_ref[...], order_ref[...]) * valid_rows(lengths_ref)
    grad_ref[...] = low(grad)


def qkv_kernel(inputs_ref, own_ref, other_ref, bias_ref, heads_ref, normed_ref, vectors_ref):
    for half, ref in ((0, own_ref), (1, other_ref)):
        vectors_ref[:, 512 * half : 512 * (half + 1)] = ref[:, 2048:].astype(f32).T[:8]
    norm, _ = norm_parts(inputs_ref[...].astype(f32))
    normed = low(norm * vectors_ref[0:1, :] + vectors_ref[1:2, :])
    normed_ref[...] = normed
    for c in range(3):
        cols = slice(512 * (c + 1), 512 * (c + 2))
        field = dot(normed[:, :512], own_ref[:, cols]) + dot(normed[:, 512:], other_ref[:, cols])
        if c != 1:
            field = field + bias_ref[c // 2 : c // 2 + 1, :].astype(f32)
        field = low(field).T
        for h in range(8):
            heads_ref[h, 64 * c : 64 * (c + 1), :] = field[64 * h : 64 * (h + 1)]


def proj_kernel(heads_ref, own_ref, other_ref, part_ref):
    rows = heads_ref[...].T
    part_ref[:, :512] = low(contract(rows, own_ref[...], 1, 1))
    part_ref[:, 512:] = low(contract(rows, other_ref[...], 1, 1))


def project_out(heads_out, own, other):
    block = pl.BlockSpec((512, 512), lambda i: (0, 0))
    return pl.pallas_call(
        proj_kernel,
        grid=(1,),
        out_shape=shape(256, 1024),
        in_specs=[pl.BlockSpec((512, 256), lambda i: (0, 0)), block, block],
        out_specs=pl.BlockSpec((256, 1024), lambda i: (0, 0)),
        compiler_params=ROOMY,
        cost_estimate=takes(2),
        name="proj",
    )(heads_out, own, other)


def grad_act_kernel(gm_ref, own_ref, out_ref):
    out_ref[...] = dot(gm_ref[...], own_ref[...])


def grad_activated(grad_mlp, own_r):
    return pl.pallas_call(
        grad_act_kernel,
        grid=(4,),
        out_shape=shape(256, 2048, kind=f32),
        in_specs=[
            pl.BlockSpec((256, 512), lambda i: (0, 0)),
            pl.BlockSpec((512, 512), lambda i: (0, 4 + i)),
        ],
        out_specs=pl.BlockSpec((256, 512), lambda i: (0, i)),
        compiler_params=ROOMY,
        cost_estimate=takes(2),
        name="grad_act",
    )(grad_mlp, far(own_r))


def feed_kernel(
    inputs_ref,
    mine_ref,
    swapped_ref,
    vectors_ref,
    gact_ref,
    gm_ref,
    bias_ref,
    own_ref,
    other_ref,
    out_ref,
    middle_ref,
    n_ref,
    act_ref,
    gh_ref,
    part_ref,
    total_ref,
):
    i = pl.program_id(0)

    @pl.when(i == 0)
    def _():
        attn_out = mine_ref[...].astype(f32) + swapped_ref[...].astype(f32) + vectors_ref[2:3, :]
        middle = inputs_ref[...].astype(f32) + attn_out
        middle_ref[...] = middle
        norm, _ = norm_parts(middle)
        n_ref[...] = low(norm * vectors_ref[3:4, :] + vectors_ref[4:5, :])
        total_ref[...] = jnp.zeros_like(total_ref)

    halves = (slice(0, 256), slice(256, 512))
    hidden = [
        dot(n_ref[:, :512], own_ref[:, cols])
        + dot(n_ref[:, 512:], other_ref[:, cols])
        + bias_ref[:, cols].astype(f32)
        for cols in halves
    ]
    for cols, field in zip(halves, hidden):
        value, slope = gelu_pair(field)
        act_ref[:, cols] = low(value)
        grad = gact_ref[:, cols] + dot(gm_ref[...], out_ref[:, cols])
        gh_ref[:, cols] = low(grad * slope)
    total_ref[:, :512] += contract(gh_ref[...], own_ref[...], 1, 1)
    total_ref[:, 512:] += contract(gh_ref[...], other_ref[...], 1, 1)

    @pl.when(i == 3)
    def _():
        part_ref[...] = low(total_ref[...])


def feed_forward(inputs, mine, swapped, vectors, grad_act, grad_mlp, fc_bias, own_r, other_r):
    def whole(*dims):
        return pl.BlockSpec(dims, lambda i: (0, 0))

    def tile(rows, first):
        return pl.BlockSpec((rows, 512), lambda i: (0, first + i))

    wide = whole(256, 1024)
    return pl.pallas_call(
        feed_kernel,
        grid=(4,),
        out_shape=(
            shape(256, 1024, kind=f32),
            shape(256, 1024),
            shape(256, 2048),
            shape(256, 2048),
            shape(256, 1024),
        ),
        in_specs=[
            wide,
            wide,
            wide,
            whole(8, 1024),
            tile(256, 0),
            pl.BlockSpec((256, 512), lambda i: (0, 1)),
            tile(1, 0),
            tile(512, 0),
            tile(512, 0),
            tile(512, 4),
        ],
        out_specs=(wide, wide, tile(256, 0), tile(256, 0), wide),
        scratch_shapes=[pltpu.VMEM((256, 1024), f32)],
        compiler_params=ROOMY,
        cost_estimate=takes(8),
        name="feed_forward",
    )(
        inputs,
        mine,
        swapped,
        vectors,
        grad_act,
        grad_mlp,
        fc_bias,
        far(own_r),
        far(other_r),
        far(other_r),
    )


def wide_kernel(
    n_ref, gh_ref, gm_ref, act_ref, own_ref, other_ref, out_ref, part_ref, left_ref, total_ref
):
    i = pl.program_id(0)
    core = lax.axis_index("c")

    @pl.when(i == 0)
    def _():
        left_ref[0] = n_ref[...].T
        left_ref[1] = gm_ref[...].T
        total_ref[...] = jnp.zeros_like(total_ref)

    def put(left, right):
        for half in (0, 1):
            rows = pl.ds(pl.multiple_of((core ^ half) * 512, 512), 512)
            out_ref[rows, :] = low(dot(left[512 * half : 512 * (half + 1)], right))

    @pl.when(i < 4)
    def _():
        put(left_ref[0], gh_ref[...])

    @pl.when(i >= 4)
    def _():
        put(left_ref[1], act_ref[...])
        total_ref[:, :512] += contract(act_ref[...], own_ref[...], 1, 1)
        total_ref[:, 512:] += contract(act_ref[...], other_ref[...], 1, 1)

    @pl.when(i == 7)
    def _():
        part_ref[...] = low(total_ref[...])


def wide_grads(normed_two, grad_hidden, grad_mlp, activated, own_r, other_r):
    whole = pl.BlockSpec((256, 1024), lambda i: (0, 0))
    weights = pl.BlockSpec((512, 512), lambda i: (0, 4 + jnp.maximum(i - 4, 0)))
    return pl.pallas_call(
        wide_kernel,
        grid=(8,),
        out_shape=(shape(1024, 4096), shape(256, 1024)),
        in_specs=[
            whole,
            pl.BlockSpec((256, 512), lambda i: (0, jnp.minimum(i, 3))),
            whole,
            pl.BlockSpec((256, 512), lambda i: (0, jnp.maximum(i - 4, 0))),
            weights,
            weights,
        ],
        out_specs=(pl.BlockSpec((1024, 512), lambda i: (0, i)), whole),
        scratch_shapes=[pltpu.VMEM((2, 1024, 256), bf16), pltpu.VMEM((256, 1024), f32)],
        compiler_params=WHOLE,
        cost_estimate=takes(8),
        name="wide_grads",
    )(normed_two, grad_hidden, grad_mlp, activated, far(own_r), far(other_r))


def middle_back_kernel(
    middle_ref, mine_ref, swapped_ref, vectors_ref, gm_ref, own_ref, other_ref, out_ref, ga_ref, gheads_ref, cols_ref
):
    gm = gm_ref[...].astype(f32)
    norm, inverse = norm_parts(middle_ref[...])
    grad = mine_ref[...].astype(f32) + swapped_ref[...].astype(f32)
    out = gm + norm_back(grad, vectors_ref[3:4, :], norm, inverse)
    out_ref[...] = out
    low_out = low(out)
    ga_ref[...] = low_out
    field = dot(low_out[:, :512], own_ref[...]) + dot(low_out[:, 512:], other_ref[...])
    field = low(field).T
    for h in range(8):
        gheads_ref[h] = field[64 * h : 64 * (h + 1)]
    rows = [low_out.astype(f32), grad * norm, grad, gm]
    rows = [jnp.sum(r, axis=0, keepdims=True) for r in rows]
    cols_ref[...] = jnp.concatenate(rows + [jnp.zeros((4, 1024), f32)], axis=0)


def middle_back(middle, mine, swapped, vectors, grad_mlp, own, other):
    def whole(*dims):
        return pl.BlockSpec(dims, lambda i: (0,) * len(dims))

    wide = whole(256, 1024)
    return pl.pallas_call(
        middle_back_kernel,
        grid=(1,),
        out_shape=(
            shape(256, 1024, kind=f32),
            shape(256, 1024),
            shape(8, 64, 256),
            shape(8, 1024, kind=f32),
        ),
        in_specs=[wide, wide, wide, whole(8, 1024), wide, whole(512, 512), whole(512, 512)],
        out_specs=(wide, wide, whole(8, 64, 256), whole(8, 1024)),
        compiler_params=ROOMY,
        cost_estimate=takes(3),
        name="middle_back",
    )(middle, mine, swapped, vectors, grad_mlp, own, other)


def put_block(ref, at, block):
    for g in range(32):
        ref[16 * g : 16 * (g + 1), at : at + 128] = block


def merge_kernel(query_ref, own_ref, other_ref, out_ref):
    out_ref[:, :64, :] = query_ref[...]
    out_ref[:, 64:, :] = low(own_ref[...] + other_ref[...].astype(f32))


def final_kernel(
    lengths_ref, inputs_ref, middle_ref, mine_ref, swapped_ref, vectors_ref, out_ref, roots_ref, order_ref
):
    feature_order(order_ref)
    valid = valid_rows(lengths_ref)
    inputs = inputs_ref[...].astype(f32)
    middle = middle_ref[...]
    mlp_out = mine_ref[...].astype(f32) + swapped_ref[...].astype(f32) + vectors_ref[5:6, :]
    final = middle + mlp_out
    out_ref[...] = low(contract(low(final), order_ref[...], 1, 1))
    lane = lax.broadcasted_iota(jnp.int32, (1, 128), 1)
    total = jnp.zeros((1, 128), f32)
    for k, field in enumerate((inputs, middle - inputs, mlp_out, final)):
        total = jnp.where(lane == k, jnp.sum(valid * field * field), total)
    roots_ref[...] = total


def side_kernel(ga_ref, heads_ref, rows_ref, mine_ref, theirs_ref):
    cols = jnp.concatenate([rows_ref[...], jnp.zeros((120, 1024), f32)], axis=0)
    for half, ref in ((0, mine_ref), (1, theirs_ref)):
        rows = slice(512 * half, 512 * (half + 1))
        ref[:, :512] = low(contract(ga_ref[:, rows].T, heads_ref[...], 1, 1))
        ref[:, 512:] = low(cols[:, rows].T)


def side_add_kernel(a_ref, b_ref, out_ref):
    out_ref[...] = low(a_ref[...].astype(f32) + b_ref[...].astype(f32))


def back_kernel(
    gback_ref,
    own_ref,
    other_ref,
    normed_ref,
    inputs_ref,
    roots_ref,
    gh_ref,
    part_ref,
    mine_ref,
    theirs_ref,
    rows_ref,
    grads_ref,
):
    for c in range(3):
        for h in range(8):
            at = 512 * c + 64 * h
            grads_ref[at : at + 64, :] = gback_ref[h, 64 * c : 64 * (c + 1), :]
    left = normed_ref[...].T
    more = contract(jnp.ones((8, 256), bf16), gh_ref[...], 1, 0)[0:1]
    more = low(jnp.concatenate([more[:, 128 * r : 128 * (r + 1)] for r in range(16)], axis=0))
    sums = contract(jnp.ones((8, 256), bf16), grads_ref[...], 1, 1)[0:1]
    sums = [sums[:, 128 * r : 128 * (r + 1)] for r in range(12)]
    sums = low(jnp.concatenate(sums + [roots_ref[...], jnp.zeros((3, 128), f32)], axis=0))
    for half, ref in ((0, mine_ref), (1, theirs_ref)):
        rows = slice(512 * half, 512 * (half + 1))
        for c in range(3):
            cols = slice(512 * c, 512 * (c + 1))
            ref[:, cols] = low(contract(left[rows], grads_ref[cols, :], 1, 1))
        put_block(ref, 1536, sums)
        put_block(ref, 1664, more)
    sides = [grads_ref[512 * c : 512 * (c + 1), :].T for c in range(3)]
    norm, _ = norm_parts(inputs_ref[...].astype(f32))
    for half, ref in ((0, own_ref), (1, other_ref)):
        rows = slice(512 * half, 512 * (half + 1))
        part = sum(contract(sides[c], ref[:, 512 * (c + 1) : 512 * (c + 2)], 1, 1) for c in range(3))
        part = low(part)
        part_ref[:, rows] = part
        part = part.astype(f32)
        gain = jnp.sum(part * norm[:, rows], axis=0, keepdims=True)
        shift = jnp.sum(part, axis=0, keepdims=True)
        rows_ref[half] = jnp.concatenate([gain, shift, jnp.zeros((6, 512), f32)], axis=0)


def core_add_kernel(a_ref, b_ref, side_ref, rows_ref, c_ref, t_ref, d_ref, out_ref):
    out_ref[:, :1792] = low(a_ref[...].astype(f32) + b_ref[...].astype(f32))
    out_ref[:, 1792:2304] = side_ref[:, :512]
    ln1 = (rows_ref[...] + t_ref[...]) + (c_ref[...] + d_ref[...])
    ln1 = jnp.concatenate([jnp.zeros((4, 128), f32), ln1[:2], jnp.zeros((122, 128), f32)], axis=0)
    out_ref[:, 2304:] = low(side_ref[:, 512:].astype(f32) + ln1.T)


def core_add(mine, theirs, side, rows, by_core, by_tp, by_both):
    def tall(cols):
        return pl.BlockSpec((128, cols), lambda i: (i, 0))

    flat = pl.BlockSpec((8, 128), lambda i: (0, i))
    return pl.pallas_call(
        core_add_kernel,
        grid=(4,),
        out_shape=shape(512, 2432),
        in_specs=[tall(1792), tall(1792), tall(640), flat, flat, flat, flat],
        out_specs=tall(2432),
        compiler_params=ROOMY,
        cost_estimate=takes(2),
        name="qkv_core_sum",
    )(mine, theirs, side, rows, by_core, by_tp, by_both)


def end_kernel(inputs_ref, gmid_ref, mine_ref, swapped_ref, vectors_ref, out_ref, order_ref):
    feature_order(order_ref)
    norm, inverse = norm_parts(inputs_ref[...].astype(f32))
    grad = mine_ref[...].astype(f32) + swapped_ref[...].astype(f32)
    grad = gmid_ref[...] + norm_back(grad, vectors_ref[0:1, :], norm, inverse)
    out_ref[...] = low(contract(low(grad), order_ref[...], 1, 1))


def total_qkv_kernel(lengths_ref, got_ref, qkv_ref, proj_ref, bias_ref, fc_ref, cols_ref, roots_ref):
    total = got_ref[0].astype(f32)
    for k in range(1, 32):
        total = total + got_ref[k].astype(f32)
    for c in range(3):
        qkv_ref[:, c, :] = total[:, 512 * c : 512 * (c + 1)]
    for k in range(2):
        for r in range(4):
            row = 8 * k + r
            bias_ref[k : k + 1, 128 * r : 128 * (r + 1)] = total[row : row + 1, 1536:1664]
    count = lengths_ref[0] + lengths_ref[1] + lengths_ref[2] + lengths_ref[3]
    mean = total[12:13, 1536:1664] / (count.astype(f32) * 1024.0)
    roots_ref[...] = jnp.sqrt(mean + ROOT_EPS)
    fc_ref[...] = total[:, 1664:1792]
    proj_ref[...] = total[:, 1792:2304]
    cols_ref[...] = total[:, 2304:].T[:8]


def total_wide_kernel(mine_ref, theirs_ref, fc_ref, out_ref):
    total = mine_ref[...].astype(f32) + theirs_ref[...].astype(f32)
    fc_ref[...] = total[:, :2048]
    out_ref[...] = total[:, 2048:]


def body(
    tokens,
    ln1_gain,
    ln1_bias,
    qkv_weight,
    qv_bias,
    proj_weight,
    proj_bias,
    ln2_gain,
    ln2_bias,
    fc_weight,
    fc_bias,
    out_weight,
    out_bias,
    piece_starts,
    seq_lengths,
    cotangent,
):
    vectors = (ln1_gain, ln1_bias, proj_bias, ln2_gain, ln2_bias, out_bias)
    pay_q = call(
        prepare_kernel,
        "weights_payload",
        shape(32, 16, 2176),
        proj_weight.T,
        qkv_weight,
        *[v.reshape(1, 16) for v in vectors],
    )
    pay_r = call(
        prepare_rest_kernel,
        "rest_payload",
        shape(16, 4096),
        fc_weight,
        out_weight.T,
    )
    own_r = lax.all_gather(pay_r, SPREAD, axis=0, tiled=True)
    own_q = exchange(pay_q, SPREAD).reshape(512, 2176)
    inputs, grad_mlp = call(
        inputs_kernel,
        "inputs",
        (shape(256, 1024), shape(256, 1024)),
        seq_lengths,
        tokens[0],
        cotangent[0],
        scalars=1,
        cost=2,
        scratch=[pltpu.VMEM((1024, 1024), bf16)],
    )
    own_q = after(own_q, inputs)
    other_q = swap(own_q, "c")
    heads, normed, vectors = call(
        qkv_kernel,
        "qkv",
        (shape(8, 192, 256), shape(256, 1024), shape(8, 1024, kind=f32)),
        inputs,
        own_q,
        other_q,
        qv_bias,
        cost=3,
    )
    own = exchange(heads, LINE)
    other = swap(own[:, 64:], "c")
    attended, attended_low, log_sum = attn_forward(seq_lengths, piece_starts, own, other)
    heads_out = exchange(attended_low, LINE).reshape(512, 256)

    attn_part = project_out(heads_out, far(own_q), far(other_q))
    own_r = after(own_r, attn_part)
    other_r = swap(own_r, "c")
    grad_act = grad_activated(grad_mlp, own_r)
    middle, normed_two, activated, grad_hidden, two_part = feed_forward(
        inputs,
        attn_part,
        swap(attn_part, "tp"),
        vectors,
        grad_act,
        grad_mlp,
        fc_bias.reshape(1, 2048),
        own_r,
        other_r,
    )
    two_swapped = swap(two_part, "tp")
    wide, mlp_part = wide_grads(normed_two, grad_hidden, grad_mlp, activated, own_r, other_r)
    wide = lax.psum_scatter(after(wide, two_swapped), "c", scatter_dimension=0, tiled=True)
    two_swapped = after(two_swapped, mlp_part)
    grad_middle, grad_attn, grad_heads, rows = middle_back(
        middle, two_part, two_swapped, vectors, grad_mlp, far(own_q), far(other_q)
    )
    grad_mine = exchange(grad_heads, LINE)

    mine_p, theirs_p = call(
        side_kernel,
        "proj_grads",
        (shape(512, 640), shape(512, 640)),
        grad_attn,
        far(heads_out),
        rows,
        cost=2,
    )
    side = call(side_add_kernel, "proj_core_sum", shape(512, 640), mine_p, swap(theirs_p, "c"))
    grad_mine = after(grad_mine, side)
    mlp_swapped = swap(after(mlp_part, grad_mine), "tp")

    wide = lax.psum_scatter(after(wide, grad_mine), "x", scatter_dimension=0, tiled=True)
    grad_query, grad_own, grad_other = attn_backward(
        seq_lengths, piece_starts, own, other, grad_mine, attended, log_sum
    )
    grad_other, mlp_swapped = lax.optimization_barrier((grad_other, mlp_swapped))
    grad_back = call(
        merge_kernel, "merge", shape(8, 192, 256), grad_query, grad_own, swap(grad_other, "c")
    )
    grad_back = exchange(grad_back, LINE)
    layer_out, roots = call(
        final_kernel,
        "final",
        (shape(256, 1024), shape(1, 128, kind=f32)),
        seq_lengths,
        far(inputs),
        far(middle),
        after(mlp_part, grad_other),
        mlp_swapped,
        vectors,
        scalars=1,
        cost=3,
        scratch=[pltpu.VMEM((1024, 1024), bf16)],
    )
    wide = lax.psum_scatter(after(wide, roots), "y", scatter_dimension=0, tiled=True)
    one_part, mine_q, theirs_q, rows = call(
        back_kernel,
        "back",
        (
            shape(256, 1024),
            shape(512, 1792),
            shape(512, 1792),
            shape(2, 8, 512, kind=f32),
        ),
        grad_back,
        far(own_q),
        far(other_q),
        far(normed),
        far(inputs),
        roots,
        far(grad_hidden),
        cost=4,
        scratch=[pltpu.VMEM((1536, 256), bf16)],
    )
    both = core_add(
        mine_q,
        swap(theirs_q, "c"),
        side,
        rows[0],
        swap(rows[1], "c"),
        swap(rows[0], "tp"),
        lax.ppermute(rows[1], ("c", "tp"), [(i, 3 - i) for i in range(4)]),
    )
    got_q = exchange(both.reshape(32, 16, 2432), SPREAD)
    grad_tokens = call(
        end_kernel,
        "end",
        shape(256, 1024),
        far(inputs),
        far(grad_middle),
        far(one_part),
        swap(one_part, "tp"),
        vectors,
        cost=3,
        scratch=[pltpu.VMEM((1024, 1024), bf16)],
    )
    zh = lax.axis_index("zh")
    keep = lax.dynamic_slice_in_dim(wide, zh * 16, 16, 0)
    send = lax.dynamic_slice_in_dim(wide, 16 - zh * 16, 16, 0)
    grad_fc, grad_out = call(
        total_wide_kernel,
        "total_wide",
        (shape(16, 2048, kind=f32), shape(16, 2048, kind=f32)),
        keep,
        swap(send, "zh"),
    )
    got_q = after(got_q, grad_fc, grad_tokens)
    grad_qkv, grad_proj, bias_sums, fc_sums, cols, roots = call(
        total_qkv_kernel,
        "total_qkv",
        (
            shape(16, 3, 512, kind=f32),
            shape(16, 512, kind=f32),
            shape(2, 512, kind=f32),
            shape(16, 128, kind=f32),
            shape(8, 16, kind=f32),
            shape(1, 128, kind=f32),
        ),
        seq_lengths,
        got_q,
        scalars=1,
    )
    return (
        layer_out[None],
        grad_tokens[None],
        cols[4],
        cols[5],
        grad_qkv,
        bias_sums,
        grad_proj.T,
        cols[0],
        cols[1],
        cols[2],
        grad_fc,
        fc_sums.reshape(2048),
        grad_out.T,
        cols[3],
        roots[0, :4],
    )


def solution(mesh):
    fine = Mesh(mesh.devices.reshape(4, 2, 4, 2, 2), ("x", "zh", "y", "c", "tp"))
    ctx = ("zh", "y", "c")
    every = ("x", "zh", "y", "c")
    in_specs = (
        P("x", ctx, None),
        P(every),
        P(every),
        P(every, None, "tp"),
        P(None, "tp"),
        P("tp", every),
        P(every),
        P(every),
        P(every),
        P(every, "tp"),
        P("tp"),
        P("tp", every),
        P(every),
        P("x", None),
        P(),
        P("x", ctx, None),
    )
    out_specs = (
        P("x", ctx, None),
        P("x", ctx, None),
        P(every),
        P(every),
        P(every, None, "tp"),
        P(None, "tp"),
        P("tp", every),
        P(every),
        P(every),
        P(every),
        P(every, "tp"),
        P("tp"),
        P("tp", every),
        P(every),
        P(),
    )
    return jax.shard_map(body, mesh=fine, in_specs=in_specs, out_specs=out_specs, check_vma=False)
```

```python
from functools import partial

import jax
import jax.numpy as jnp
from jax import lax
from jax.experimental import pallas as pl
from jax.experimental.pallas import tpu as pltpu
from jax.sharding import Mesh
from jax.sharding import PartitionSpec as P

f32 = jnp.float32
bf16 = jnp.bfloat16
NORM_EPS = 1e-05
ROOT_EPS = 1e-06
B=256; E=64; NB=16; MASKED=-1e30; PIECE=256

class Facts:
    def __init__(self, lengths_ref, starts_ref):
        self.core = lax.axis_index("c")
        self.items = (self.core, lengths_ref[lax.axis_index("x")], starts_ref[0, 0], starts_ref[0, 1])

    def __getitem__(self, at):
        return self.items[at]


def piece_of(pos, info_ref):
    n0=(pos>=info_ref[2])&(pos<info_ref[2]+PIECE)
    n1=(pos>=info_ref[3])&(pos<info_ref[3]+PIECE)
    return jnp.where(n0,1,0)+jnp.where(n1,2,0)

def allowed_block(key_block, query_block, info_ref):
    kpos=key_block*B+lax.broadcasted_iota(jnp.int32,(B,1),0)
    qpos=query_block*B+lax.broadcasted_iota(jnp.int32,(1,B),1)
    kp=piece_of(kpos,info_ref); qp=piece_of(qpos,info_ref)
    qp=jnp.where(qp==0,-1,qp)
    kp=jnp.where(kpos<info_ref[1],kp,-2)
    kpos=jnp.where(kpos<info_ref[1],kpos,1<<20)
    return (kpos<=qpos)|(kp==qp)

def extra_blocks(p, info_ref):
    edge=(2*p+2)*B
    crosses=((info_ref[2]<edge)&(edge<info_ref[2]+PIECE))|((info_ref[3]<edge)&(edge<info_ref[3]+PIECE))
    return jnp.where((info_ref[0]==1)&(p<NB//2-1)&crosses,1,0)

def dot(a,b): return jnp.dot(a,b,preferred_element_type=f32)

SAFE = 60.0


def split3(row):
    top = row.astype(bf16).astype(f32)
    mid = (row - top).astype(bf16).astype(f32)
    rows = jnp.concatenate([top, mid, row - top - mid, jnp.zeros((13, B), f32)], axis=0)
    return rows.astype(bf16)


def ones_beside(block):
    lane = lax.broadcasted_iota(jnp.int32, (B, 16), 1)
    return jnp.concatenate([block, jnp.where(lane < 3, 1.0, 0.0).astype(bf16)], axis=1)


FORWARD_CHUNK = 1024
BACKWARD_CHUNK = 4096


def walk(p, extra, step, carry, chunk):
    end = 2 * B * (p + 1)
    for first in range(0, end, chunk):
        last = min(first + chunk, end)
        carry = step(first, last - first, max(0, last - (end - 2 * B)) // B, carry)
    if p == NB // 2 - 1:
        return carry
    return lax.fori_loop(0, extra, lambda i, c: step(end, B, 1, c), carry)


def masked_from(e, first, count, masked, query_block, info_ref):
    if not masked:
        return e
    keep = count - masked * B
    parts = [e[:keep]] if keep else []
    for at in range(keep, count, B):
        allowed = allowed_block((first + at) // B, query_block, info_ref)
        parts.append(jnp.where(allowed, e[at : at + B], 0.0))
    return jnp.concatenate(parts, axis=0)


def place(block):
    return pl.ds(pl.multiple_of(block * B, B), B)


def forward_kernel(lengths_ref, starts_ref, own_ref, other_ref, out_ref, low_ref, lse_ref, key_ref, value_ref):
    info_ref = Facts(lengths_ref, starts_ref)
    core = info_ref[0]
    sublane = lax.broadcasted_iota(jnp.int32, (16, NB * B), 0)
    value_ref[E:, :] = jnp.where(sublane == 0, 1.0, 0.0).astype(bf16)

    def squares(block):
        field = block.astype(f32)
        return jnp.sum(field * field, axis=0, keepdims=True)

    query_top = jnp.zeros((1, B), f32)
    key_top = jnp.zeros((1, B), f32)
    for p in range(NB // 2):
        mine, theirs = own_ref[p, E : 2 * E, :], other_ref[p, :E, :]
        here, there = place(2 * p + core), place(2 * p + 1 - core)
        key_ref[here, :] = mine.T
        key_ref[there, :] = theirs.T
        value_ref[:E, here] = own_ref[p, 2 * E :, :]
        value_ref[:E, there] = other_ref[p, E:, :]
        query_top = jnp.maximum(query_top, squares(own_ref[p, :E, :]))
        key_top = jnp.maximum(key_top, jnp.maximum(squares(mine), squares(theirs)))
    bound = jnp.max(query_top) * jnp.max(key_top)

    def finish(p, top, acc):
        total = acc[E : E + 1]
        o = acc[:E] / total
        out_ref[p] = o
        low_ref[p, 0] = o.astype(bf16)
        low_ref[p, 1] = o.astype(bf16)
        lse_ref[p] = top + jnp.log(total)

    @pl.when(bound <= (8.0 * SAFE) ** 2)
    def _():
        for p in range(NB // 2):
            query = own_ref[p, :E, :] * jnp.asarray(0.125, bf16)
            qb = 2 * p + core

            def step(first, count, masked, acc):
                e = jnp.exp(dot(key_ref[first : first + count, :], query))
                e = masked_from(e, first, count, masked, qb, info_ref)
                return acc + dot(value_ref[:, first : first + count], e.astype(bf16))

            acc = walk(p, extra_blocks(p, info_ref), step, jnp.zeros((E + 16, B), f32), FORWARD_CHUNK)
            finish(p, 0.0, acc)

    @pl.when(bound > (8.0 * SAFE) ** 2)
    def _():
        def one(p, _):
            query = own_ref[p, :E, :] * jnp.asarray(0.125, bf16)
            qb = 2 * p + core

            def step(blocks, masked, carry):
                top, acc = carry
                scores = [dot(key_ref[place(j), :], query) for j in blocks]
                if masked:
                    scores = [
                        jnp.where(allowed_block(j, qb, info_ref), s, MASKED)
                        for j, s in zip(blocks, scores)
                    ]
                new = top
                for s in scores:
                    new = jnp.maximum(new, jnp.max(s, axis=0, keepdims=True))
                acc = acc * jnp.exp(top - new)
                for j, s in zip(blocks, scores):
                    acc = acc + dot(value_ref[:, place(j)], jnp.exp(s - new).astype(bf16))
                return new, acc

            carry = (jnp.full((1, B), MASKED, f32), jnp.zeros((E + 16, B), f32))
            carry = step((2 * p, 2 * p + 1), True, carry)
            carry = lax.fori_loop(0, p, lambda i, c: step((2 * i, 2 * i + 1), False, c), carry)
            carry = lax.fori_loop(
                0, extra_blocks(p, info_ref), lambda i, c: step((2 * p + 2,), True, c), carry
            )
            finish(p, *carry)
            return 0

        lax.fori_loop(0, NB // 2, one, 0)


def backward_kernel(
    lengths_ref,
    starts_ref,
    own_ref,
    other_ref,
    gout_ref,
    out_ref,
    lse_ref,
    gq_ref,
    gown_ref,
    gother_ref,
    key_ref,
    keyt_ref,
    value_ref,
    grad_ref,
):
    info_ref = Facts(lengths_ref, starts_ref)
    core = info_ref[0]
    for p in range(NB // 2):
        mine, theirs = own_ref[p, E : 2 * E, :], other_ref[p, :E, :]
        here, there = place(2 * p + core), place(2 * p + 1 - core)
        keyt_ref[:, here] = mine
        keyt_ref[:, there] = theirs
        key_ref[here, :] = ones_beside(mine.T)
        key_ref[there, :] = ones_beside(theirs.T)
        value_ref[here, :] = ones_beside(own_ref[p, 2 * E :, :].T)
        value_ref[there, :] = ones_beside(other_ref[p, E:, :].T)
    grad_ref[...] = jnp.zeros_like(grad_ref)
    blank = jnp.zeros((B, E), bf16)

    for p in range(NB // 2):
        query = own_ref[p, :E, :] * jnp.asarray(0.125, bf16)
        gout = gout_ref[p]
        delta = jnp.sum(gout.astype(f32) * out_ref[p], axis=0, keepdims=True)
        rows = jnp.concatenate([blank, query.T], axis=1)
        gout_rows = jnp.concatenate([gout.T, blank], axis=1)
        query = jnp.concatenate([query, split3(-lse_ref[p])], axis=0)
        gout = jnp.concatenate([gout, split3(-delta)], axis=0)
        qb = 2 * p + core

        def step(first, count, masked, acc):
            at = slice(first, first + count)
            e = jnp.exp(dot(key_ref[at, :], query))
            e = masked_from(e, first, count, masked, qb, info_ref)
            gs = (e * dot(value_ref[at, :], gout)).astype(bf16)
            grad_ref[at, :] += dot(e.astype(bf16), gout_rows) + dot(gs, rows)
            return acc + dot(keyt_ref[:, at], gs)

        acc = walk(p, extra_blocks(p, info_ref), step, jnp.zeros((E, B), f32), BACKWARD_CHUNK)
        gq_ref[p] = (acc * 0.125).astype(bf16)

    for p in range(NB // 2):
        mine = grad_ref[place(2 * p + core), :].T
        theirs = grad_ref[place(2 * p + 1 - core), :].T.astype(bf16)
        gown_ref[p, :E, :] = mine[E:]
        gown_ref[p, E:, :] = mine[:E]
        gother_ref[p, :E, :] = theirs[E:]
        gother_ref[p, E:, :] = theirs[:E]


VM=pl.BlockSpec(memory_space=pltpu.VMEM); SM=pl.BlockSpec(memory_space=pltpu.SMEM)
LIMIT=40*1024*1024
def attn_forward(lengths,starts,own,other):
    H=NB//2
    return pl.pallas_call(forward_kernel,
        out_shape=(jax.ShapeDtypeStruct((H,E,B),f32),jax.ShapeDtypeStruct((H,2,E,B),bf16),jax.ShapeDtypeStruct((H,1,B),f32)),
        in_specs=[SM,SM,VM,VM],out_specs=(VM,VM,VM),
        scratch_shapes=[pltpu.VMEM((NB*B,E),bf16),pltpu.VMEM((E+16,NB*B),bf16)],
        compiler_params=pltpu.CompilerParams(vmem_limit_bytes=LIMIT),
        cost_estimate=takes(8),
        name="attention_forward")(lengths,starts,own,other)
def attn_backward(lengths,starts,own,other,gout,out,lse):
    H=NB//2
    return pl.pallas_call(backward_kernel,
        out_shape=(jax.ShapeDtypeStruct((H,E,B),bf16),jax.ShapeDtypeStruct((H,2*E,B),f32),jax.ShapeDtypeStruct((H,2*E,B),bf16)),
        in_specs=[SM,SM]+[VM]*5,out_specs=(VM,VM,VM),
        scratch_shapes=[pltpu.VMEM((NB*B,E+16),bf16),pltpu.VMEM((E,NB*B),bf16),pltpu.VMEM((NB*B,E+16),bf16),pltpu.VMEM((NB*B,2*E),f32)],
        compiler_params=pltpu.CompilerParams(vmem_limit_bytes=LIMIT),
        cost_estimate=takes(26),
        name="attention_backward")(lengths,starts,own,other,gout,out,lse)


SPREAD = ("x", "y", "zh")
LINE = ("zh", "y")
VM = pl.BlockSpec(memory_space=pltpu.VMEM)
SM = pl.BlockSpec(memory_space=pltpu.SMEM)
ANY = pl.BlockSpec(memory_space=pl.ANY)
ROOMY = pltpu.CompilerParams(vmem_limit_bytes=40 * 1024 * 1024)
WHOLE = pltpu.CompilerParams(vmem_limit_bytes=50 * 1024 * 1024)
ALL = pltpu.CompilerParams(vmem_limit_bytes=58 * 1024 * 1024)


def takes(microseconds):
    return pl.CostEstimate(
        flops=int(microseconds * 1.15e9), bytes_accessed=1 << 20, transcendentals=0
    )


def low(field):
    return field.astype(bf16)


def swap(field, axis):
    return lax.ppermute(field, axis, [(0, 1), (1, 0)])


def exchange(field, axes):
    return lax.all_to_all(field, axes, split_axis=0, concat_axis=0, tiled=True)


def after(field, *others):
    return lax.optimization_barrier((field, *others))[0]


def contract(a, b, dim_a, dim_b):
    return lax.dot_general(a, b, (((dim_a,), (dim_b,)), ((), ())), preferred_element_type=f32)


def shape(*dims, kind=bf16):
    return jax.ShapeDtypeStruct(dims, kind)


def far(field):
    return pltpu.with_memory_space_constraint(field, pltpu.HBM)


def block_of(array):
    dims = len(array.shape)
    return pl.BlockSpec(array.shape, lambda *_: (0,) * dims)


def call(kernel, name, outs, *args, scalars=0, cost=1, scratch=(), memory=ROOMY):
    return pl.pallas_call(
        kernel,
        grid=(1,),
        out_shape=outs,
        in_specs=[SM] * scalars + [block_of(a) for a in args[scalars:]],
        out_specs=jax.tree.map(block_of, outs),
        scratch_shapes=list(scratch),
        compiler_params=memory,
        cost_estimate=takes(cost),
        name=name,
    )(*args)


def feature_order(order_ref):
    place = lax.broadcasted_iota(jnp.int32, (1, 1024), 1)
    x, core, y, zh = place >> 8, (place >> 7) & 1, (place >> 5) & 3, (place >> 4) & 1
    feature = ((((x * 2 + zh) * 4 + y) * 2 + core) << 4) + (place & 15)
    for at in range(0, 1024, 256):
        rows = at + lax.broadcasted_iota(jnp.int32, (256, 1024), 0)
        order_ref[at : at + 256, :] = jnp.where(rows == feature, 1.0, 0.0).astype(bf16)


def core_lanes(side):
    core = lax.axis_index("c") ^ side
    return [pl.ds(pl.multiple_of(256 * x + 128 * core, 128), 128) for x in range(4)]


def of_core(ref, side):
    return jnp.concatenate([ref[:, lanes] for lanes in core_lanes(side)], axis=1)


def valid_rows(lengths_ref):
    ctx = (lax.axis_index("zh") * 4 + lax.axis_index("y")) * 2 + lax.axis_index("c")
    position = ctx * 256 + lax.broadcasted_iota(jnp.int32, (256, 1), 0)
    return jnp.where(position < lengths_ref[lax.axis_index("x")], 1.0, 0.0)


def norm_parts(values):
    center = values - jnp.mean(values, axis=-1, keepdims=True)
    inverse = lax.rsqrt(jnp.mean(center * center, axis=-1, keepdims=True) + NORM_EPS)
    return center * inverse, inverse


def norm_back(grad, gain, norm, inverse):
    scaled = grad * gain
    return inverse * (
        scaled
        - jnp.mean(scaled, axis=-1, keepdims=True)
        - norm * jnp.mean(scaled * norm, axis=-1, keepdims=True)
    )


def gelu_pair(u):
    k = 0.7978845608028654
    square = u * u
    t = jnp.tanh(u * (k + (k * 0.044715) * square))
    half = 0.5 + 0.5 * t
    value = u * half
    slope = half + (0.5 * u) * (1.0 - t * t) * (k + (3 * 0.044715 * k) * square)
    return value, slope


def prepare_kernel(qkv_ref, a_ref, b_ref, c_ref, d_ref, e_ref, g_ref, out_ref):
    rows = [r[...].astype(f32) for r in (a_ref, b_ref, c_ref, d_ref, e_ref, g_ref)]
    small = jnp.concatenate(rows + [jnp.zeros((2, 16), f32)], axis=0).T
    small = low(jnp.concatenate([small, jnp.zeros((16, 120), f32)], axis=1))

    def one(k, _):
        for c in range(3):
            out_ref[k, :, 512 * c : 512 * (c + 1)] = qkv_ref[:, c, :]
        out_ref[k, :, 1536:] = small
        return 0

    lax.fori_loop(0, 32, one, 0)


def prepare_rest_kernel(proj_ref, fc_ref, out_ref, rest_ref):
    rest_ref[:, :512] = proj_ref[...]
    rest_ref[:, 512:2560] = fc_ref[...]
    rest_ref[:, 2560:] = out_ref[...]


def pair_kernel(mine_ref, by_zh_ref, by_tp_ref, by_both_ref, out_ref):
    zh, tp = lax.axis_index("zh"), lax.axis_index("tp")
    here = pl.ds(pl.multiple_of(zh * 16, 16), 16)
    there = pl.ds(pl.multiple_of(16 - zh * 16, 16), 16)
    near = pl.ds(pl.multiple_of(tp * 512, 512), 512)
    far_off = pl.ds(pl.multiple_of(512 - tp * 512, 512), 512)
    for rows, ref, other_ref in ((here, mine_ref, by_tp_ref), (there, by_zh_ref, by_both_ref)):
        out_ref[rows, near] = ref[:, :512]
        out_ref[rows, far_off] = other_ref[...]
        out_ref[rows, 1024:] = ref[:, 512:]


def inputs_kernel(lengths_ref, tokens_ref, cotangent_ref, inputs_ref, grad_ref, order_ref):
    feature_order(order_ref)
    inputs_ref[...] = low(dot(tokens_ref[...], order_ref[...]))
    grad = dot(cotangent_ref[...], order_ref[...]) * valid_rows(lengths_ref)
    grad_ref[...] = low(grad)


def qkv_kernel(
    inputs_ref, own_ref, other_ref, bias_ref, heads_ref, own_n_ref, other_n_ref, vectors_ref, normed_ref
):
    for side, ref in ((0, own_ref), (1, other_ref)):
        small = ref[:, 1536:].astype(f32).T[:8]
        for x, lanes in enumerate(core_lanes(side)):
            vectors_ref[:, lanes] = small[:, 128 * x : 128 * (x + 1)]
    norm, _ = norm_parts(inputs_ref[...].astype(f32))
    normed_ref[...] = low(norm * vectors_ref[0:1, :] + vectors_ref[1:2, :])
    own_n_ref[...] = of_core(normed_ref, 0)
    other_n_ref[...] = of_core(normed_ref, 1)
    for c in range(3):
        cols = slice(512 * c, 512 * (c + 1))
        field = dot(own_n_ref[...], own_ref[:, cols]) + dot(other_n_ref[...], other_ref[:, cols])
        if c != 1:
            field = field + bias_ref[c // 2 : c // 2 + 1, :].astype(f32)
        field = low(field).T
        for h in range(8):
            heads_ref[h, 64 * c : 64 * (c + 1), :] = field[64 * h : 64 * (h + 1)]


def attn_end_kernel(heads_ref, weight_ref, inputs_ref, vectors_ref, middle_ref, n_ref, own_ref, wide_ref):
    tp = lax.axis_index("tp")
    for h in range(8):
        for t in range(2):
            at = 512 * t + 64 * h
            wide_ref[at : at + 64, :] = heads_ref[2 * h + t]
        own_ref[64 * h : 64 * (h + 1), :] = heads_ref[2 * h + tp]
    attn_out = contract(wide_ref[...].T, weight_ref[...], 1, 1) + vectors_ref[2:3, :]
    middle = inputs_ref[...].astype(f32) + attn_out
    middle_ref[...] = middle
    norm, _ = norm_parts(middle)
    n_ref[...] = low(norm * vectors_ref[3:4, :] + vectors_ref[4:5, :])


def attention_end(heads_all, rest, inputs, vectors):
    wide = pl.BlockSpec((256, 1024), lambda i: (0, 0))
    return pl.pallas_call(
        attn_end_kernel,
        grid=(1,),
        out_shape=(shape(256, 1024, kind=f32), shape(256, 1024), shape(512, 256)),
        in_specs=[
            pl.BlockSpec((16, 64, 256), lambda i: (0, 0, 0)),
            pl.BlockSpec((1024, 1024), lambda i: (0, 0)),
            wide,
            pl.BlockSpec((8, 1024), lambda i: (0, 0)),
        ],
        out_specs=(wide, wide, pl.BlockSpec((512, 256), lambda i: (0, 0))),
        scratch_shapes=[pltpu.VMEM((1024, 256), bf16)],
        compiler_params=ROOMY,
        cost_estimate=takes(3),
        name="attn_end",
    )(heads_all, far(rest), inputs, vectors)


def grad_act_kernel(gm_ref, weight_ref, out_ref):
    out_ref[...] = dot(gm_ref[...], weight_ref[...])


def grad_activated(grad_mlp, rest):
    return pl.pallas_call(
        grad_act_kernel,
        grid=(4,),
        out_shape=shape(256, 2048, kind=f32),
        in_specs=[
            pl.BlockSpec((256, 1024), lambda i: (0, 0)),
            pl.BlockSpec((1024, 512), lambda i: (0, 6 + i)),
        ],
        out_specs=pl.BlockSpec((256, 512), lambda i: (0, i)),
        compiler_params=ROOMY,
        cost_estimate=takes(3),
        name="grad_act",
    )(grad_mlp, far(rest))


def feed_kernel(n_ref, gact_ref, bias_ref, weight_ref, act_ref, gh_ref, part_ref, total_ref):
    i = pl.program_id(0)

    @pl.when(i == 0)
    def _():
        total_ref[...] = jnp.zeros_like(total_ref)

    halves = (slice(0, 256), slice(256, 512))
    hidden = [
        dot(n_ref[...], weight_ref[:, cols]) + bias_ref[:, cols].astype(f32) for cols in halves
    ]
    for cols, field in zip(halves, hidden):
        value, slope = gelu_pair(field)
        act_ref[:, cols] = low(value)
        gh_ref[:, cols] = low(gact_ref[:, cols] * slope)
    total_ref[...] += contract(gh_ref[...], weight_ref[...], 1, 1)

    @pl.when(i == 3)
    def _():
        part_ref[...] = low(total_ref[...])


def feed_forward(normed_two, grad_act, fc_bias, rest):
    def tile(rows, first):
        return pl.BlockSpec((rows, 512), lambda i: (0, first + i))

    wide = pl.BlockSpec((256, 1024), lambda i: (0, 0))
    return pl.pallas_call(
        feed_kernel,
        grid=(4,),
        out_shape=(shape(256, 2048), shape(256, 2048), shape(256, 1024)),
        in_specs=[wide, tile(256, 0), tile(1, 0), tile(1024, 2)],
        out_specs=(tile(256, 0), tile(256, 0), wide),
        scratch_shapes=[pltpu.VMEM((256, 1024), f32)],
        compiler_params=ROOMY,
        cost_estimate=takes(6),
        name="feed_forward",
    )(normed_two, grad_act, fc_bias, far(rest))


def wide_kernel(n_ref, gh_ref, gm_ref, act_ref, weight_ref, out_ref, part_ref, left_ref, total_ref):
    i = pl.program_id(0)

    @pl.when(i == 0)
    def _():
        left_ref[0] = n_ref[...].T
        left_ref[1] = gm_ref[...].T
        total_ref[...] = jnp.zeros_like(total_ref)

    @pl.when(i < 4)
    def _():
        out_ref[...] = low(dot(left_ref[0], gh_ref[...]))

    @pl.when(i >= 4)
    def _():
        out_ref[...] = low(dot(left_ref[1], act_ref[...]))
        total_ref[...] += contract(act_ref[...], weight_ref[...], 1, 1)

    @pl.when(i == 7)
    def _():
        part_ref[...] = low(total_ref[...])


def wide_grads(normed_two, grad_hidden, grad_mlp, activated, rest):
    whole = pl.BlockSpec((256, 1024), lambda i: (0, 0))
    return pl.pallas_call(
        wide_kernel,
        grid=(8,),
        out_shape=(shape(1024, 4096), shape(256, 1024)),
        in_specs=[
            whole,
            pl.BlockSpec((256, 512), lambda i: (0, jnp.minimum(i, 3))),
            whole,
            pl.BlockSpec((256, 512), lambda i: (0, jnp.maximum(i - 4, 0))),
            pl.BlockSpec((1024, 512), lambda i: (0, 6 + jnp.maximum(i - 4, 0))),
        ],
        out_specs=(pl.BlockSpec((1024, 512), lambda i: (0, i)), whole),
        scratch_shapes=[pltpu.VMEM((2, 1024, 256), bf16), pltpu.VMEM((256, 1024), f32)],
        compiler_params=WHOLE,
        cost_estimate=takes(8),
        name="wide_grads",
    )(normed_two, grad_hidden, grad_mlp, activated, far(rest))


def middle_back_kernel(
    middle_ref, mine_ref, swapped_ref, vectors_ref, gm_ref, weight_ref, out_ref, ga_ref, gheads_ref, cols_ref
):
    gm = gm_ref[...].astype(f32)
    norm, inverse = norm_parts(middle_ref[...])
    grad = mine_ref[...].astype(f32) + swapped_ref[...].astype(f32)
    out = gm + norm_back(grad, vectors_ref[3:4, :], norm, inverse)
    out_ref[...] = out
    low_out = low(out)
    ga_ref[...] = low_out
    tp = lax.axis_index("tp")
    field = low(dot(low_out, weight_ref[:, pl.ds(pl.multiple_of(tp * 512, 512), 512)])).T
    for h in range(8):
        gheads_ref[h] = field[64 * h : 64 * (h + 1)]
    rows = [low_out.astype(f32), grad * norm, grad, gm]
    rows = [jnp.sum(r, axis=0, keepdims=True) for r in rows]
    cols_ref[...] = jnp.concatenate(rows + [jnp.zeros((4, 1024), f32)], axis=0)


def middle_back(middle, mine, swapped, vectors, grad_mlp, rest):
    def whole(*dims):
        return pl.BlockSpec(dims, lambda i: (0,) * len(dims))

    wide = whole(256, 1024)
    return pl.pallas_call(
        middle_back_kernel,
        grid=(1,),
        out_shape=(
            shape(256, 1024, kind=f32),
            shape(256, 1024),
            shape(8, 64, 256),
            shape(8, 1024, kind=f32),
        ),
        in_specs=[wide, wide, wide, whole(8, 1024), wide, whole(1024, 1024)],
        out_specs=(wide, wide, whole(8, 64, 256), whole(8, 1024)),
        compiler_params=ROOMY,
        cost_estimate=takes(3),
        name="middle_back",
    )(middle, mine, swapped, vectors, grad_mlp, far(rest))


def put_block(ref, at, block):
    for g in range(32):
        ref[16 * g : 16 * (g + 1), at : at + 128] = block


def merge_kernel(query_ref, own_ref, other_ref, out_ref):
    out_ref[:, :64, :] = query_ref[...]
    out_ref[:, 64:, :] = low(own_ref[...] + other_ref[...].astype(f32))


def final_kernel(
    lengths_ref, inputs_ref, middle_ref, mine_ref, swapped_ref, vectors_ref, out_ref, roots_ref, order_ref
):
    feature_order(order_ref)
    valid = valid_rows(lengths_ref)
    inputs = inputs_ref[...].astype(f32)
    middle = middle_ref[...]
    mlp_out = mine_ref[...].astype(f32) + swapped_ref[...].astype(f32) + vectors_ref[5:6, :]
    final = middle + mlp_out
    out_ref[...] = low(contract(low(final), order_ref[...], 1, 1))
    lane = lax.broadcasted_iota(jnp.int32, (1, 128), 1)
    total = jnp.zeros((1, 128), f32)
    for k, field in enumerate((inputs, middle - inputs, mlp_out, final)):
        total = jnp.where(lane == k, jnp.sum(valid * field * field), total)
    roots_ref[...] = total


def side_kernel(ga_ref, heads_ref, rows_ref, mine_ref, theirs_ref):
    for side, ref in ((0, mine_ref), (1, theirs_ref)):
        ref[:, :512] = low(contract(of_core(ga_ref, side).T, heads_ref[...], 1, 1))
        cols = jnp.concatenate([of_core(rows_ref, side), jnp.zeros((120, 512), f32)], axis=0)
        ref[:, 512:] = low(cols.T)


def grads_into(ref, normed, grads_ref, sums):
    left = normed.T
    for c in range(3):
        cols = slice(512 * c, 512 * (c + 1))
        ref[:, cols] = low(contract(left, grads_ref[cols, :], 1, 1))
    put_block(ref, 1536, sums[0])
    put_block(ref, 1664, sums[1])


def sum_rows(field, dim, count, extra):
    sums = contract(jnp.ones((8, 256), bf16), field, 1, dim)[0:1]
    sums = [sums[:, 128 * r : 128 * (r + 1)] for r in range(count)]
    return low(jnp.concatenate(sums + extra, axis=0))


def back_kernel(
    gback_ref,
    own_ref,
    other_ref,
    inputs_ref,
    other_n_ref,
    roots_ref,
    gh_ref,
    keep_ref,
    send_ref,
    rows_ref,
    theirs_ref,
    grads_ref,
    sums_ref,
    norm_ref,
    part_ref,
):
    for c in range(3):
        for h in range(8):
            at = 512 * c + 64 * h
            grads_ref[at : at + 64, :] = gback_ref[h, 64 * c : 64 * (c + 1), :]
    sides = [grads_ref[512 * c : 512 * (c + 1), :].T for c in range(3)]
    norm_ref[...], _ = norm_parts(inputs_ref[...].astype(f32))
    for side, ref in ((0, own_ref), (1, other_ref)):
        part = sum(contract(sides[c], ref[:, 512 * c : 512 * (c + 1)], 1, 1) for c in range(3))
        part = low(part)
        for x, lanes in enumerate(core_lanes(side)):
            part_ref[:, lanes] = part[:, 128 * x : 128 * (x + 1)]
        part = part.astype(f32)
        gain = jnp.sum(part * of_core(norm_ref, side), axis=0, keepdims=True)
        shift = jnp.sum(part, axis=0, keepdims=True)
        rows_ref[side] = jnp.concatenate([gain, shift, jnp.zeros((6, 512), f32)], axis=0)
    tp = lax.axis_index("tp")
    keep_ref[...] = part_ref[pl.ds(pl.multiple_of(tp * 128, 128), 128), :]
    send_ref[...] = part_ref[pl.ds(pl.multiple_of(128 - tp * 128, 128), 128), :]
    extra = [roots_ref[...], jnp.zeros((3, 128), f32)]
    sums_ref[0] = sum_rows(grads_ref[...], 1, 12, extra)
    sums_ref[1] = sum_rows(gh_ref[...], 0, 16, [])
    grads_into(theirs_ref, other_n_ref[...], grads_ref, sums_ref)


def core_add_kernel(
    grads_ref, own_n_ref, sums_ref, b_ref, p_ref, q_ref, rows_ref, c_ref, t_ref, d_ref, out_ref, left_ref
):
    i = pl.program_id(0)

    @pl.when(i == 0)
    def _():
        left_ref[...] = own_n_ref[...].T

    rows = pl.ds(pl.multiple_of(i * 128, 128), 128)
    for c in range(3):
        cols = slice(512 * c, 512 * (c + 1))
        mine = low(contract(left_ref[rows, :], grads_ref[cols, :], 1, 1)).astype(f32)
        out_ref[:, cols] = low(mine + b_ref[:, cols].astype(f32))
    for k in range(2):
        at = 1536 + 128 * k
        for g in range(8):
            theirs = b_ref[16 * g : 16 * (g + 1), at : at + 128].astype(f32)
            out_ref[16 * g : 16 * (g + 1), at : at + 128] = low(sums_ref[k].astype(f32) + theirs)
    side = p_ref[...].astype(f32) + q_ref[...].astype(f32)
    out_ref[:, 1792:2304] = low(side[:, :512])
    ln1 = (rows_ref[...] + t_ref[...]) + (c_ref[...] + d_ref[...])
    ln1 = jnp.concatenate([jnp.zeros((4, 128), f32), ln1[:2], jnp.zeros((122, 128), f32)], axis=0)
    out_ref[:, 2304:] = low(side[:, 512:] + ln1.T)


def core_add(grads, own_n, sums, theirs, mine_p, theirs_p, rows, by_core, by_tp, by_both):
    def tall(cols):
        return pl.BlockSpec((128, cols), lambda i: (i, 0))

    flat = pl.BlockSpec((8, 128), lambda i: (0, i))
    return pl.pallas_call(
        core_add_kernel,
        grid=(4,),
        out_shape=shape(512, 2432),
        in_specs=[
            block_of(grads),
            block_of(own_n),
            block_of(sums),
            tall(1792),
            tall(640),
            tall(640),
            flat,
            flat,
            flat,
            flat,
        ],
        out_specs=tall(2432),
        scratch_shapes=[pltpu.VMEM((512, 256), bf16)],
        compiler_params=ROOMY,
        cost_estimate=takes(4),
        name="qkv_core_sum",
    )(grads, far(own_n), sums, theirs, far(mine_p), theirs_p, rows, by_core, by_tp, by_both)


def end_kernel(inputs_ref, gmid_ref, mine_ref, swapped_ref, vectors_ref, out_ref, order_ref):
    feature_order(order_ref)
    rows = pl.ds(pl.multiple_of(lax.axis_index("tp") * 128, 128), 128)
    norm, inverse = norm_parts(inputs_ref[rows, :].astype(f32))
    grad = mine_ref[...].astype(f32) + swapped_ref[...].astype(f32)
    grad = gmid_ref[rows, :] + norm_back(grad, vectors_ref[0:1, :], norm, inverse)
    out_ref[...] = low(contract(low(grad), order_ref[...], 1, 1))


def join_kernel(mine_ref, theirs_ref, out_ref):
    tp = lax.axis_index("tp")
    out_ref[pl.ds(pl.multiple_of(tp * 128, 128), 128), :] = mine_ref[...]
    out_ref[pl.ds(pl.multiple_of(128 - tp * 128, 128), 128), :] = theirs_ref[...]


def total_qkv_kernel(lengths_ref, got_ref, qkv_ref, proj_ref, bias_ref, fc_ref, cols_ref, roots_ref):
    total = got_ref[0].astype(f32)
    for k in range(1, 32):
        total = total + got_ref[k].astype(f32)
    for c in range(3):
        qkv_ref[:, c, :] = total[:, 512 * c : 512 * (c + 1)]
    for k in range(2):
        for r in range(4):
            row = 8 * k + r
            bias_ref[k : k + 1, 128 * r : 128 * (r + 1)] = total[row : row + 1, 1536:1664]
    count = lengths_ref[0] + lengths_ref[1] + lengths_ref[2] + lengths_ref[3]
    mean = total[12:13, 1536:1664] / (count.astype(f32) * 1024.0)
    roots_ref[...] = jnp.sqrt(mean + ROOT_EPS)
    fc_ref[...] = total[:, 1664:1792]
    proj_ref[...] = total[:, 1792:2304]
    cols_ref[...] = total[:, 2304:].T[:8]


def total_wide_kernel(mine_ref, theirs_ref, fc_ref, out_ref):
    total = mine_ref[...].astype(f32) + theirs_ref[...].astype(f32)
    fc_ref[...] = total[:, :2048]
    out_ref[...] = total[:, 2048:]


def body(
    tokens,
    ln1_gain,
    ln1_bias,
    qkv_weight,
    qv_bias,
    proj_weight,
    proj_bias,
    ln2_gain,
    ln2_bias,
    fc_weight,
    fc_bias,
    out_weight,
    out_bias,
    piece_starts,
    seq_lengths,
    cotangent,
):
    vectors = (ln1_gain, ln1_bias, proj_bias, ln2_gain, ln2_bias, out_bias)
    pay_q = call(
        prepare_kernel,
        "weights_payload",
        shape(32, 16, 1664),
        qkv_weight,
        *[v.reshape(1, 16) for v in vectors],
    )
    own_q = exchange(pay_q, SPREAD).reshape(512, 1664)
    proj_rows = proj_weight.T
    pay_r = call(
        prepare_rest_kernel, "rest_payload", shape(16, 4608), proj_rows, fc_weight, out_weight.T
    )
    pair_r = call(
        pair_kernel,
        "rest_pair",
        shape(32, 5120),
        pay_r,
        swap(pay_r, "zh"),
        swap(proj_rows, "tp"),
        lax.ppermute(proj_rows, ("zh", "tp"), [(i, 3 - i) for i in range(4)]),
    )
    rest = lax.all_gather(pair_r, ("x", "c", "y"), axis=0, tiled=True)

    inputs, grad_mlp = call(
        inputs_kernel,
        "inputs",
        (shape(256, 1024), shape(256, 1024)),
        seq_lengths,
        tokens[0],
        cotangent[0],
        scalars=1,
        cost=2,
        scratch=[pltpu.VMEM((1024, 1024), bf16)],
    )
    own_q = after(own_q, inputs)
    other_q = swap(own_q, "c")
    heads, own_n, other_n, vectors = call(
        qkv_kernel,
        "qkv",
        (shape(8, 192, 256), shape(256, 512), shape(256, 512), shape(8, 1024, kind=f32)),
        inputs,
        own_q,
        other_q,
        qv_bias,
        scratch=[pltpu.VMEM((256, 1024), bf16)],
        cost=3,
    )
    own = exchange(heads, LINE)
    other = swap(own[:, 64:], "c")
    attended, attended_low, log_sum = attn_forward(seq_lengths, piece_starts, own, other)
    heads_all = exchange(attended_low.reshape(16, 64, 256), ("zh", "y", "tp"))
    grad_act = grad_activated(grad_mlp, after(rest, attended_low))
    middle, normed_two, heads_out = attention_end(
        heads_all, after(rest, grad_act), inputs, vectors
    )
    activated, grad_hidden, two_part = feed_forward(
        normed_two, grad_act, fc_bias.reshape(1, 2048), rest
    )
    two_swapped = swap(two_part, "tp")
    wide, mlp_part = wide_grads(normed_two, grad_hidden, grad_mlp, activated, rest)
    wide = lax.psum_scatter(
        after(wide, two_swapped), ("x", "c"), scatter_dimension=0, tiled=True
    )
    two_swapped = after(two_swapped, mlp_part)
    grad_middle, grad_attn, grad_heads, rows = middle_back(
        middle, two_part, two_swapped, vectors, grad_mlp, rest
    )
    grad_mine = exchange(grad_heads, LINE)

    mine_p, theirs_p = call(
        side_kernel,
        "proj_grads",
        (shape(512, 640), shape(512, 640)),
        grad_attn,
        far(heads_out),
        rows,
        cost=2,
    )
    grad_mine = after(grad_mine, mine_p)
    theirs_p = swap(after(theirs_p, grad_mine), "c")
    mlp_swapped = swap(after(mlp_part, grad_mine), "tp")

    grad_query, grad_own, grad_other = attn_backward(
        seq_lengths, piece_starts, own, other, grad_mine, attended, log_sum
    )
    grad_other, mlp_swapped = lax.optimization_barrier((grad_other, mlp_swapped))
    grad_back = call(
        merge_kernel, "merge", shape(8, 192, 256), grad_query, grad_own, swap(grad_other, "c")
    )
    grad_back = exchange(grad_back, LINE)
    layer_out, roots = call(
        final_kernel,
        "final",
        (shape(256, 1024), shape(1, 128, kind=f32)),
        seq_lengths,
        far(inputs),
        far(middle),
        after(mlp_part, grad_other),
        mlp_swapped,
        vectors,
        scalars=1,
        cost=3,
        scratch=[pltpu.VMEM((1024, 1024), bf16)],
    )
    one_keep, one_send, rows, theirs_q, grads, sums = call(
        back_kernel,
        "back",
        (
            shape(128, 1024),
            shape(128, 1024),
            shape(2, 8, 512, kind=f32),
            shape(512, 1792),
            shape(1536, 256),
            shape(2, 16, 128),
        ),
        grad_back,
        far(own_q),
        far(other_q),
        far(inputs),
        far(other_n),
        roots,
        far(grad_hidden),
        cost=5,
        scratch=[pltpu.VMEM((256, 1024), f32), pltpu.VMEM((256, 1024), bf16)],
    )
    one_swapped = swap(one_send, "tp")
    wide = lax.psum_scatter(after(wide, roots), "y", scatter_dimension=0, tiled=True)
    both = core_add(
        grads,
        own_n,
        sums,
        after(swap(theirs_q, "c"), one_swapped),
        mine_p,
        theirs_p,
        rows[0],
        swap(rows[1], "c"),
        swap(rows[0], "tp"),
        lax.ppermute(rows[1], ("c", "tp"), [(i, 3 - i) for i in range(4)]),
    )
    got_q = exchange(both.reshape(32, 16, 2432), SPREAD)
    half_tokens = call(
        end_kernel,
        "end",
        shape(128, 1024),
        far(inputs),
        far(grad_middle),
        one_keep,
        one_swapped,
        vectors,
        cost=2,
        scratch=[pltpu.VMEM((1024, 1024), bf16)],
    )
    grad_tokens = call(
        join_kernel, "join", shape(256, 1024), half_tokens, swap(half_tokens, "tp")
    )
    zh = lax.axis_index("zh")
    keep = lax.dynamic_slice_in_dim(wide, zh * 16, 16, 0)
    send = lax.dynamic_slice_in_dim(wide, 16 - zh * 16, 16, 0)
    grad_fc, grad_out = call(
        total_wide_kernel,
        "total_wide",
        (shape(16, 2048, kind=f32), shape(16, 2048, kind=f32)),
        keep,
        swap(send, "zh"),        cost=14,
    )
    got_q = after(got_q, grad_fc, grad_tokens)
    grad_qkv, grad_proj, bias_sums, fc_sums, cols, roots = call(
        total_qkv_kernel,
        "total_qkv",
        (
            shape(16, 3, 512, kind=f32),
            shape(16, 512, kind=f32),
            shape(2, 512, kind=f32),
            shape(16, 128, kind=f32),
            shape(8, 16, kind=f32),
            shape(1, 128, kind=f32),
        ),
        seq_lengths,
        got_q,
        scalars=1,
    )
    return (
        layer_out[None],
        grad_tokens[None],
        cols[4],
        cols[5],
        grad_qkv,
        bias_sums,
        grad_proj.T,
        cols[0],
        cols[1],
        cols[2],
        grad_fc,
        fc_sums.reshape(2048),
        grad_out.T,
        cols[3],
        roots[0, :4],
    )


def solution(mesh):
    fine = Mesh(mesh.devices.reshape(4, 2, 4, 2, 2), ("x", "zh", "y", "c", "tp"))
    ctx = ("zh", "y", "c")
    every = ("x", "zh", "y", "c")
    in_specs = (
        P("x", ctx, None),
        P(every),
        P(every),
        P(every, None, "tp"),
        P(None, "tp"),
        P("tp", every),
        P(every),
        P(every),
        P(every),
        P(every, "tp"),
        P("tp"),
        P("tp", every),
        P(every),
        P("x", None),
        P(),
        P("x", ctx, None),
    )
    out_specs = (
        P("x", ctx, None),
        P("x", ctx, None),
        P(every),
        P(every),
        P(every, None, "tp"),
        P(None, "tp"),
        P("tp", every),
        P(every),
        P(every),
        P(every),
        P(every, "tp"),
        P("tp"),
        P("tp", every),
        P(every),
        P(),
    )
    return jax.shard_map(body, mesh=fine, in_specs=in_specs, out_specs=out_specs, check_vma=False)
```

```python
from functools import partial

import jax
import jax.numpy as jnp
from jax import lax
from jax.experimental import pallas as pl
from jax.experimental.pallas import tpu as pltpu
from jax.sharding import Mesh
from jax.sharding import PartitionSpec as P

f32 = jnp.float32
bf16 = jnp.bfloat16
NORM_EPS = 1e-05
ROOT_EPS = 1e-06
B=256; E=64; NB=16; MASKED=-1e30; PIECE=256

class Facts:
    def __init__(self, lengths_ref, starts_ref):
        self.core = lax.axis_index("c")
        self.items = (self.core, lengths_ref[lax.axis_index("x")], starts_ref[0, 0], starts_ref[0, 1])

    def __getitem__(self, at):
        return self.items[at]


def piece_of(pos, info_ref):
    n0=(pos>=info_ref[2])&(pos<info_ref[2]+PIECE)
    n1=(pos>=info_ref[3])&(pos<info_ref[3]+PIECE)
    return jnp.where(n0,1,0)+jnp.where(n1,2,0)

def allowed_block(key_block, query_block, info_ref):
    kpos=key_block*B+lax.broadcasted_iota(jnp.int32,(B,1),0)
    qpos=query_block*B+lax.broadcasted_iota(jnp.int32,(1,B),1)
    kp=piece_of(kpos,info_ref); qp=piece_of(qpos,info_ref)
    qp=jnp.where(qp==0,-1,qp)
    kp=jnp.where(kpos<info_ref[1],kp,-2)
    kpos=jnp.where(kpos<info_ref[1],kpos,1<<20)
    return (kpos<=qpos)|(kp==qp)

def extra_blocks(p, info_ref):
    edge=(2*p+2)*B
    crosses=((info_ref[2]<edge)&(edge<info_ref[2]+PIECE))|((info_ref[3]<edge)&(edge<info_ref[3]+PIECE))
    return jnp.where((info_ref[0]==1)&(p<NB//2-1)&crosses,1,0)

def dot(a,b): return jnp.dot(a,b,preferred_element_type=f32)

SAFE = 60.0


def split3(row):
    top = row.astype(bf16).astype(f32)
    mid = (row - top).astype(bf16).astype(f32)
    rows = jnp.concatenate([top, mid, row - top - mid, jnp.zeros((13, B), f32)], axis=0)
    return rows.astype(bf16)


def ones_beside(block):
    lane = lax.broadcasted_iota(jnp.int32, (B, 16), 1)
    return jnp.concatenate([block, jnp.where(lane < 3, 1.0, 0.0).astype(bf16)], axis=1)


CHUNK = 1024


def walk(m, odd, extra, step, carry):
    first = pl.multiple_of(m * CHUNK, CHUNK)
    carry = lax.fori_loop(
        0, m, lambda i, c: step(pl.multiple_of(i * CHUNK, CHUNK), CHUNK, 0, c), carry
    )
    carry = step(first, 2 * B * (1 + odd), 2, carry)
    end = pl.multiple_of(first + 2 * B * (1 + odd), B)
    return lax.fori_loop(0, extra, lambda i, c: step(end, B, 1, c), carry)


def masked_from(e, first, count, masked, query_block, info_ref):
    if not masked:
        return e
    keep = count - masked * B
    parts = [e[:keep]] if keep else []
    for at in range(keep, count, B):
        allowed = allowed_block((first + at) // B, query_block, info_ref)
        parts.append(jnp.where(allowed, e[at : at + B], 0.0))
    return jnp.concatenate(parts, axis=0)


def place(block):
    return pl.ds(pl.multiple_of(block * B, B), B)


def walk_all(p, extra, step, carry, chunk):
    end = 2 * B * (p + 1)
    for first in range(0, end, chunk):
        last = min(first + chunk, end)
        carry = step(first, last - first, max(0, last - (end - 2 * B)) // B, carry)
    if p == NB // 2 - 1:
        return carry
    return lax.fori_loop(0, extra, lambda i, c: step(end, B, 1, c), carry)


def forward_kernel(lengths_ref, starts_ref, own_ref, other_ref, out_ref, low_ref, lse_ref, key_ref, value_ref):
    info_ref = Facts(lengths_ref, starts_ref)
    core = info_ref[0]
    sublane = lax.broadcasted_iota(jnp.int32, (16, NB * B), 0)
    value_ref[E:, :] = jnp.where(sublane == 0, 1.0, 0.0).astype(bf16)

    def squares(block):
        field = block.astype(f32)
        return jnp.sum(field * field, axis=0, keepdims=True)

    query_top = jnp.zeros((1, B), f32)
    key_top = jnp.zeros((1, B), f32)
    for p in range(NB // 2):
        mine, theirs = own_ref[p, E : 2 * E, :], other_ref[p, :E, :]
        here, there = place(2 * p + core), place(2 * p + 1 - core)
        key_ref[here, :] = mine.T
        key_ref[there, :] = theirs.T
        value_ref[:E, here] = own_ref[p, 2 * E :, :]
        value_ref[:E, there] = other_ref[p, E:, :]
        query_top = jnp.maximum(query_top, squares(own_ref[p, :E, :]))
        key_top = jnp.maximum(key_top, jnp.maximum(squares(mine), squares(theirs)))
    bound = jnp.max(query_top) * jnp.max(key_top)

    def finish(p, top, acc):
        total = acc[E : E + 1]
        o = acc[:E] / total
        out_ref[p] = o
        low_ref[p, 0] = o.astype(bf16)
        low_ref[p, 1] = o.astype(bf16)
        lse_ref[p] = top + jnp.log(total)

    @pl.when(bound <= (8.0 * SAFE) ** 2)
    def _():
        for p in range(NB // 2):
            query = own_ref[p, :E, :] * jnp.asarray(0.125, bf16)
            qb = 2 * p + core

            def step(first, count, masked, acc):
                e = jnp.exp(dot(key_ref[first : first + count, :], query))
                e = masked_from(e, first, count, masked, qb, info_ref)
                return acc + dot(value_ref[:, first : first + count], e.astype(bf16))

            acc = walk_all(p, extra_blocks(p, info_ref), step, jnp.zeros((E + 16, B), f32), CHUNK)
            finish(p, 0.0, acc)

    @pl.when(bound > (8.0 * SAFE) ** 2)
    def _():
        def one(p, _):
            query = own_ref[p, :E, :] * jnp.asarray(0.125, bf16)
            qb = 2 * p + core

            def step(blocks, masked, carry):
                top, acc = carry
                scores = [dot(key_ref[place(j), :], query) for j in blocks]
                if masked:
                    scores = [
                        jnp.where(allowed_block(j, qb, info_ref), s, MASKED)
                        for j, s in zip(blocks, scores)
                    ]
                new = top
                for s in scores:
                    new = jnp.maximum(new, jnp.max(s, axis=0, keepdims=True))
                acc = acc * jnp.exp(top - new)
                for j, s in zip(blocks, scores):
                    acc = acc + dot(value_ref[:, place(j)], jnp.exp(s - new).astype(bf16))
                return new, acc

            carry = (jnp.full((1, B), MASKED, f32), jnp.zeros((E + 16, B), f32))
            carry = step((2 * p, 2 * p + 1), True, carry)
            carry = lax.fori_loop(0, p, lambda i, c: step((2 * i, 2 * i + 1), False, c), carry)
            carry = lax.fori_loop(
                0, extra_blocks(p, info_ref), lambda i, c: step((2 * p + 2,), True, c), carry
            )
            finish(p, *carry)
            return 0

        lax.fori_loop(0, NB // 2, one, 0)


def backward_kernel(
    lengths_ref,
    starts_ref,
    own_ref,
    other_ref,
    gout_ref,
    out_ref,
    lse_ref,
    gq_ref,
    gown_ref,
    gother_ref,
    key_ref,
    keyt_ref,
    value_ref,
    grad_ref,
):
    info_ref = Facts(lengths_ref, starts_ref)
    core = info_ref[0]
    for p in range(NB // 2):
        mine, theirs = own_ref[p, E : 2 * E, :], other_ref[p, :E, :]
        here, there = place(2 * p + core), place(2 * p + 1 - core)
        keyt_ref[:, here] = mine
        keyt_ref[:, there] = theirs
        key_ref[here, :] = ones_beside(mine.T)
        key_ref[there, :] = ones_beside(theirs.T)
        value_ref[here, :] = ones_beside(own_ref[p, 2 * E :, :].T)
        value_ref[there, :] = ones_beside(other_ref[p, E:, :].T)
    grad_ref[...] = jnp.zeros_like(grad_ref)
    blank = jnp.zeros((B, E), bf16)

    def one(m, odd):
        p = 2 * m + odd
        query = own_ref[p, :E, :] * jnp.asarray(0.125, bf16)
        gout = gout_ref[p]
        delta = jnp.sum(gout.astype(f32) * out_ref[p], axis=0, keepdims=True)
        rows = jnp.concatenate([blank, query.T], axis=1)
        gout_rows = jnp.concatenate([gout.T, blank], axis=1)
        query = jnp.concatenate([query, split3(-lse_ref[p])], axis=0)
        gout = jnp.concatenate([gout, split3(-delta)], axis=0)
        qb = 2 * p + core

        def step(first, count, masked, acc):
            at = pl.ds(first, count)
            e = jnp.exp(dot(key_ref[at, :], query))
            e = masked_from(e, first, count, masked, qb, info_ref)
            gs = (e * dot(value_ref[at, :], gout)).astype(bf16)
            grad_ref[at, :] += dot(e.astype(bf16), gout_rows) + dot(gs, rows)
            return acc + dot(keyt_ref[:, at], gs)

        acc = walk(m, odd, extra_blocks(p, info_ref), step, jnp.zeros((E, B), f32))
        gq_ref[p] = (acc * 0.125).astype(bf16)

    def both(m, _):
        one(m, 0)
        one(m, 1)
        return 0

    lax.fori_loop(0, NB // 4, both, 0)
    for p in range(NB // 2):
        mine = grad_ref[place(2 * p + core), :].T
        theirs = grad_ref[place(2 * p + 1 - core), :].T.astype(bf16)
        gown_ref[p, :E, :] = mine[E:]
        gown_ref[p, E:, :] = mine[:E]
        gother_ref[p, :E, :] = theirs[E:]
        gother_ref[p, E:, :] = theirs[:E]


VM=pl.BlockSpec(memory_space=pltpu.VMEM); SM=pl.BlockSpec(memory_space=pltpu.SMEM)
LIMIT=40*1024*1024
def attn_forward(lengths,starts,own,other):
    H=NB//2
    return pl.pallas_call(forward_kernel,
        out_shape=(jax.ShapeDtypeStruct((H,E,B),f32),jax.ShapeDtypeStruct((H,2,E,B),bf16),jax.ShapeDtypeStruct((H,1,B),f32)),
        in_specs=[SM,SM,VM,VM],out_specs=(VM,VM,VM),
        scratch_shapes=[pltpu.VMEM((NB*B,E),bf16),pltpu.VMEM((E+16,NB*B),bf16)],
        compiler_params=pltpu.CompilerParams(vmem_limit_bytes=LIMIT),
        cost_estimate=takes(8),
        name="attention_forward")(lengths,starts,own,other)
def attn_backward(lengths,starts,own,other,gout,out,lse):
    H=NB//2
    def full(*dims): return pl.BlockSpec(dims,lambda i:(0,)*len(dims))
    return pl.pallas_call(backward_kernel,grid=(1,),
        out_shape=(jax.ShapeDtypeStruct((H,E,B),bf16),jax.ShapeDtypeStruct((H,2*E,B),f32),jax.ShapeDtypeStruct((H,2*E,B),bf16)),
        in_specs=[SM,SM,full(H,192,B),full(H,128,B),full(H,E,B),full(H,E,B),full(H,1,B)],out_specs=(full(H,E,B),full(H,128,B),full(H,128,B)),
        scratch_shapes=[pltpu.VMEM((NB*B,E+16),bf16),pltpu.VMEM((E,NB*B),bf16),pltpu.VMEM((NB*B,E+16),bf16),pltpu.VMEM((NB*B,2*E),f32)],
        compiler_params=pltpu.CompilerParams(vmem_limit_bytes=LIMIT),
        cost_estimate=takes(26),
        name="attention_backward")(lengths,starts,own,other,gout,far(out),lse)


SPREAD = ("x", "y", "zh")
LINE = ("zh", "y")
VM = pl.BlockSpec(memory_space=pltpu.VMEM)
SM = pl.BlockSpec(memory_space=pltpu.SMEM)
ANY = pl.BlockSpec(memory_space=pl.ANY)
ROOMY = pltpu.CompilerParams(vmem_limit_bytes=40 * 1024 * 1024)
WHOLE = pltpu.CompilerParams(vmem_limit_bytes=50 * 1024 * 1024)
ALL = pltpu.CompilerParams(vmem_limit_bytes=62 * 1024 * 1024)


def takes(microseconds):
    return pl.CostEstimate(
        flops=int(microseconds * 1.15e9), bytes_accessed=1 << 20, transcendentals=0
    )


def low(field):
    return field.astype(bf16)


def swap(field, axis):
    return lax.ppermute(field, axis, [(0, 1), (1, 0)])


def exchange(field, axes):
    return lax.all_to_all(field, axes, split_axis=0, concat_axis=0, tiled=True)


def after(field, *others):
    return lax.optimization_barrier((field, *others))[0]


def contract(a, b, dim_a, dim_b):
    return lax.dot_general(a, b, (((dim_a,), (dim_b,)), ((), ())), preferred_element_type=f32)


def shape(*dims, kind=bf16):
    return jax.ShapeDtypeStruct(dims, kind)


def far(field):
    return pltpu.with_memory_space_constraint(field, pltpu.HBM)


def block_of(array):
    dims = len(array.shape)
    return pl.BlockSpec(array.shape, lambda *_: (0,) * dims)


def call(kernel, name, outs, *args, scalars=0, cost=1, scratch=(), memory=ROOMY):
    return pl.pallas_call(
        kernel,
        grid=(1,),
        out_shape=outs,
        in_specs=[SM] * scalars + [block_of(a) for a in args[scalars:]],
        out_specs=jax.tree.map(block_of, outs),
        scratch_shapes=list(scratch),
        compiler_params=memory,
        cost_estimate=takes(cost),
        name=name,
    )(*args)


def feature_order(order_ref):
    place = lax.broadcasted_iota(jnp.int32, (1, 1024), 1)
    x, core, y, zh = place >> 8, (place >> 7) & 1, (place >> 5) & 3, (place >> 4) & 1
    feature = ((((x * 2 + zh) * 4 + y) * 2 + core) << 4) + (place & 15)
    for at in range(0, 1024, 256):
        rows = at + lax.broadcasted_iota(jnp.int32, (256, 1024), 0)
        order_ref[at : at + 256, :] = jnp.where(rows == feature, 1.0, 0.0).astype(bf16)


def core_lanes(side):
    core = lax.axis_index("c") ^ side
    return [pl.ds(pl.multiple_of(256 * x + 128 * core, 128), 128) for x in range(4)]


def of_core(ref, side):
    return jnp.concatenate([ref[:, lanes] for lanes in core_lanes(side)], axis=1)


def valid_rows(lengths_ref):
    ctx = (lax.axis_index("zh") * 4 + lax.axis_index("y")) * 2 + lax.axis_index("c")
    position = ctx * 256 + lax.broadcasted_iota(jnp.int32, (256, 1), 0)
    return jnp.where(position < lengths_ref[lax.axis_index("x")], 1.0, 0.0)


def norm_parts(values):
    center = values - jnp.mean(values, axis=-1, keepdims=True)
    inverse = lax.rsqrt(jnp.mean(center * center, axis=-1, keepdims=True) + NORM_EPS)
    return center * inverse, inverse


def norm_back(grad, gain, norm, inverse):
    scaled = grad * gain
    return inverse * (
        scaled
        - jnp.mean(scaled, axis=-1, keepdims=True)
        - norm * jnp.mean(scaled * norm, axis=-1, keepdims=True)
    )


def gelu_pair(u):
    k = 0.7978845608028654
    square = u * u
    t = jnp.tanh(u * (k + (k * 0.044715) * square))
    half = 0.5 + 0.5 * t
    value = u * half
    slope = half + (0.5 * u) * (1.0 - t * t) * (k + (3 * 0.044715 * k) * square)
    return value, slope


def prepare_kernel(qkv_ref, a_ref, b_ref, c_ref, d_ref, e_ref, g_ref, out_ref):
    rows = [r[...].astype(f32) for r in (a_ref, b_ref, c_ref, d_ref, e_ref, g_ref)]
    small = jnp.concatenate(rows + [jnp.zeros((2, 16), f32)], axis=0).T
    small = low(jnp.concatenate([small, jnp.zeros((16, 120), f32)], axis=1))

    def one(k, _):
        for c in range(3):
            out_ref[k, :, 512 * c : 512 * (c + 1)] = qkv_ref[:, c, :]
        out_ref[k, :, 1536:] = small
        return 0

    lax.fori_loop(0, 32, one, 0)


def prepare_rest_kernel(proj_ref, fc_ref, out_ref, rest_ref):
    rest_ref[:, :512] = proj_ref[...]
    rest_ref[:, 512:2560] = fc_ref[...]
    rest_ref[:, 2560:] = out_ref[...]


def pair_kernel(mine_ref, by_zh_ref, by_tp_ref, by_both_ref, out_ref):
    zh, tp = lax.axis_index("zh"), lax.axis_index("tp")
    here = pl.ds(pl.multiple_of(zh * 16, 16), 16)
    there = pl.ds(pl.multiple_of(16 - zh * 16, 16), 16)
    near = pl.ds(pl.multiple_of(tp * 512, 512), 512)
    far_off = pl.ds(pl.multiple_of(512 - tp * 512, 512), 512)
    for rows, ref, other_ref in ((here, mine_ref, by_tp_ref), (there, by_zh_ref, by_both_ref)):
        out_ref[rows, near] = ref[:, :512]
        out_ref[rows, far_off] = other_ref[...]
        out_ref[rows, 1024:] = ref[:, 512:]


def inputs_kernel(lengths_ref, tokens_ref, cotangent_ref, inputs_ref, grad_ref, order_ref):
    feature_order(order_ref)
    inputs_ref[...] = low(dot(tokens_ref[...], order_ref[...]))
    grad = dot(cotangent_ref[...], order_ref[...]) * valid_rows(lengths_ref)
    grad_ref[...] = low(grad)


def qkv_kernel(
    inputs_ref, own_ref, other_ref, bias_ref, heads_ref, own_n_ref, other_n_ref, vectors_ref, normed_ref
):
    for side, ref in ((0, own_ref), (1, other_ref)):
        small = ref[:, 1536:].astype(f32).T[:8]
        for x, lanes in enumerate(core_lanes(side)):
            vectors_ref[:, lanes] = small[:, 128 * x : 128 * (x + 1)]
    norm, _ = norm_parts(inputs_ref[...].astype(f32))
    normed_ref[...] = low(norm * vectors_ref[0:1, :] + vectors_ref[1:2, :])
    own_n_ref[...] = of_core(normed_ref, 0)
    other_n_ref[...] = of_core(normed_ref, 1)
    for c in range(3):
        cols = slice(512 * c, 512 * (c + 1))
        field = dot(own_n_ref[...], own_ref[:, cols]) + dot(other_n_ref[...], other_ref[:, cols])
        if c != 1:
            field = field + bias_ref[c // 2 : c // 2 + 1, :].astype(f32)
        field = low(field).T
        for h in range(8):
            heads_ref[h, 64 * c : 64 * (c + 1), :] = field[64 * h : 64 * (h + 1)]


def attn_end_kernel(heads_ref, weight_ref, inputs_ref, vectors_ref, middle_ref, n_ref, own_ref, wide_ref):
    tp = lax.axis_index("tp")
    for h in range(8):
        for t in range(2):
            at = 512 * t + 64 * h
            wide_ref[at : at + 64, :] = heads_ref[2 * h + t]
        own_ref[64 * h : 64 * (h + 1), :] = heads_ref[2 * h + tp]
    attn_out = contract(wide_ref[...].T, weight_ref[...], 1, 1) + vectors_ref[2:3, :]
    middle = inputs_ref[...].astype(f32) + attn_out
    middle_ref[...] = middle
    norm, _ = norm_parts(middle)
    n_ref[...] = low(norm * vectors_ref[3:4, :] + vectors_ref[4:5, :])


def attention_end(heads_all, rest, inputs, vectors):
    wide = pl.BlockSpec((256, 1024), lambda i: (0, 0))
    return pl.pallas_call(
        attn_end_kernel,
        grid=(1,),
        out_shape=(shape(256, 1024, kind=f32), shape(256, 1024), shape(512, 256)),
        in_specs=[
            pl.BlockSpec((16, 64, 256), lambda i: (0, 0, 0)),
            pl.BlockSpec((1024, 1024), lambda i: (0, 0)),
            wide,
            pl.BlockSpec((8, 1024), lambda i: (0, 0)),
        ],
        out_specs=(wide, wide, pl.BlockSpec((512, 256), lambda i: (0, 0))),
        scratch_shapes=[pltpu.VMEM((1024, 256), bf16)],
        compiler_params=ROOMY,
        cost_estimate=takes(3),
        name="attn_end",
    )(heads_all, far(rest), far(inputs), vectors)


def grad_act_kernel(gm_ref, weight_ref, out_ref):
    out_ref[...] = dot(gm_ref[...], weight_ref[...])


def grad_activated(grad_mlp, rest):
    return pl.pallas_call(
        grad_act_kernel,
        grid=(4,),
        out_shape=shape(256, 2048, kind=f32),
        in_specs=[
            pl.BlockSpec((256, 1024), lambda i: (0, 0)),
            pl.BlockSpec((1024, 512), lambda i: (0, 6 + i)),
        ],
        out_specs=pl.BlockSpec((256, 512), lambda i: (0, i)),
        compiler_params=ROOMY,
        cost_estimate=takes(3),
        name="grad_act",
    )(far(grad_mlp), far(rest))


def feed_kernel(n_ref, gact_ref, bias_ref, weight_ref, act_ref, gh_ref, part_ref, total_ref):
    i = pl.program_id(0)

    @pl.when(i == 0)
    def _():
        total_ref[...] = jnp.zeros_like(total_ref)

    halves = (slice(0, 256), slice(256, 512))
    hidden = [
        dot(n_ref[...], weight_ref[:, cols]) + bias_ref[:, cols].astype(f32) for cols in halves
    ]
    for cols, field in zip(halves, hidden):
        value, slope = gelu_pair(field)
        act_ref[:, cols] = low(value)
        gh_ref[:, cols] = low(gact_ref[:, cols] * slope)
    total_ref[...] += contract(gh_ref[...], weight_ref[...], 1, 1)

    @pl.when(i == 3)
    def _():
        part_ref[...] = low(total_ref[...])


def feed_forward(normed_two, grad_act, fc_bias, rest):
    def tile(rows, first):
        return pl.BlockSpec((rows, 512), lambda i: (0, first + i))

    wide = pl.BlockSpec((256, 1024), lambda i: (0, 0))
    return pl.pallas_call(
        feed_kernel,
        grid=(4,),
        out_shape=(shape(256, 2048), shape(256, 2048), shape(256, 1024)),
        in_specs=[wide, tile(256, 0), tile(1, 0), tile(1024, 2)],
        out_specs=(tile(256, 0), tile(256, 0), wide),
        scratch_shapes=[pltpu.VMEM((256, 1024), f32)],
        compiler_params=ROOMY,
        cost_estimate=takes(6),
        name="feed_forward",
    )(normed_two, grad_act, fc_bias, far(rest))


def wide_kernel(n_ref, gh_ref, gm_ref, act_ref, weight_ref, out_ref, part_ref, left_ref, total_ref):
    i = pl.program_id(0)

    @pl.when(i == 0)
    def _():
        left_ref[0] = n_ref[...].T
        left_ref[1] = gm_ref[...].T
        total_ref[...] = jnp.zeros_like(total_ref)

    @pl.when(i < 4)
    def _():
        out_ref[...] = low(dot(left_ref[0], gh_ref[...]))

    @pl.when(i >= 4)
    def _():
        out_ref[...] = low(dot(left_ref[1], act_ref[...]))
        total_ref[...] += contract(act_ref[...], weight_ref[...], 1, 1)

    @pl.when(i == 7)
    def _():
        part_ref[...] = low(total_ref[...])


def wide_grads(normed_two, grad_hidden, grad_mlp, activated, rest):
    whole = pl.BlockSpec((256, 1024), lambda i: (0, 0))
    return pl.pallas_call(
        wide_kernel,
        grid=(8,),
        out_shape=(shape(1024, 4096), shape(256, 1024)),
        in_specs=[
            whole,
            pl.BlockSpec((256, 512), lambda i: (0, jnp.minimum(i, 3))),
            whole,
            pl.BlockSpec((256, 512), lambda i: (0, jnp.maximum(i - 4, 0))),
            pl.BlockSpec((1024, 512), lambda i: (0, 6 + jnp.maximum(i - 4, 0))),
        ],
        out_specs=(pl.BlockSpec((1024, 512), lambda i: (0, i)), whole),
        scratch_shapes=[pltpu.VMEM((2, 1024, 256), bf16), pltpu.VMEM((256, 1024), f32)],
        compiler_params=WHOLE,
        cost_estimate=takes(8),
        name="wide_grads",
    )(normed_two, grad_hidden, far(grad_mlp), activated, far(rest))


def middle_back_kernel(
    middle_ref, mine_ref, swapped_ref, vectors_ref, gm_ref, weight_ref, out_ref, ga_ref, gheads_ref, cols_ref
):
    gm = gm_ref[...].astype(f32)
    norm, inverse = norm_parts(middle_ref[...])
    grad = mine_ref[...].astype(f32) + swapped_ref[...].astype(f32)
    out = gm + norm_back(grad, vectors_ref[3:4, :], norm, inverse)
    out_ref[...] = out
    low_out = low(out)
    ga_ref[...] = low_out
    tp = lax.axis_index("tp")
    field = low(dot(low_out, weight_ref[:, pl.ds(pl.multiple_of(tp * 512, 512), 512)])).T
    for h in range(8):
        gheads_ref[h] = field[64 * h : 64 * (h + 1)]
    rows = [low_out.astype(f32), grad * norm, grad, gm]
    rows = [jnp.sum(r, axis=0, keepdims=True) for r in rows]
    cols_ref[...] = jnp.concatenate(rows + [jnp.zeros((4, 1024), f32)], axis=0)


def middle_back(middle, mine, swapped, vectors, grad_mlp, rest):
    def whole(*dims):
        return pl.BlockSpec(dims, lambda i: (0,) * len(dims))

    wide = whole(256, 1024)
    return pl.pallas_call(
        middle_back_kernel,
        grid=(1,),
        out_shape=(
            shape(256, 1024, kind=f32),
            shape(256, 1024),
            shape(8, 64, 256),
            shape(8, 1024, kind=f32),
        ),
        in_specs=[wide, wide, wide, whole(8, 1024), wide, whole(1024, 1024)],
        out_specs=(wide, wide, whole(8, 64, 256), whole(8, 1024)),
        compiler_params=ALL,
        cost_estimate=takes(3),
        name="middle_back",
    )(far(middle), mine, swapped, vectors, far(grad_mlp), far(rest))


def put_block(ref, at, block):
    for g in range(32):
        ref[16 * g : 16 * (g + 1), at : at + 128] = block


def merge_kernel(query_ref, own_ref, other_ref, out_ref):
    out_ref[:, :64, :] = query_ref[...]
    out_ref[:, 64:, :] = low(own_ref[...] + other_ref[...].astype(f32))


def final_kernel(
    lengths_ref, inputs_ref, middle_ref, mine_ref, swapped_ref, vectors_ref, out_ref, roots_ref, order_ref
):
    feature_order(order_ref)
    valid = valid_rows(lengths_ref)
    inputs = inputs_ref[...].astype(f32)
    middle = middle_ref[...]
    mlp_out = mine_ref[...].astype(f32) + swapped_ref[...].astype(f32) + vectors_ref[5:6, :]
    final = middle + mlp_out
    out_ref[...] = low(contract(low(final), order_ref[...], 1, 1))
    lane = lax.broadcasted_iota(jnp.int32, (1, 128), 1)
    total = jnp.zeros((1, 128), f32)
    for k, field in enumerate((inputs, middle - inputs, mlp_out, final)):
        total = jnp.where(lane == k, jnp.sum(valid * field * field), total)
    roots_ref[...] = total


def side_kernel(ga_ref, heads_ref, rows_ref, mine_ref, theirs_ref):
    for side, ref in ((0, mine_ref), (1, theirs_ref)):
        ref[:, :512] = low(contract(of_core(ga_ref, side).T, heads_ref[...], 1, 1))
        cols = jnp.concatenate([of_core(rows_ref, side), jnp.zeros((120, 512), f32)], axis=0)
        ref[:, 512:] = low(cols.T)


def grads_into(ref, normed, grads_ref, sums, rows):
    left = normed.T
    for c in range(3):
        cols = slice(512 * c, 512 * (c + 1))
        ref[:, cols] = low(contract(left, grads_ref[cols, :], 1, 1))
    put_block(ref, 1536, sums[0])
    put_block(ref, 1664, sums[1])
    cols = [jnp.zeros((4, 512), f32), rows[:2], jnp.zeros((122, 512), f32)]
    ref[:, 1792:] = low(jnp.concatenate(cols, axis=0).T)


def sum_rows(field, dim, count, extra):
    sums = contract(jnp.ones((8, 256), bf16), field, 1, dim)[0:1]
    sums = [sums[:, 128 * r : 128 * (r + 1)] for r in range(count)]
    return low(jnp.concatenate(sums + extra, axis=0))


def back_kernel(
    gback_ref,
    own_ref,
    other_ref,
    inputs_ref,
    other_n_ref,
    roots_ref,
    gh_ref,
    keep_ref,
    send_ref,
    rows_ref,
    theirs_ref,
    grads_ref,
    sums_ref,
    norm_ref,
    part_ref,
):
    for c in range(3):
        for h in range(8):
            at = 512 * c + 64 * h
            grads_ref[at : at + 64, :] = gback_ref[h, 64 * c : 64 * (c + 1), :]
    sides = [grads_ref[512 * c : 512 * (c + 1), :].T for c in range(3)]
    norm_ref[...], _ = norm_parts(inputs_ref[...].astype(f32))
    parts = []
    for side, ref in ((0, own_ref), (1, other_ref)):
        part = sum(contract(sides[c], ref[:, 512 * c : 512 * (c + 1)], 1, 1) for c in range(3))
        part = low(part)
        for x, lanes in enumerate(core_lanes(side)):
            part_ref[:, lanes] = part[:, 128 * x : 128 * (x + 1)]
        part = part.astype(f32)
        gain = jnp.sum(part * of_core(norm_ref, side), axis=0, keepdims=True)
        shift = jnp.sum(part, axis=0, keepdims=True)
        parts.append(jnp.concatenate([gain, shift, jnp.zeros((6, 512), f32)], axis=0))
    rows_ref[...] = parts[0]
    tp = lax.axis_index("tp")
    keep_ref[...] = part_ref[pl.ds(pl.multiple_of(tp * 128, 128), 128), :]
    send_ref[...] = part_ref[pl.ds(pl.multiple_of(128 - tp * 128, 128), 128), :]
    extra = [roots_ref[...], jnp.zeros((3, 128), f32)]
    sums_ref[0] = sum_rows(grads_ref[...], 1, 12, extra)
    sums_ref[1] = sum_rows(gh_ref[...], 0, 16, [])
    grads_into(theirs_ref, other_n_ref[...], grads_ref, sums_ref, parts[1])


def core_add_kernel(
    grads_ref, own_n_ref, sums_ref, b_ref, p_ref, q_ref, rows_ref, out_ref, left_ref
):
    i = pl.program_id(0)

    @pl.when(i == 0)
    def _():
        left_ref[...] = own_n_ref[...].T

    rows = pl.ds(pl.multiple_of(i * 128, 128), 128)
    for c in range(3):
        cols = slice(512 * c, 512 * (c + 1))
        mine = low(contract(left_ref[rows, :], grads_ref[cols, :], 1, 1)).astype(f32)
        out_ref[:, cols] = low(mine + b_ref[:, cols].astype(f32))
    for k in range(2):
        at = 1536 + 128 * k
        for g in range(8):
            theirs = b_ref[16 * g : 16 * (g + 1), at : at + 128].astype(f32)
            out_ref[16 * g : 16 * (g + 1), at : at + 128] = low(sums_ref[k].astype(f32) + theirs)
    side = p_ref[...].astype(f32) + q_ref[...].astype(f32)
    out_ref[:, 1792:2304] = low(side[:, :512])
    ln1 = jnp.concatenate([jnp.zeros((4, 128), f32), rows_ref[:2], jnp.zeros((122, 128), f32)], axis=0)
    both = low(ln1.T).astype(f32) + b_ref[:, 1792:].astype(f32)
    out_ref[:, 2304:] = low(side[:, 512:] + both)


def core_add(grads, own_n, sums, theirs, mine_p, theirs_p, rows):
    def tall(cols):
        return pl.BlockSpec((128, cols), lambda i: (i, 0))

    flat = pl.BlockSpec((8, 128), lambda i: (0, i))
    return pl.pallas_call(
        core_add_kernel,
        grid=(4,),
        out_shape=shape(512, 2432),
        in_specs=[
            block_of(grads),
            block_of(own_n),
            block_of(sums),
            tall(1920),
            tall(640),
            tall(640),
            flat,
        ],
        out_specs=tall(2432),
        scratch_shapes=[pltpu.VMEM((512, 256), bf16)],
        compiler_params=ALL,
        cost_estimate=takes(4),
        name="qkv_core_sum",
    )(grads, far(own_n), sums, theirs, far(mine_p), theirs_p, rows)


def end_kernel(inputs_ref, gmid_ref, mine_ref, swapped_ref, vectors_ref, out_ref, order_ref):
    feature_order(order_ref)
    rows = pl.ds(pl.multiple_of(lax.axis_index("tp") * 128, 128), 128)
    norm, inverse = norm_parts(inputs_ref[rows, :].astype(f32))
    grad = mine_ref[...].astype(f32) + swapped_ref[...].astype(f32)
    grad = gmid_ref[rows, :] + norm_back(grad, vectors_ref[0:1, :], norm, inverse)
    out_ref[...] = low(contract(low(grad), order_ref[...], 1, 1))


def join_kernel(mine_ref, theirs_ref, out_ref):
    tp = lax.axis_index("tp")
    out_ref[pl.ds(pl.multiple_of(tp * 128, 128), 128), :] = mine_ref[...]
    out_ref[pl.ds(pl.multiple_of(128 - tp * 128, 128), 128), :] = theirs_ref[...]


def total_qkv_kernel(lengths_ref, got_ref, qkv_ref, proj_ref, bias_ref, fc_ref, roots_ref):
    total = got_ref[0].astype(f32)
    for k in range(1, 32):
        total = total + got_ref[k].astype(f32)
    for c in range(3):
        qkv_ref[:, c, :] = total[:, 512 * c : 512 * (c + 1)]
    for k in range(2):
        for r in range(4):
            row = 8 * k + r
            bias_ref[k : k + 1, 128 * r : 128 * (r + 1)] = total[row : row + 1, 1536:1664]
    count = lengths_ref[0] + lengths_ref[1] + lengths_ref[2] + lengths_ref[3]
    mean = total[12:13, 1536:1664] / (count.astype(f32) * 1024.0)
    roots_ref[...] = jnp.sqrt(mean + ROOT_EPS)
    fc_ref[...] = total[:, 1664:1792]
    proj_ref[...] = total[:, 1792:2304]


def total_cols_kernel(got_ref, cols_ref):
    total = got_ref[0].astype(f32)
    for k in range(1, 32):
        total = total + got_ref[k].astype(f32)
    cols_ref[...] = total.T[:8]


def total_cols(got):
    return pl.pallas_call(
        total_cols_kernel,
        grid=(1,),
        out_shape=shape(8, 16, kind=f32),
        in_specs=[pl.BlockSpec((32, 16, 128), lambda i: (0, 0, 18))],
        out_specs=pl.BlockSpec((8, 16), lambda i: (0, 0)),
        compiler_params=ROOMY,
        cost_estimate=takes(1),
        name="total_cols",
    )(got)


def total_wide_kernel(mine_ref, theirs_ref, fc_ref, out_ref):
    total = mine_ref[...].astype(f32) + theirs_ref[...].astype(f32)
    fc_ref[...] = total[:, :2048]
    out_ref[...] = total[:, 2048:]


def body(
    tokens,
    ln1_gain,
    ln1_bias,
    qkv_weight,
    qv_bias,
    proj_weight,
    proj_bias,
    ln2_gain,
    ln2_bias,
    fc_weight,
    fc_bias,
    out_weight,
    out_bias,
    piece_starts,
    seq_lengths,
    cotangent,
):
    vectors = (ln1_gain, ln1_bias, proj_bias, ln2_gain, ln2_bias, out_bias)
    pay_q = call(
        prepare_kernel,
        "weights_payload",
        shape(32, 16, 1664),
        qkv_weight,
        *[v.reshape(1, 16) for v in vectors],
    )
    own_q = exchange(pay_q, SPREAD).reshape(512, 1664)
    proj_rows = proj_weight.T
    pay_r = call(
        prepare_rest_kernel, "rest_payload", shape(16, 4608), proj_rows, fc_weight, out_weight.T
    )
    pair_r = call(
        pair_kernel,
        "rest_pair",
        shape(32, 5120),
        after(pay_r, pay_q),
        swap(pay_r, "zh"),
        swap(proj_rows, "tp"),
        lax.ppermute(proj_rows, ("zh", "tp"), [(i, 3 - i) for i in range(4)]),
    )
    rest = lax.all_gather(pair_r, ("x", "c", "y"), axis=0, tiled=True)

    inputs, grad_mlp = call(
        inputs_kernel,
        "inputs",
        (shape(256, 1024), shape(256, 1024)),
        seq_lengths,
        tokens[0],
        cotangent[0],
        scalars=1,
        cost=2,
        scratch=[pltpu.VMEM((1024, 1024), bf16)],
    )
    own_q = after(own_q, inputs)
    other_q = swap(own_q, "c")
    heads, own_n, other_n, vectors = call(
        qkv_kernel,
        "qkv",
        (shape(8, 192, 256), shape(256, 512), shape(256, 512), shape(8, 1024, kind=f32)),
        far(inputs),
        own_q,
        other_q,
        qv_bias,
        scratch=[pltpu.VMEM((256, 1024), bf16)],
        cost=3,
    )
    own = exchange(heads, LINE)
    other = swap(own[:, 64:], "c")
    attended, attended_low, log_sum = attn_forward(seq_lengths, piece_starts, own, other)
    heads_all = exchange(attended_low.reshape(16, 64, 256), ("zh", "y", "tp"))
    grad_act = grad_activated(grad_mlp, after(rest, attended_low))
    middle, normed_two, heads_out = attention_end(
        heads_all, after(rest, grad_act), inputs, vectors
    )
    activated, grad_hidden, two_part = feed_forward(
        normed_two, grad_act, fc_bias.reshape(1, 2048), rest
    )
    two_swapped = swap(two_part, "tp")
    wide, mlp_part = wide_grads(normed_two, grad_hidden, grad_mlp, activated, rest)
    wide = lax.psum_scatter(
        after(wide, two_swapped), ("x", "c"), scatter_dimension=0, tiled=True
    )
    two_swapped = after(two_swapped, mlp_part)
    grad_middle, grad_attn, grad_heads, rows = middle_back(
        middle, two_part, two_swapped, vectors, grad_mlp, rest
    )
    grad_mine = exchange(grad_heads, LINE)

    mine_p, theirs_p = call(
        side_kernel,
        "proj_grads",
        (shape(512, 640), shape(512, 640)),
        far(grad_attn),
        far(heads_out),
        rows,
        cost=2,
    )
    grad_mine = after(grad_mine, mine_p)
    theirs_p = swap(after(theirs_p, grad_mine), "c")
    mlp_swapped = swap(after(mlp_part, grad_mine), "tp")

    grad_query, grad_own, grad_other = attn_backward(
        seq_lengths, piece_starts, own, other, grad_mine, attended, log_sum
    )
    grad_other, mlp_swapped = lax.optimization_barrier((grad_other, mlp_swapped))
    grad_back = call(
        merge_kernel, "merge", shape(8, 192, 256), grad_query, grad_own, swap(grad_other, "c")
    )
    grad_back = exchange(grad_back, LINE)
    layer_out, roots = call(
        final_kernel,
        "final",
        (shape(256, 1024), shape(1, 128, kind=f32)),
        seq_lengths,
        far(inputs),
        far(middle),
        after(mlp_part, grad_other),
        mlp_swapped,
        vectors,
        scalars=1,
        cost=3,
        scratch=[pltpu.VMEM((1024, 1024), bf16)],
    )
    one_keep, one_send, rows, theirs_q, grads, sums = call(
        back_kernel,
        "back",
        (
            shape(128, 1024),
            shape(128, 1024),
            shape(8, 512, kind=f32),
            shape(512, 1920),
            shape(1536, 256),
            shape(2, 16, 128),
        ),
        grad_back,
        far(own_q),
        far(other_q),
        far(inputs),
        far(other_n),
        roots,
        far(grad_hidden),
        cost=5,
        scratch=[pltpu.VMEM((256, 1024), f32), pltpu.VMEM((256, 1024), bf16)],
        memory=ALL,
    )
    one_swapped = swap(one_send, "tp")
    wide = lax.psum_scatter(after(wide, roots), "y", scatter_dimension=0, tiled=True)
    both = core_add(
        grads,
        own_n,
        sums,
        after(swap(theirs_q, "c"), one_swapped),
        mine_p,
        theirs_p,
        rows,
    )
    got_q = exchange(both.reshape(32, 16, 2432), SPREAD)
    half_tokens = call(
        end_kernel,
        "end",
        shape(128, 1024),
        far(inputs),
        far(grad_middle),
        one_keep,
        one_swapped,
        vectors,
        cost=2,
        scratch=[pltpu.VMEM((1024, 1024), bf16)],
    )
    grad_tokens = call(
        join_kernel, "join", shape(256, 1024), half_tokens, swap(half_tokens, "tp")
    )
    zh = lax.axis_index("zh")
    keep = lax.dynamic_slice_in_dim(wide, zh * 16, 16, 0)
    send = lax.dynamic_slice_in_dim(wide, 16 - zh * 16, 16, 0)
    grad_fc, grad_out = call(
        total_wide_kernel,
        "total_wide",
        (shape(16, 2048, kind=f32), shape(16, 2048, kind=f32)),
        keep,
        swap(send, "zh"),        cost=14,
    )
    got_q = after(got_q, grad_fc, grad_tokens)
    cols = total_cols(got_q)
    ln1 = cols[4:6]
    grad_qkv, grad_proj, bias_sums, fc_sums, roots = call(
        total_qkv_kernel,
        "total_qkv",
        (
            shape(16, 3, 512, kind=f32),
            shape(16, 512, kind=f32),
            shape(2, 512, kind=f32),
            shape(16, 128, kind=f32),
            shape(1, 128, kind=f32),
        ),
        seq_lengths,
        after(got_q, cols),
        scalars=1,
    )
    ln1 = ln1 + swap(ln1, "tp")
    return (
        layer_out[None],
        grad_tokens[None],
        ln1[0],
        ln1[1],
        grad_qkv,
        bias_sums,
        grad_proj.T,
        cols[0],
        cols[1],
        cols[2],
        grad_fc,
        fc_sums.reshape(2048),
        grad_out.T,
        cols[3],
        roots[0, :4],
    )


def solution(mesh):
    fine = Mesh(mesh.devices.reshape(4, 2, 4, 2, 2), ("x", "zh", "y", "c", "tp"))
    ctx = ("zh", "y", "c")
    every = ("x", "zh", "y", "c")
    in_specs = (
        P("x", ctx, None),
        P(every),
        P(every),
        P(every, None, "tp"),
        P(None, "tp"),
        P("tp", every),
        P(every),
        P(every),
        P(every),
        P(every, "tp"),
        P("tp"),
        P("tp", every),
        P(every),
        P("x", None),
        P(),
        P("x", ctx, None),
    )
    out_specs = (
        P("x", ctx, None),
        P("x", ctx, None),
        P(every),
        P(every),
        P(every, None, "tp"),
        P(None, "tp"),
        P("tp", every),
        P(every),
        P(every),
        P(every),
        P(every, "tp"),
        P("tp"),
        P("tp", every),
        P(every),
        P(),
    )
    return jax.shard_map(body, mesh=fine, in_specs=in_specs, out_specs=out_specs, check_vma=False)
```

```python
from functools import partial

import jax
import jax.numpy as jnp
from jax import lax
from jax.experimental import pallas as pl
from jax.experimental.pallas import tpu as pltpu
from jax.sharding import Mesh
from jax.sharding import PartitionSpec as P

f32 = jnp.float32
bf16 = jnp.bfloat16
NORM_EPS = 1e-05
ROOT_EPS = 1e-06
B=256; E=64; NB=16; MASKED=-1e30; PIECE=256

class Facts:
    def __init__(self, lengths_ref, starts_ref):
        self.core = lax.axis_index("c")
        self.items = (self.core, lengths_ref[lax.axis_index("x")], starts_ref[0, 0], starts_ref[0, 1])

    def __getitem__(self, at):
        return self.items[at]


def piece_of(pos, info_ref):
    n0=(pos>=info_ref[2])&(pos<info_ref[2]+PIECE)
    n1=(pos>=info_ref[3])&(pos<info_ref[3]+PIECE)
    return jnp.where(n0,1,0)+jnp.where(n1,2,0)

def allowed_block(key_block, query_block, info_ref):
    kpos=key_block*B+lax.broadcasted_iota(jnp.int32,(B,1),0)
    qpos=query_block*B+lax.broadcasted_iota(jnp.int32,(1,B),1)
    kp=piece_of(kpos,info_ref); qp=piece_of(qpos,info_ref)
    qp=jnp.where(qp==0,-1,qp)
    kp=jnp.where(kpos<info_ref[1],kp,-2)
    kpos=jnp.where(kpos<info_ref[1],kpos,1<<20)
    return (kpos<=qpos)|(kp==qp)

def extra_blocks(p, info_ref):
    edge=(2*p+2)*B
    crosses=((info_ref[2]<edge)&(edge<info_ref[2]+PIECE))|((info_ref[3]<edge)&(edge<info_ref[3]+PIECE))
    return jnp.where((info_ref[0]==1)&(p<NB//2-1)&crosses,1,0)

def dot(a,b): return jnp.dot(a,b,preferred_element_type=f32)

SAFE = 60.0


def split3(row):
    top = row.astype(bf16).astype(f32)
    mid = (row - top).astype(bf16).astype(f32)
    rows = jnp.concatenate([top, mid, row - top - mid, jnp.zeros((13, row.shape[1]), f32)], axis=0)
    return rows.astype(bf16)


def ones_beside(block):
    lane = lax.broadcasted_iota(jnp.int32, (B, 16), 1)
    return jnp.concatenate([block, jnp.where(lane < 3, 1.0, 0.0).astype(bf16)], axis=1)


CHUNK = 4 * B


def pair_allowed(m, info_ref):
    key = m * CHUNK + lax.broadcasted_iota(jnp.int32, (CHUNK, 1), 0)
    lane = lax.broadcasted_iota(jnp.int32, (1, 2 * B), 1)
    query = (4 * m + info_ref[0]) * B + lane + jnp.where(lane >= B, B, 0)
    key_piece, query_piece = piece_of(key, info_ref), piece_of(query, info_ref)
    query_piece = jnp.where(query_piece == 0, -1, query_piece)
    valid = key < info_ref[1]
    key_piece = jnp.where(valid, key_piece, -2)
    key = jnp.where(valid, key, 1 << 20)
    return (key <= query) | (key_piece == query_piece)


def pair_of(ref, m):
    return jnp.concatenate([ref[2 * m], ref[2 * m + 1]], axis=1)


def walk(m, extra, step, beyond, carry):
    def chunk(i, c):
        return step(pl.multiple_of(i * CHUNK, CHUNK), None, c)

    carry = lax.fori_loop(0, m, chunk, carry)
    first = pl.multiple_of(m * CHUNK, CHUNK)
    carry = step(first, m, carry)
    second = lax.fori_loop(
        0, extra, lambda i, c: beyond(pl.multiple_of(first + CHUNK, B), c), carry[:, B:]
    )
    return carry[:, :B], second


def masked_from(e, first, count, masked, query_block, info_ref):
    if not masked:
        return e
    keep = count - masked * B
    parts = [e[:keep]] if keep else []
    for at in range(keep, count, B):
        allowed = allowed_block((first >> 8) + at // B, query_block, info_ref)
        parts.append(jnp.where(allowed, e[at : at + B], 0.0))
    return jnp.concatenate(parts, axis=0)


def place(block):
    return pl.ds(pl.multiple_of(block * B, B), B)


def walk_all(p, extra, step, carry, chunk):
    end = 2 * B * (p + 1)
    for first in range(0, end, chunk):
        last = min(first + chunk, end)
        carry = step(first, last - first, max(0, last - (end - 2 * B)) // B, carry)
    if p == NB // 2 - 1:
        return carry
    return lax.fori_loop(0, extra, lambda i, c: step(end, B, 1, c), carry)


def forward_kernel(lengths_ref, starts_ref, own_ref, other_ref, out_ref, low_ref, lse_ref, key_ref, value_ref):
    info_ref = Facts(lengths_ref, starts_ref)
    core = info_ref[0]
    sublane = lax.broadcasted_iota(jnp.int32, (16, NB * B), 0)
    value_ref[E:, :] = jnp.where(sublane == 0, 1.0, 0.0).astype(bf16)

    def squares(block):
        field = block.astype(f32)
        return jnp.sum(field * field, axis=0, keepdims=True)

    query_top = jnp.zeros((1, B), f32)
    key_top = jnp.zeros((1, B), f32)
    for p in range(NB // 2):
        mine, theirs = own_ref[p, E : 2 * E, :], other_ref[p, :E, :]
        here, there = place(2 * p + core), place(2 * p + 1 - core)
        key_ref[here, :] = mine.T
        key_ref[there, :] = theirs.T
        value_ref[:E, here] = own_ref[p, 2 * E :, :]
        value_ref[:E, there] = other_ref[p, E:, :]
        query_top = jnp.maximum(query_top, squares(own_ref[p, :E, :]))
        key_top = jnp.maximum(key_top, jnp.maximum(squares(mine), squares(theirs)))
    bound = jnp.max(query_top) * jnp.max(key_top)

    def finish(p, top, acc):
        total = acc[E : E + 1]
        o = acc[:E] / total
        out_ref[p] = o
        low_ref[p, 0] = o.astype(bf16)
        low_ref[p, 1] = o.astype(bf16)
        lse_ref[p] = top + jnp.log(total)

    @pl.when(bound <= (8.0 * SAFE) ** 2)
    def _():
        def both(m, _):
            query = pair_of(own_ref.at[:, :E, :], m) * jnp.asarray(0.125, bf16)

            def step(first, masked, acc):
                at = pl.ds(first, CHUNK)
                e = jnp.exp(dot(key_ref[at, :], query))
                if masked is not None:
                    e = jnp.where(pair_allowed(masked, info_ref), e, 0.0)
                return acc + dot(value_ref[:, at], e.astype(bf16))

            def beyond(first, acc):
                at = pl.ds(first, B)
                e = jnp.exp(dot(key_ref[at, :], query[:, B:]))
                e = jnp.where(allowed_block(4 * m + 4, 4 * m + 2 + core, info_ref), e, 0.0)
                return acc + dot(value_ref[:, at], e.astype(bf16))

            accs = walk(
                m, extra_blocks(2 * m + 1, info_ref), step, beyond, jnp.zeros((E + 16, 2 * B), f32)
            )
            for odd in range(2):
                finish(2 * m + odd, 0.0, accs[odd])
            return 0

        lax.fori_loop(0, NB // 4, both, 0)

    @pl.when(bound > (8.0 * SAFE) ** 2)
    def _():
        def one(p, _):
            query = own_ref[p, :E, :] * jnp.asarray(0.125, bf16)
            qb = 2 * p + core

            def step(blocks, masked, carry):
                top, acc = carry
                scores = [dot(key_ref[place(j), :], query) for j in blocks]
                if masked:
                    scores = [
                        jnp.where(allowed_block(j, qb, info_ref), s, MASKED)
                        for j, s in zip(blocks, scores)
                    ]
                new = top
                for s in scores:
                    new = jnp.maximum(new, jnp.max(s, axis=0, keepdims=True))
                acc = acc * jnp.exp(top - new)
                for j, s in zip(blocks, scores):
                    acc = acc + dot(value_ref[:, place(j)], jnp.exp(s - new).astype(bf16))
                return new, acc

            carry = (jnp.full((1, B), MASKED, f32), jnp.zeros((E + 16, B), f32))
            carry = step((2 * p, 2 * p + 1), True, carry)
            carry = lax.fori_loop(0, p, lambda i, c: step((2 * i, 2 * i + 1), False, c), carry)
            carry = lax.fori_loop(
                0, extra_blocks(p, info_ref), lambda i, c: step((2 * p + 2,), True, c), carry
            )
            finish(p, *carry)
            return 0

        lax.fori_loop(0, NB // 2, one, 0)


def stage_kernel(own_ref, other_ref, lse_ref, key_ref, keyt_ref, value_ref, query_ref, rows_ref):
    core = lax.axis_index("c")
    blank = jnp.zeros((B, E), bf16)
    for p in range(NB // 2):
        mine, theirs = own_ref[p, E : 2 * E, :], other_ref[p, :E, :]
        here, there = place(2 * p + core), place(2 * p + 1 - core)
        keyt_ref[:, here] = mine
        keyt_ref[:, there] = theirs
        key_ref[here, :] = ones_beside(mine.T)
        key_ref[there, :] = ones_beside(theirs.T)
        value_ref[here, :] = ones_beside(own_ref[p, 2 * E :, :].T)
        value_ref[there, :] = ones_beside(other_ref[p, E:, :].T)
        query = own_ref[p, :E, :] * jnp.asarray(0.125, bf16)
        query_ref[p, :E, :] = query
        query_ref[p, E:, :] = split3(-lse_ref[p])
        rows_ref[p] = jnp.concatenate([blank, query.T], axis=1)


def backward_kernel(
    lengths_ref,
    starts_ref,
    key_ref,
    keyt_ref,
    value_ref,
    query_ref,
    rows_ref,
    gout_ref,
    out_ref,
    gq_ref,
    gown_ref,
    gother_ref,
    grad_ref,
    gouts_ref,
    grows_ref,
    sum_ref,
):
    info_ref = Facts(lengths_ref, starts_ref)
    core = info_ref[0]
    grad_ref[...] = jnp.zeros_like(grad_ref)
    blank = jnp.zeros((B, E), bf16)
    for p in range(NB // 2):
        gout = gout_ref[p]
        delta = jnp.sum(gout.astype(f32) * out_ref[p], axis=0, keepdims=True)
        gouts_ref[p, :E, :] = gout
        gouts_ref[p, E:, :] = split3(-delta)
        grows_ref[p] = jnp.concatenate([gout.T, blank], axis=1)
    sum_ref[...] = jnp.zeros_like(sum_ref)

    def chunk(p, first, count, masked):
        at = pl.ds(pl.multiple_of(first, B), count)
        e = jnp.exp(dot(key_ref[at, :], query_ref[p]))
        if masked:
            e = masked_from(e, first, count, masked, 2 * p + core, info_ref)
        gs = (e * dot(value_ref[at, :], gouts_ref[p])).astype(bf16)
        grad_ref[at, :] += dot(e.astype(bf16), grows_ref[p]) + dot(gs, rows_ref[p])
        sum_ref[p] += dot(keyt_ref[:, at], gs)

    def both(m, _):
        top = NB // 2 - 1 - m
        for k in range(NB // 2 - 1):
            late = k < top
            chunk(jnp.where(late, top, m), 2 * B * jnp.where(late, k, k - top), 2 * B, 0)
        chunk(top, 2 * B * top, 2 * B, 2)
        chunk(m, 2 * B * m, 2 * B, 2)
        return 0

    lax.fori_loop(0, NB // 4, both, 0)

    def beyond(p, _):
        def add(i, _):
            chunk(p, 2 * B * (p + 1), B, 1)
            return 0

        return lax.fori_loop(0, extra_blocks(p, info_ref), add, 0)

    lax.fori_loop(0, NB // 2 - 1, beyond, 0)
    for p in range(NB // 2):
        gq_ref[p] = (sum_ref[p] * 0.125).astype(bf16)
    for p in range(NB // 2):
        mine = grad_ref[place(2 * p + core), :].T
        theirs = grad_ref[place(2 * p + 1 - core), :].T.astype(bf16)
        gown_ref[p, :E, :] = mine[E:]
        gown_ref[p, E:, :] = mine[:E]
        gother_ref[p, :E, :] = theirs[E:]
        gother_ref[p, E:, :] = theirs[:E]


VM=pl.BlockSpec(memory_space=pltpu.VMEM); SM=pl.BlockSpec(memory_space=pltpu.SMEM)
LIMIT=40*1024*1024
def attn_forward(lengths,starts,own,other):
    H=NB//2
    return pl.pallas_call(forward_kernel,
        out_shape=(jax.ShapeDtypeStruct((H,E,B),f32),jax.ShapeDtypeStruct((H,2,E,B),bf16),jax.ShapeDtypeStruct((H,1,B),f32)),
        in_specs=[SM,SM,VM,VM],out_specs=(VM,VM,VM),
        scratch_shapes=[pltpu.VMEM((NB*B,E),bf16),pltpu.VMEM((E+16,NB*B),bf16)],
        compiler_params=pltpu.CompilerParams(vmem_limit_bytes=LIMIT),
        cost_estimate=takes(8),
        name="attention_forward")(lengths,starts,own,other)
def attn_stage(own, other, lse):
    half = NB // 2
    outs = (
        jax.ShapeDtypeStruct((NB * B, E + 16), bf16),
        jax.ShapeDtypeStruct((E, NB * B), bf16),
        jax.ShapeDtypeStruct((NB * B, E + 16), bf16),
        jax.ShapeDtypeStruct((half, E + 16, B), bf16),
        jax.ShapeDtypeStruct((half, B, 2 * E), bf16),
    )
    return pl.pallas_call(
        stage_kernel,
        out_shape=outs,
        in_specs=[VM] * 3,
        out_specs=(VM,) * 5,
        compiler_params=pltpu.CompilerParams(vmem_limit_bytes=LIMIT),
        cost_estimate=takes(1),
        name="attention_stage",
    )(own, other, lse)


def attn_backward(lengths, starts, staged, gout, out):
    half = NB // 2

    def full(array):
        return pl.BlockSpec(array.shape, lambda i: (0,) * len(array.shape))

    outs = (
        jax.ShapeDtypeStruct((half, E, B), bf16),
        jax.ShapeDtypeStruct((half, 2 * E, B), f32),
        jax.ShapeDtypeStruct((half, 2 * E, B), bf16),
    )
    return pl.pallas_call(
        backward_kernel,
        grid=(1,),
        out_shape=outs,
        in_specs=[SM, SM] + [full(x) for x in (*staged, gout, out)],
        out_specs=tuple(full(x) for x in outs),
        scratch_shapes=[
            pltpu.VMEM((NB * B, 2 * E), f32),
            pltpu.VMEM((half, E + 16, B), bf16),
            pltpu.VMEM((half, B, 2 * E), bf16),
            pltpu.VMEM((half, E, B), f32),
        ],
        compiler_params=pltpu.CompilerParams(vmem_limit_bytes=LIMIT),
        cost_estimate=takes(26),
        name="attention_backward",
    )(lengths, starts, *[far(x) for x in staged], gout, far(out))


SPREAD = ("x", "y", "zh")
LINE = ("zh", "y")
VM = pl.BlockSpec(memory_space=pltpu.VMEM)
SM = pl.BlockSpec(memory_space=pltpu.SMEM)
ANY = pl.BlockSpec(memory_space=pl.ANY)
ROOMY = pltpu.CompilerParams(vmem_limit_bytes=40 * 1024 * 1024)
WHOLE = pltpu.CompilerParams(vmem_limit_bytes=50 * 1024 * 1024)
ALL = pltpu.CompilerParams(vmem_limit_bytes=62 * 1024 * 1024)


def takes(microseconds):
    return pl.CostEstimate(
        flops=int(microseconds * 1.15e9), bytes_accessed=1 << 20, transcendentals=0
    )


def low(field):
    return field.astype(bf16)


def swap(field, axis):
    return lax.ppermute(field, axis, [(0, 1), (1, 0)])


def exchange(field, axes):
    return lax.all_to_all(field, axes, split_axis=0, concat_axis=0, tiled=True)


def after(field, *others):
    return lax.optimization_barrier((field, *others))[0]


def contract(a, b, dim_a, dim_b):
    return lax.dot_general(a, b, (((dim_a,), (dim_b,)), ((), ())), preferred_element_type=f32)


def shape(*dims, kind=bf16):
    return jax.ShapeDtypeStruct(dims, kind)


def far(field):
    return pltpu.with_memory_space_constraint(field, pltpu.HBM)


def block_of(array):
    dims = len(array.shape)
    return pl.BlockSpec(array.shape, lambda *_: (0,) * dims)


def call(kernel, name, outs, *args, scalars=0, cost=1, scratch=(), memory=ROOMY):
    return pl.pallas_call(
        kernel,
        grid=(1,),
        out_shape=outs,
        in_specs=[SM] * scalars + [block_of(a) for a in args[scalars:]],
        out_specs=jax.tree.map(block_of, outs),
        scratch_shapes=list(scratch),
        compiler_params=memory,
        cost_estimate=takes(cost),
        name=name,
    )(*args)


def feature_order(order_ref):
    place = lax.broadcasted_iota(jnp.int32, (1, 1024), 1)
    x, core, y, zh = place >> 8, (place >> 7) & 1, (place >> 5) & 3, (place >> 4) & 1
    feature = ((((x * 2 + zh) * 4 + y) * 2 + core) << 4) + (place & 15)
    for at in range(0, 1024, 256):
        rows = at + lax.broadcasted_iota(jnp.int32, (256, 1024), 0)
        order_ref[at : at + 256, :] = jnp.where(rows == feature, 1.0, 0.0).astype(bf16)


def core_lanes(side):
    core = lax.axis_index("c") ^ side
    return [pl.ds(pl.multiple_of(256 * x + 128 * core, 128), 128) for x in range(4)]


def of_core(ref, side):
    return jnp.concatenate([ref[:, lanes] for lanes in core_lanes(side)], axis=1)


def valid_rows(lengths_ref):
    ctx = (lax.axis_index("zh") * 4 + lax.axis_index("y")) * 2 + lax.axis_index("c")
    position = ctx * 256 + lax.broadcasted_iota(jnp.int32, (256, 1), 0)
    return jnp.where(position < lengths_ref[lax.axis_index("x")], 1.0, 0.0)


def norm_parts(values):
    center = values - jnp.mean(values, axis=-1, keepdims=True)
    inverse = lax.rsqrt(jnp.mean(center * center, axis=-1, keepdims=True) + NORM_EPS)
    return center * inverse, inverse


def norm_back(grad, gain, norm, inverse):
    scaled = grad * gain
    return inverse * (
        scaled
        - jnp.mean(scaled, axis=-1, keepdims=True)
        - norm * jnp.mean(scaled * norm, axis=-1, keepdims=True)
    )


def gelu_pair(u):
    k = 0.7978845608028654
    square = u * u
    t = jnp.tanh(u * (k + (k * 0.044715) * square))
    half = 0.5 + 0.5 * t
    value = u * half
    slope = half + (0.5 * u) * (1.0 - t * t) * (k + (3 * 0.044715 * k) * square)
    return value, slope


def prepare_kernel(qkv_ref, a_ref, b_ref, c_ref, d_ref, e_ref, g_ref, out_ref):
    rows = [r[...].astype(f32) for r in (a_ref, b_ref, c_ref, d_ref, e_ref, g_ref)]
    small = jnp.concatenate(rows + [jnp.zeros((2, 16), f32)], axis=0).T
    small = low(jnp.concatenate([small, jnp.zeros((16, 120), f32)], axis=1))

    def one(k, _):
        for c in range(3):
            out_ref[k, :, 512 * c : 512 * (c + 1)] = qkv_ref[:, c, :]
        out_ref[k, :, 1536:] = small
        return 0

    lax.fori_loop(0, 32, one, 0)


def prepare_rest_kernel(proj_ref, fc_ref, out_ref, rest_ref):
    rest_ref[:, :512] = proj_ref[...]
    rest_ref[:, 512:2560] = fc_ref[...]
    rest_ref[:, 2560:] = out_ref[...]


def pair_kernel(mine_ref, by_zh_ref, by_tp_ref, by_both_ref, out_ref):
    zh, tp = lax.axis_index("zh"), lax.axis_index("tp")
    here = pl.ds(pl.multiple_of(zh * 16, 16), 16)
    there = pl.ds(pl.multiple_of(16 - zh * 16, 16), 16)
    near = pl.ds(pl.multiple_of(tp * 512, 512), 512)
    far_off = pl.ds(pl.multiple_of(512 - tp * 512, 512), 512)
    for rows, ref, other_ref in ((here, mine_ref, by_tp_ref), (there, by_zh_ref, by_both_ref)):
        out_ref[rows, near] = ref[:, :512]
        out_ref[rows, far_off] = other_ref[...]
        out_ref[rows, 1024:] = ref[:, 512:]


def inputs_kernel(lengths_ref, tokens_ref, cotangent_ref, inputs_ref, grad_ref, order_ref):
    feature_order(order_ref)
    inputs_ref[...] = low(dot(tokens_ref[...], order_ref[...]))
    grad = dot(cotangent_ref[...], order_ref[...]) * valid_rows(lengths_ref)
    grad_ref[...] = low(grad)


def qkv_kernel(
    inputs_ref, own_ref, other_ref, bias_ref, heads_ref, own_n_ref, other_n_ref, vectors_ref, normed_ref
):
    for side, ref in ((0, own_ref), (1, other_ref)):
        small = ref[:, 1536:].astype(f32).T[:8]
        for x, lanes in enumerate(core_lanes(side)):
            vectors_ref[:, lanes] = small[:, 128 * x : 128 * (x + 1)]
    norm, _ = norm_parts(inputs_ref[...].astype(f32))
    normed_ref[...] = low(norm * vectors_ref[0:1, :] + vectors_ref[1:2, :])
    own_n_ref[...] = of_core(normed_ref, 0)
    other_n_ref[...] = of_core(normed_ref, 1)
    for c in range(3):
        cols = slice(512 * c, 512 * (c + 1))
        field = dot(own_n_ref[...], own_ref[:, cols]) + dot(other_n_ref[...], other_ref[:, cols])
        if c != 1:
            field = field + bias_ref[c // 2 : c // 2 + 1, :].astype(f32)
        field = low(field).T
        for h in range(8):
            heads_ref[h, 64 * c : 64 * (c + 1), :] = field[64 * h : 64 * (h + 1)]


def attn_end_kernel(heads_ref, weight_ref, inputs_ref, vectors_ref, middle_ref, n_ref, own_ref, wide_ref):
    tp = lax.axis_index("tp")
    for h in range(8):
        for t in range(2):
            at = 512 * t + 64 * h
            wide_ref[at : at + 64, :] = heads_ref[2 * h + t]
        own_ref[64 * h : 64 * (h + 1), :] = heads_ref[2 * h + tp]
    attn_out = contract(wide_ref[...].T, weight_ref[...], 1, 1) + vectors_ref[2:3, :]
    middle = inputs_ref[...].astype(f32) + attn_out
    middle_ref[...] = middle
    norm, _ = norm_parts(middle)
    n_ref[...] = low(norm * vectors_ref[3:4, :] + vectors_ref[4:5, :])


def attention_end(heads_all, rest, inputs, vectors):
    wide = pl.BlockSpec((256, 1024), lambda i: (0, 0))
    return pl.pallas_call(
        attn_end_kernel,
        grid=(1,),
        out_shape=(shape(256, 1024, kind=f32), shape(256, 1024), shape(512, 256)),
        in_specs=[
            pl.BlockSpec((16, 64, 256), lambda i: (0, 0, 0)),
            pl.BlockSpec((1024, 1024), lambda i: (0, 0)),
            wide,
            pl.BlockSpec((8, 1024), lambda i: (0, 0)),
        ],
        out_specs=(wide, wide, pl.BlockSpec((512, 256), lambda i: (0, 0))),
        scratch_shapes=[pltpu.VMEM((1024, 256), bf16)],
        compiler_params=ROOMY,
        cost_estimate=takes(3),
        name="attn_end",
    )(heads_all, far(rest), far(inputs), vectors)


def grad_act_kernel(gm_ref, weight_ref, out_ref):
    out_ref[...] = dot(gm_ref[...], weight_ref[...])


def grad_activated(grad_mlp, rest):
    return pl.pallas_call(
        grad_act_kernel,
        grid=(4,),
        out_shape=shape(256, 2048, kind=f32),
        in_specs=[
            pl.BlockSpec((256, 1024), lambda i: (0, 0)),
            pl.BlockSpec((1024, 512), lambda i: (0, 6 + i)),
        ],
        out_specs=pl.BlockSpec((256, 512), lambda i: (0, i)),
        compiler_params=ROOMY,
        cost_estimate=takes(3),
        name="grad_act",
    )(far(grad_mlp), far(rest))


def feed_kernel(n_ref, gact_ref, bias_ref, weight_ref, act_ref, gh_ref, part_ref, total_ref):
    i = pl.program_id(0)

    @pl.when(i == 0)
    def _():
        total_ref[...] = jnp.zeros_like(total_ref)

    halves = (slice(0, 256), slice(256, 512))
    hidden = [
        dot(n_ref[...], weight_ref[:, cols]) + bias_ref[:, cols].astype(f32) for cols in halves
    ]
    for cols, field in zip(halves, hidden):
        value, slope = gelu_pair(field)
        act_ref[:, cols] = low(value)
        gh_ref[:, cols] = low(gact_ref[:, cols] * slope)
    total_ref[...] += contract(gh_ref[...], weight_ref[...], 1, 1)

    @pl.when(i == 3)
    def _():
        part_ref[...] = low(total_ref[...])


def feed_forward(normed_two, grad_act, fc_bias, rest):
    def tile(rows, first):
        return pl.BlockSpec((rows, 512), lambda i: (0, first + i))

    wide = pl.BlockSpec((256, 1024), lambda i: (0, 0))
    return pl.pallas_call(
        feed_kernel,
        grid=(4,),
        out_shape=(shape(256, 2048), shape(256, 2048), shape(256, 1024)),
        in_specs=[wide, tile(256, 0), tile(1, 0), tile(1024, 2)],
        out_specs=(tile(256, 0), tile(256, 0), wide),
        scratch_shapes=[pltpu.VMEM((256, 1024), f32)],
        compiler_params=ROOMY,
        cost_estimate=takes(6),
        name="feed_forward",
    )(normed_two, grad_act, fc_bias, far(rest))


def wide_kernel(n_ref, gh_ref, gm_ref, act_ref, weight_ref, out_ref, part_ref, left_ref, total_ref):
    i = pl.program_id(0)

    @pl.when(i == 0)
    def _():
        left_ref[0] = n_ref[...].T
        left_ref[1] = gm_ref[...].T
        total_ref[...] = jnp.zeros_like(total_ref)

    @pl.when(i < 4)
    def _():
        out_ref[...] = low(dot(left_ref[0], gh_ref[...]))

    @pl.when(i >= 4)
    def _():
        out_ref[...] = low(dot(left_ref[1], act_ref[...]))
        total_ref[...] += contract(act_ref[...], weight_ref[...], 1, 1)

    @pl.when(i == 7)
    def _():
        part_ref[...] = low(total_ref[...])


def wide_grads(normed_two, grad_hidden, grad_mlp, activated, rest):
    whole = pl.BlockSpec((256, 1024), lambda i: (0, 0))
    return pl.pallas_call(
        wide_kernel,
        grid=(8,),
        out_shape=(shape(1024, 4096), shape(256, 1024)),
        in_specs=[
            whole,
            pl.BlockSpec((256, 512), lambda i: (0, jnp.minimum(i, 3))),
            whole,
            pl.BlockSpec((256, 512), lambda i: (0, jnp.maximum(i - 4, 0))),
            pl.BlockSpec((1024, 512), lambda i: (0, 6 + jnp.maximum(i - 4, 0))),
        ],
        out_specs=(pl.BlockSpec((1024, 512), lambda i: (0, i)), whole),
        scratch_shapes=[pltpu.VMEM((2, 1024, 256), bf16), pltpu.VMEM((256, 1024), f32)],
        compiler_params=WHOLE,
        cost_estimate=takes(8),
        name="wide_grads",
    )(normed_two, grad_hidden, far(grad_mlp), activated, far(rest))


def middle_back_kernel(
    middle_ref, mine_ref, swapped_ref, vectors_ref, gm_ref, weight_ref, out_ref, ga_ref, gheads_ref, cols_ref
):
    gm = gm_ref[...].astype(f32)
    norm, inverse = norm_parts(middle_ref[...])
    grad = mine_ref[...].astype(f32) + swapped_ref[...].astype(f32)
    out = gm + norm_back(grad, vectors_ref[3:4, :], norm, inverse)
    out_ref[...] = out
    low_out = low(out)
    ga_ref[...] = low_out
    tp = lax.axis_index("tp")
    field = low(dot(low_out, weight_ref[:, pl.ds(pl.multiple_of(tp * 512, 512), 512)])).T
    for h in range(8):
        gheads_ref[h] = field[64 * h : 64 * (h + 1)]
    rows = [low_out.astype(f32), grad * norm, grad, gm]
    rows = [jnp.sum(r, axis=0, keepdims=True) for r in rows]
    cols_ref[...] = jnp.concatenate(rows + [jnp.zeros((4, 1024), f32)], axis=0)


def middle_back(middle, mine, swapped, vectors, grad_mlp, rest):
    def whole(*dims):
        return pl.BlockSpec(dims, lambda i: (0,) * len(dims))

    wide = whole(256, 1024)
    return pl.pallas_call(
        middle_back_kernel,
        grid=(1,),
        out_shape=(
            shape(256, 1024, kind=f32),
            shape(256, 1024),
            shape(8, 64, 256),
            shape(8, 1024, kind=f32),
        ),
        in_specs=[wide, wide, wide, whole(8, 1024), wide, whole(1024, 1024)],
        out_specs=(wide, wide, whole(8, 64, 256), whole(8, 1024)),
        compiler_params=ALL,
        cost_estimate=takes(3),
        name="middle_back",
    )(far(middle), mine, swapped, vectors, far(grad_mlp), far(rest))


def put_block(ref, at, block):
    for g in range(32):
        ref[16 * g : 16 * (g + 1), at : at + 128] = block


def merge_kernel(query_ref, own_ref, other_ref, out_ref):
    out_ref[:, :64, :] = query_ref[...]
    out_ref[:, 64:, :] = low(own_ref[...] + other_ref[...].astype(f32))


def final_kernel(
    lengths_ref, inputs_ref, middle_ref, mine_ref, swapped_ref, vectors_ref, out_ref, roots_ref, order_ref
):
    feature_order(order_ref)
    valid = valid_rows(lengths_ref)
    inputs = inputs_ref[...].astype(f32)
    middle = middle_ref[...]
    mlp_out = mine_ref[...].astype(f32) + swapped_ref[...].astype(f32) + vectors_ref[5:6, :]
    final = middle + mlp_out
    out_ref[...] = low(contract(low(final), order_ref[...], 1, 1))
    lane = lax.broadcasted_iota(jnp.int32, (1, 128), 1)
    total = jnp.zeros((1, 128), f32)
    for k, field in enumerate((inputs, middle - inputs, mlp_out, final)):
        total = jnp.where(lane == k, jnp.sum(valid * field * field), total)
    roots_ref[...] = total


def side_kernel(ga_ref, heads_ref, rows_ref, mine_ref, theirs_ref):
    for side, ref in ((0, mine_ref), (1, theirs_ref)):
        ref[:, :512] = low(contract(of_core(ga_ref, side).T, heads_ref[...], 1, 1))
        cols = jnp.concatenate([of_core(rows_ref, side), jnp.zeros((120, 512), f32)], axis=0)
        ref[:, 512:] = low(cols.T)


def grads_into(ref, normed, grads_ref, sums, rows):
    left = normed.T
    for c in range(3):
        cols = slice(512 * c, 512 * (c + 1))
        ref[:, cols] = low(contract(left, grads_ref[cols, :], 1, 1))
    put_block(ref, 1536, sums[0])
    put_block(ref, 1664, sums[1])
    cols = [jnp.zeros((4, 512), f32), rows[:2], jnp.zeros((122, 512), f32)]
    ref[:, 1792:] = low(jnp.concatenate(cols, axis=0).T)


def sum_rows(field, dim, count, extra):
    sums = contract(jnp.ones((8, 256), bf16), field, 1, dim)[0:1]
    sums = [sums[:, 128 * r : 128 * (r + 1)] for r in range(count)]
    return low(jnp.concatenate(sums + extra, axis=0))


def back_kernel(
    gback_ref,
    own_ref,
    other_ref,
    inputs_ref,
    other_n_ref,
    roots_ref,
    gh_ref,
    keep_ref,
    send_ref,
    rows_ref,
    theirs_ref,
    grads_ref,
    sums_ref,
    norm_ref,
    part_ref,
):
    for c in range(3):
        for h in range(8):
            at = 512 * c + 64 * h
            grads_ref[at : at + 64, :] = gback_ref[h, 64 * c : 64 * (c + 1), :]
    sides = [grads_ref[512 * c : 512 * (c + 1), :].T for c in range(3)]
    norm_ref[...], _ = norm_parts(inputs_ref[...].astype(f32))
    parts = []
    for side, ref in ((0, own_ref), (1, other_ref)):
        part = sum(contract(sides[c], ref[:, 512 * c : 512 * (c + 1)], 1, 1) for c in range(3))
        part = low(part)
        for x, lanes in enumerate(core_lanes(side)):
            part_ref[:, lanes] = part[:, 128 * x : 128 * (x + 1)]
        part = part.astype(f32)
        gain = jnp.sum(part * of_core(norm_ref, side), axis=0, keepdims=True)
        shift = jnp.sum(part, axis=0, keepdims=True)
        parts.append(jnp.concatenate([gain, shift, jnp.zeros((6, 512), f32)], axis=0))
    rows_ref[...] = parts[0]
    tp = lax.axis_index("tp")
    keep_ref[...] = part_ref[pl.ds(pl.multiple_of(tp * 128, 128), 128), :]
    send_ref[...] = part_ref[pl.ds(pl.multiple_of(128 - tp * 128, 128), 128), :]
    extra = [roots_ref[...], jnp.zeros((3, 128), f32)]
    sums_ref[0] = sum_rows(grads_ref[...], 1, 12, extra)
    sums_ref[1] = sum_rows(gh_ref[...], 0, 16, [])
    grads_into(theirs_ref, other_n_ref[...], grads_ref, sums_ref, parts[1])


def core_add_kernel(
    grads_ref, own_n_ref, sums_ref, b_ref, p_ref, q_ref, rows_ref, out_ref, left_ref
):
    i = pl.program_id(0)

    @pl.when(i == 0)
    def _():
        left_ref[...] = own_n_ref[...].T

    rows = pl.ds(pl.multiple_of(i * 128, 128), 128)
    for c in range(3):
        cols = slice(512 * c, 512 * (c + 1))
        mine = low(contract(left_ref[rows, :], grads_ref[cols, :], 1, 1)).astype(f32)
        out_ref[:, cols] = low(mine + b_ref[:, cols].astype(f32))
    for k in range(2):
        at = 1536 + 128 * k
        for g in range(8):
            theirs = b_ref[16 * g : 16 * (g + 1), at : at + 128].astype(f32)
            out_ref[16 * g : 16 * (g + 1), at : at + 128] = low(sums_ref[k].astype(f32) + theirs)
    side = p_ref[...].astype(f32) + q_ref[...].astype(f32)
    out_ref[:, 1792:2304] = low(side[:, :512])
    ln1 = jnp.concatenate([jnp.zeros((4, 128), f32), rows_ref[:2], jnp.zeros((122, 128), f32)], axis=0)
    both = low(ln1.T).astype(f32) + b_ref[:, 1792:].astype(f32)
    out_ref[:, 2304:] = low(side[:, 512:] + both)


def core_add(grads, own_n, sums, theirs, mine_p, theirs_p, rows):
    def tall(cols):
        return pl.BlockSpec((128, cols), lambda i: (i, 0))

    flat = pl.BlockSpec((8, 128), lambda i: (0, i))
    return pl.pallas_call(
        core_add_kernel,
        grid=(4,),
        out_shape=shape(512, 2432),
        in_specs=[
            block_of(grads),
            block_of(own_n),
            block_of(sums),
            tall(1920),
            tall(640),
            tall(640),
            flat,
        ],
        out_specs=tall(2432),
        scratch_shapes=[pltpu.VMEM((512, 256), bf16)],
        compiler_params=ROOMY,
        cost_estimate=takes(4),
        name="qkv_core_sum",
    )(grads, far(own_n), sums, theirs, far(mine_p), theirs_p, rows)


def end_kernel(inputs_ref, gmid_ref, mine_ref, swapped_ref, vectors_ref, out_ref, order_ref):
    feature_order(order_ref)
    rows = pl.ds(pl.multiple_of(lax.axis_index("tp") * 128, 128), 128)
    norm, inverse = norm_parts(inputs_ref[rows, :].astype(f32))
    grad = mine_ref[...].astype(f32) + swapped_ref[...].astype(f32)
    grad = gmid_ref[rows, :] + norm_back(grad, vectors_ref[0:1, :], norm, inverse)
    out_ref[...] = low(contract(low(grad), order_ref[...], 1, 1))


def join_kernel(mine_ref, theirs_ref, out_ref):
    tp = lax.axis_index("tp")
    out_ref[pl.ds(pl.multiple_of(tp * 128, 128), 128), :] = mine_ref[...]
    out_ref[pl.ds(pl.multiple_of(128 - tp * 128, 128), 128), :] = theirs_ref[...]


def total_qkv_kernel(lengths_ref, got_ref, qkv_ref, proj_ref, bias_ref, fc_ref, roots_ref):
    total = got_ref[0].astype(f32)
    for k in range(1, 32):
        total = total + got_ref[k].astype(f32)
    for c in range(3):
        qkv_ref[:, c, :] = total[:, 512 * c : 512 * (c + 1)]
    for k in range(2):
        for r in range(4):
            row = 8 * k + r
            bias_ref[k : k + 1, 128 * r : 128 * (r + 1)] = total[row : row + 1, 1536:1664]
    count = lengths_ref[0] + lengths_ref[1] + lengths_ref[2] + lengths_ref[3]
    mean = total[12:13, 1536:1664] / (count.astype(f32) * 1024.0)
    roots_ref[...] = jnp.sqrt(mean + ROOT_EPS)
    fc_ref[...] = total[:, 1664:1792]
    proj_ref[...] = total[:, 1792:2304]


def total_cols_kernel(got_ref, cols_ref):
    total = got_ref[0].astype(f32)
    for k in range(1, 32):
        total = total + got_ref[k].astype(f32)
    cols_ref[...] = total.T[:8]


def total_cols(got):
    return pl.pallas_call(
        total_cols_kernel,
        grid=(1,),
        out_shape=shape(8, 16, kind=f32),
        in_specs=[pl.BlockSpec((32, 16, 128), lambda i: (0, 0, 18))],
        out_specs=pl.BlockSpec((8, 16), lambda i: (0, 0)),
        compiler_params=ROOMY,
        cost_estimate=takes(1),
        name="total_cols",
    )(got)


def total_wide_kernel(mine_ref, theirs_ref, fc_ref, out_ref):
    total = mine_ref[...].astype(f32) + theirs_ref[...].astype(f32)
    fc_ref[...] = total[:, :2048]
    out_ref[...] = total[:, 2048:]


def body(
    tokens,
    ln1_gain,
    ln1_bias,
    qkv_weight,
    qv_bias,
    proj_weight,
    proj_bias,
    ln2_gain,
    ln2_bias,
    fc_weight,
    fc_bias,
    out_weight,
    out_bias,
    piece_starts,
    seq_lengths,
    cotangent,
):
    vectors = (ln1_gain, ln1_bias, proj_bias, ln2_gain, ln2_bias, out_bias)
    pay_q = call(
        prepare_kernel,
        "weights_payload",
        shape(32, 16, 1664),
        qkv_weight,
        *[v.reshape(1, 16) for v in vectors],
    )
    own_q = exchange(pay_q, SPREAD).reshape(512, 1664)
    proj_rows = proj_weight.T
    pay_r = call(
        prepare_rest_kernel, "rest_payload", shape(16, 4608), proj_rows, fc_weight, out_weight.T
    )
    pair_r = call(
        pair_kernel,
        "rest_pair",
        shape(32, 5120),
        after(pay_r, pay_q),
        swap(pay_r, "zh"),
        swap(proj_rows, "tp"),
        lax.ppermute(proj_rows, ("zh", "tp"), [(i, 3 - i) for i in range(4)]),
    )
    rest = lax.all_gather(pair_r, ("x", "c", "y"), axis=0, tiled=True)

    inputs, grad_mlp = call(
        inputs_kernel,
        "inputs",
        (shape(256, 1024), shape(256, 1024)),
        seq_lengths,
        tokens[0],
        cotangent[0],
        scalars=1,
        cost=300,
        scratch=[pltpu.VMEM((1024, 1024), bf16)],
    )
    own_q = after(own_q, inputs)
    other_q = swap(own_q, "c")
    heads, own_n, other_n, vectors = call(
        qkv_kernel,
        "qkv",
        (shape(8, 192, 256), shape(256, 512), shape(256, 512), shape(8, 1024, kind=f32)),
        inputs,
        own_q,
        other_q,
        qv_bias,
        scratch=[pltpu.VMEM((256, 1024), bf16)],
        cost=3,
    )
    own = exchange(heads, LINE)
    other = swap(own[:, 64:], "c")
    attended, attended_low, log_sum = attn_forward(seq_lengths, piece_starts, own, other)
    heads_all = exchange(attended_low.reshape(16, 64, 256), ("zh", "y", "tp"))
    staged = attn_stage(own, other, log_sum)
    grad_act = grad_activated(grad_mlp, after(rest, attended_low))
    middle, normed_two, heads_out = attention_end(
        after(heads_all, staged[0], grad_act), rest, inputs, vectors
    )
    activated, grad_hidden, two_part = feed_forward(
        normed_two, grad_act, fc_bias.reshape(1, 2048), rest
    )
    two_swapped = swap(two_part, "tp")
    wide, mlp_part = wide_grads(normed_two, grad_hidden, grad_mlp, activated, rest)
    wide = lax.psum_scatter(
        after(wide, two_swapped), ("x", "c"), scatter_dimension=0, tiled=True
    )
    two_swapped = after(two_swapped, mlp_part)
    grad_middle, grad_attn, grad_heads, rows = middle_back(
        middle, two_part, two_swapped, vectors, grad_mlp, rest
    )
    grad_mine = exchange(grad_heads, LINE)

    mine_p, theirs_p = call(
        side_kernel,
        "proj_grads",
        (shape(512, 640), shape(512, 640)),
        far(grad_attn),
        far(heads_out),
        rows,
        cost=2,
    )
    grad_mine = after(grad_mine, mine_p)
    theirs_p = swap(after(theirs_p, grad_mine), "c")
    mlp_swapped = swap(after(mlp_part, grad_mine), "tp")

    grad_query, grad_own, grad_other = attn_backward(
        seq_lengths, piece_starts, staged, grad_mine, attended
    )
    grad_other, mlp_swapped = lax.optimization_barrier((grad_other, mlp_swapped))
    grad_back = call(
        merge_kernel, "merge", shape(8, 192, 256), grad_query, grad_own, swap(grad_other, "c")
    )
    grad_back = exchange(grad_back, LINE)
    layer_out, roots = call(
        final_kernel,
        "final",
        (shape(256, 1024), shape(1, 128, kind=f32)),
        seq_lengths,
        far(inputs),
        far(middle),
        after(mlp_part, grad_other),
        mlp_swapped,
        vectors,
        scalars=1,
        cost=3,
        scratch=[pltpu.VMEM((1024, 1024), bf16)],
    )
    one_keep, one_send, rows, theirs_q, grads, sums = call(
        back_kernel,
        "back",
        (
            shape(128, 1024),
            shape(128, 1024),
            shape(8, 512, kind=f32),
            shape(512, 1920),
            shape(1536, 256),
            shape(2, 16, 128),
        ),
        grad_back,
        far(own_q),
        far(other_q),
        far(inputs),
        far(other_n),
        roots,
        far(grad_hidden),
        cost=5,
        scratch=[pltpu.VMEM((256, 1024), f32), pltpu.VMEM((256, 1024), bf16)],
        memory=ALL,
    )
    one_swapped = swap(one_send, "tp")
    wide = lax.psum_scatter(after(wide, roots), "y", scatter_dimension=0, tiled=True)
    both = core_add(
        grads,
        own_n,
        sums,
        after(swap(theirs_q, "c"), one_swapped),
        mine_p,
        theirs_p,
        rows,
    )
    got_q = exchange(both.reshape(32, 16, 2432), SPREAD)
    half_tokens = call(
        end_kernel,
        "end",
        shape(128, 1024),
        far(inputs),
        far(grad_middle),
        one_keep,
        one_swapped,
        vectors,
        cost=2,
        scratch=[pltpu.VMEM((1024, 1024), bf16)],
    )
    grad_tokens = call(
        join_kernel, "join", shape(256, 1024), half_tokens, swap(half_tokens, "tp")
    )
    zh = lax.axis_index("zh")
    keep = lax.dynamic_slice_in_dim(wide, zh * 16, 16, 0)
    send = lax.dynamic_slice_in_dim(wide, 16 - zh * 16, 16, 0)
    grad_fc, grad_out = call(
        total_wide_kernel,
        "total_wide",
        (shape(16, 2048, kind=f32), shape(16, 2048, kind=f32)),
        keep,
        swap(send, "zh"),        cost=14,
    )
    got_q = after(got_q, grad_fc, grad_tokens)
    cols = total_cols(got_q)
    ln1 = cols[4:6]
    grad_qkv, grad_proj, bias_sums, fc_sums, roots = call(
        total_qkv_kernel,
        "total_qkv",
        (
            shape(16, 3, 512, kind=f32),
            shape(16, 512, kind=f32),
            shape(2, 512, kind=f32),
            shape(16, 128, kind=f32),
            shape(1, 128, kind=f32),
        ),
        seq_lengths,
        after(got_q, cols),
        scalars=1,
    )
    ln1 = ln1 + swap(ln1, "tp")
    return (
        layer_out[None],
        grad_tokens[None],
        ln1[0],
        ln1[1],
        grad_qkv,
        bias_sums,
        grad_proj.T,
        cols[0],
        cols[1],
        cols[2],
        grad_fc,
        fc_sums.reshape(2048),
        grad_out.T,
        cols[3],
        roots[0, :4],
    )


def solution(mesh):
    fine = Mesh(mesh.devices.reshape(4, 2, 4, 2, 2), ("x", "zh", "y", "c", "tp"))
    ctx = ("zh", "y", "c")
    every = ("x", "zh", "y", "c")
    in_specs = (
        P("x", ctx, None),
        P(every),
        P(every),
        P(every, None, "tp"),
        P(None, "tp"),
        P("tp", every),
        P(every),
        P(every),
        P(every),
        P(every, "tp"),
        P("tp"),
        P("tp", every),
        P(every),
        P("x", None),
        P(),
        P("x", ctx, None),
    )
    out_specs = (
        P("x", ctx, None),
        P("x", ctx, None),
        P(every),
        P(every),
        P(every, None, "tp"),
        P(None, "tp"),
        P("tp", every),
        P(every),
        P(every),
        P(every),
        P(every, "tp"),
        P("tp"),
        P("tp", every),
        P(every),
        P(),
    )
    return jax.shard_map(body, mesh=fine, in_specs=in_specs, out_specs=out_specs, check_vma=False)
```

```python
from functools import partial

import jax
import jax.numpy as jnp
from jax import lax
from jax.experimental import pallas as pl
from jax.experimental.pallas import tpu as pltpu
from jax.sharding import Mesh
from jax.sharding import PartitionSpec as P

f32 = jnp.float32
bf16 = jnp.bfloat16
NORM_EPS = 1e-05
ROOT_EPS = 1e-06
B=256; E=64; NB=16; MASKED=-1e30; PIECE=256

class Facts:
    def __init__(self, lengths_ref, starts_ref):
        self.core = lax.axis_index("c")
        self.items = (self.core, lengths_ref[lax.axis_index("x")], starts_ref[0, 0], starts_ref[0, 1])

    def __getitem__(self, at):
        return self.items[at]


def piece_of(pos, info_ref):
    n0=(pos>=info_ref[2])&(pos<info_ref[2]+PIECE)
    n1=(pos>=info_ref[3])&(pos<info_ref[3]+PIECE)
    return jnp.where(n0,1,0)+jnp.where(n1,2,0)

def allowed_block(key_block, query_block, info_ref):
    kpos=key_block*B+lax.broadcasted_iota(jnp.int32,(B,1),0)
    qpos=query_block*B+lax.broadcasted_iota(jnp.int32,(1,B),1)
    kp=piece_of(kpos,info_ref); qp=piece_of(qpos,info_ref)
    qp=jnp.where(qp==0,-1,qp)
    kp=jnp.where(kpos<info_ref[1],kp,-2)
    kpos=jnp.where(kpos<info_ref[1],kpos,1<<20)
    return (kpos<=qpos)|(kp==qp)

def extra_blocks(p, info_ref):
    edge=(2*p+2)*B
    crosses=((info_ref[2]<edge)&(edge<info_ref[2]+PIECE))|((info_ref[3]<edge)&(edge<info_ref[3]+PIECE))
    return jnp.where((info_ref[0]==1)&(p<NB//2-1)&crosses,1,0)

def dot(a,b): return jnp.dot(a,b,preferred_element_type=f32)

SAFE = 60.0


def split3(row):
    top = row.astype(bf16).astype(f32)
    mid = (row - top).astype(bf16).astype(f32)
    rows = jnp.concatenate([top, mid, row - top - mid, jnp.zeros((13, row.shape[1]), f32)], axis=0)
    return rows.astype(bf16)


def ones_beside(block):
    lane = lax.broadcasted_iota(jnp.int32, (B, 16), 1)
    return jnp.concatenate([block, jnp.where(lane < 3, 1.0, 0.0).astype(bf16)], axis=1)


CHUNK = 4 * B


def pair_allowed(m, info_ref):
    key = m * CHUNK + lax.broadcasted_iota(jnp.int32, (CHUNK, 1), 0)
    lane = lax.broadcasted_iota(jnp.int32, (1, 2 * B), 1)
    query = (4 * m + info_ref[0]) * B + lane + jnp.where(lane >= B, B, 0)
    key_piece, query_piece = piece_of(key, info_ref), piece_of(query, info_ref)
    query_piece = jnp.where(query_piece == 0, -1, query_piece)
    valid = key < info_ref[1]
    key_piece = jnp.where(valid, key_piece, -2)
    key = jnp.where(valid, key, 1 << 20)
    return (key <= query) | (key_piece == query_piece)


def pair_of(ref, m):
    return jnp.concatenate([ref[2 * m], ref[2 * m + 1]], axis=1)


def walk(m, extra, step, beyond, carry):
    def chunk(i, c):
        return step(pl.multiple_of(i * CHUNK, CHUNK), None, c)

    carry = lax.fori_loop(0, m, chunk, carry)
    first = pl.multiple_of(m * CHUNK, CHUNK)
    carry = step(first, m, carry)
    second = lax.fori_loop(
        0, extra, lambda i, c: beyond(pl.multiple_of(first + CHUNK, B), c), carry[:, B:]
    )
    return carry[:, :B], second


def masked_from(e, first, count, masked, query_block, info_ref):
    if not masked:
        return e
    keep = count - masked * B
    parts = [e[:keep]] if keep else []
    for at in range(keep, count, B):
        allowed = allowed_block((first >> 8) + at // B, query_block, info_ref)
        parts.append(jnp.where(allowed, e[at : at + B], 0.0))
    return jnp.concatenate(parts, axis=0)


def place(block):
    return pl.ds(pl.multiple_of(block * B, B), B)


def walk_all(p, extra, step, carry, chunk):
    end = 2 * B * (p + 1)
    for first in range(0, end, chunk):
        last = min(first + chunk, end)
        carry = step(first, last - first, max(0, last - (end - 2 * B)) // B, carry)
    if p == NB // 2 - 1:
        return carry
    return lax.fori_loop(0, extra, lambda i, c: step(end, B, 1, c), carry)


def forward_kernel(lengths_ref, starts_ref, own_ref, other_ref, out_ref, low_ref, lse_ref, key_ref, value_ref):
    info_ref = Facts(lengths_ref, starts_ref)
    core = info_ref[0]
    sublane = lax.broadcasted_iota(jnp.int32, (16, NB * B), 0)
    value_ref[E:, :] = jnp.where(sublane == 0, 1.0, 0.0).astype(bf16)

    def squares(block):
        field = block.astype(f32)
        return jnp.sum(field * field, axis=0, keepdims=True)

    query_top = jnp.zeros((1, B), f32)
    key_top = jnp.zeros((1, B), f32)
    for p in range(NB // 2):
        mine, theirs = own_ref[p, E : 2 * E, :], other_ref[p, :E, :]
        here, there = place(2 * p + core), place(2 * p + 1 - core)
        key_ref[here, :] = mine.T
        key_ref[there, :] = theirs.T
        value_ref[:E, here] = own_ref[p, 2 * E :, :]
        value_ref[:E, there] = other_ref[p, E:, :]
        query_top = jnp.maximum(query_top, squares(own_ref[p, :E, :]))
        key_top = jnp.maximum(key_top, jnp.maximum(squares(mine), squares(theirs)))
    bound = jnp.max(query_top) * jnp.max(key_top)

    def finish(p, top, acc):
        total = acc[E : E + 1]
        o = acc[:E] / total
        out_ref[p] = o
        low_ref[p, 0] = o.astype(bf16)
        low_ref[p, 1] = o.astype(bf16)
        lse_ref[p] = top + jnp.log(total)

    @pl.when(bound <= (8.0 * SAFE) ** 2)
    def _():
        def both(m, _):
            query = pair_of(own_ref.at[:, :E, :], m) * jnp.asarray(0.125, bf16)

            def step(first, masked, acc):
                at = pl.ds(first, CHUNK)
                e = jnp.exp(dot(key_ref[at, :], query))
                if masked is not None:
                    e = jnp.where(pair_allowed(masked, info_ref), e, 0.0)
                return acc + dot(value_ref[:, at], e.astype(bf16))

            def beyond(first, acc):
                at = pl.ds(first, B)
                e = jnp.exp(dot(key_ref[at, :], query[:, B:]))
                e = jnp.where(allowed_block(4 * m + 4, 4 * m + 2 + core, info_ref), e, 0.0)
                return acc + dot(value_ref[:, at], e.astype(bf16))

            accs = walk(
                m, extra_blocks(2 * m + 1, info_ref), step, beyond, jnp.zeros((E + 16, 2 * B), f32)
            )
            for odd in range(2):
                finish(2 * m + odd, 0.0, accs[odd])
            return 0

        lax.fori_loop(0, NB // 4, both, 0)

    @pl.when(bound > (8.0 * SAFE) ** 2)
    def _():
        def one(p, _):
            query = own_ref[p, :E, :] * jnp.asarray(0.125, bf16)
            qb = 2 * p + core

            def step(blocks, masked, carry):
                top, acc = carry
                scores = [dot(key_ref[place(j), :], query) for j in blocks]
                if masked:
                    scores = [
                        jnp.where(allowed_block(j, qb, info_ref), s, MASKED)
                        for j, s in zip(blocks, scores)
                    ]
                new = top
                for s in scores:
                    new = jnp.maximum(new, jnp.max(s, axis=0, keepdims=True))
                acc = acc * jnp.exp(top - new)
                for j, s in zip(blocks, scores):
                    acc = acc + dot(value_ref[:, place(j)], jnp.exp(s - new).astype(bf16))
                return new, acc

            carry = (jnp.full((1, B), MASKED, f32), jnp.zeros((E + 16, B), f32))
            carry = step((2 * p, 2 * p + 1), True, carry)
            carry = lax.fori_loop(0, p, lambda i, c: step((2 * i, 2 * i + 1), False, c), carry)
            carry = lax.fori_loop(
                0, extra_blocks(p, info_ref), lambda i, c: step((2 * p + 2,), True, c), carry
            )
            finish(p, *carry)
            return 0

        lax.fori_loop(0, NB // 2, one, 0)


def stage_kernel(own_ref, other_ref, lse_ref, key_ref, keyt_ref, value_ref, query_ref, rows_ref):
    core = lax.axis_index("c")
    blank = jnp.zeros((B, E), bf16)
    for p in range(NB // 2):
        mine, theirs = own_ref[p, E : 2 * E, :], other_ref[p, :E, :]
        here, there = place(2 * p + core), place(2 * p + 1 - core)
        keyt_ref[:, here] = mine
        keyt_ref[:, there] = theirs
        key_ref[here, :] = ones_beside(mine.T)
        key_ref[there, :] = ones_beside(theirs.T)
        value_ref[here, :] = ones_beside(own_ref[p, 2 * E :, :].T)
        value_ref[there, :] = ones_beside(other_ref[p, E:, :].T)
        query = own_ref[p, :E, :] * jnp.asarray(0.125, bf16)
        query_ref[p, :E, :] = query
        query_ref[p, E:, :] = split3(-lse_ref[p])
        rows_ref[p] = jnp.concatenate([blank, query.T], axis=1)


def backward_kernel(
    lengths_ref,
    starts_ref,
    key_ref,
    keyt_ref,
    value_ref,
    query_ref,
    rows_ref,
    gout_ref,
    out_ref,
    gq_ref,
    gown_ref,
    gother_ref,
    grad_ref,
    gouts_ref,
    grows_ref,
    sum_ref,
):
    info_ref = Facts(lengths_ref, starts_ref)
    core = info_ref[0]
    grad_ref[...] = jnp.zeros_like(grad_ref)
    blank = jnp.zeros((B, E), bf16)
    for p in range(NB // 2):
        gout = gout_ref[p]
        delta = jnp.sum(gout.astype(f32) * out_ref[p], axis=0, keepdims=True)
        gouts_ref[p, :E, :] = gout
        gouts_ref[p, E:, :] = split3(-delta)
        grows_ref[p] = jnp.concatenate([gout.T, blank], axis=1)
    sum_ref[...] = jnp.zeros_like(sum_ref)

    def chunk(p, first, count, masked):
        at = pl.ds(pl.multiple_of(first, B), count)
        e = jnp.exp(dot(key_ref[at, :], query_ref[p]))
        if masked:
            e = masked_from(e, first, count, masked, 2 * p + core, info_ref)
        gs = (e * dot(value_ref[at, :], gouts_ref[p])).astype(bf16)
        grad_ref[at, :] += dot(e.astype(bf16), grows_ref[p]) + dot(gs, rows_ref[p])
        sum_ref[p] += dot(keyt_ref[:, at], gs)

    def both(m, _):
        top = NB // 2 - 1 - m
        for k in range(NB // 2 - 1):
            late = k < top
            chunk(jnp.where(late, top, m), 2 * B * jnp.where(late, k, k - top), 2 * B, 0)
        chunk(top, 2 * B * top, 2 * B, 2)
        chunk(m, 2 * B * m, 2 * B, 2)
        return 0

    lax.fori_loop(0, NB // 4, both, 0)

    def beyond(p, _):
        def add(i, _):
            chunk(p, 2 * B * (p + 1), B, 1)
            return 0

        return lax.fori_loop(0, extra_blocks(p, info_ref), add, 0)

    lax.fori_loop(0, NB // 2 - 1, beyond, 0)
    for p in range(NB // 2):
        gq_ref[p] = (sum_ref[p] * 0.125).astype(bf16)
    for p in range(NB // 2):
        mine = grad_ref[place(2 * p + core), :].T
        theirs = grad_ref[place(2 * p + 1 - core), :].T.astype(bf16)
        gown_ref[p, :E, :] = mine[E:]
        gown_ref[p, E:, :] = mine[:E]
        gother_ref[p, :E, :] = theirs[E:]
        gother_ref[p, E:, :] = theirs[:E]


VM=pl.BlockSpec(memory_space=pltpu.VMEM); SM=pl.BlockSpec(memory_space=pltpu.SMEM)
LIMIT=40*1024*1024
def attn_forward(lengths,starts,own,other):
    H=NB//2
    return pl.pallas_call(forward_kernel,
        out_shape=(jax.ShapeDtypeStruct((H,E,B),f32),jax.ShapeDtypeStruct((H,2,E,B),bf16),jax.ShapeDtypeStruct((H,1,B),f32)),
        in_specs=[SM,SM,VM,VM],out_specs=(VM,VM,VM),
        scratch_shapes=[pltpu.VMEM((NB*B,E),bf16),pltpu.VMEM((E+16,NB*B),bf16)],
        compiler_params=pltpu.CompilerParams(vmem_limit_bytes=LIMIT),
        cost_estimate=takes(8),
        name="attention_forward")(lengths,starts,own,other)
def attn_stage(own, other, lse):
    half = NB // 2
    outs = (
        jax.ShapeDtypeStruct((NB * B, E + 16), bf16),
        jax.ShapeDtypeStruct((E, NB * B), bf16),
        jax.ShapeDtypeStruct((NB * B, E + 16), bf16),
        jax.ShapeDtypeStruct((half, E + 16, B), bf16),
        jax.ShapeDtypeStruct((half, B, 2 * E), bf16),
    )
    return pl.pallas_call(
        stage_kernel,
        out_shape=outs,
        in_specs=[VM] * 3,
        out_specs=(VM,) * 5,
        compiler_params=pltpu.CompilerParams(vmem_limit_bytes=LIMIT),
        cost_estimate=takes(1),
        name="attention_stage",
    )(own, other, lse)


def attn_backward(lengths, starts, staged, gout, out):
    half = NB // 2

    def full(array):
        return pl.BlockSpec(array.shape, lambda i: (0,) * len(array.shape))

    outs = (
        jax.ShapeDtypeStruct((half, E, B), bf16),
        jax.ShapeDtypeStruct((half, 2 * E, B), f32),
        jax.ShapeDtypeStruct((half, 2 * E, B), bf16),
    )
    return pl.pallas_call(
        backward_kernel,
        grid=(1,),
        out_shape=outs,
        in_specs=[SM, SM] + [full(x) for x in (*staged, gout, out)],
        out_specs=tuple(full(x) for x in outs),
        scratch_shapes=[
            pltpu.VMEM((NB * B, 2 * E), f32),
            pltpu.VMEM((half, E + 16, B), bf16),
            pltpu.VMEM((half, B, 2 * E), bf16),
            pltpu.VMEM((half, E, B), f32),
        ],
        compiler_params=pltpu.CompilerParams(vmem_limit_bytes=LIMIT),
        cost_estimate=takes(26),
        name="attention_backward",
    )(lengths, starts, *[far(x) for x in staged], gout, far(out))


SPREAD = ("x", "y", "zh")
LINE = ("zh", "y")
VM = pl.BlockSpec(memory_space=pltpu.VMEM)
SM = pl.BlockSpec(memory_space=pltpu.SMEM)
ANY = pl.BlockSpec(memory_space=pl.ANY)
ROOMY = pltpu.CompilerParams(vmem_limit_bytes=40 * 1024 * 1024)
WHOLE = pltpu.CompilerParams(vmem_limit_bytes=50 * 1024 * 1024)
ALL = pltpu.CompilerParams(vmem_limit_bytes=62 * 1024 * 1024)


def takes(microseconds):
    return pl.CostEstimate(
        flops=int(microseconds * 1.15e9), bytes_accessed=1 << 20, transcendentals=0
    )


def low(field):
    return field.astype(bf16)


def swap(field, axis):
    return lax.ppermute(field, axis, [(0, 1), (1, 0)])


def exchange(field, axes):
    return lax.all_to_all(field, axes, split_axis=0, concat_axis=0, tiled=True)


def after(field, *others):
    return lax.optimization_barrier((field, *others))[0]


def contract(a, b, dim_a, dim_b):
    return lax.dot_general(a, b, (((dim_a,), (dim_b,)), ((), ())), preferred_element_type=f32)


def shape(*dims, kind=bf16):
    return jax.ShapeDtypeStruct(dims, kind)


def far(field):
    return pltpu.with_memory_space_constraint(field, pltpu.HBM)


def block_of(array):
    dims = len(array.shape)
    return pl.BlockSpec(array.shape, lambda *_: (0,) * dims)


def call(kernel, name, outs, *args, scalars=0, cost=1, scratch=(), memory=ROOMY):
    return pl.pallas_call(
        kernel,
        grid=(1,),
        out_shape=outs,
        in_specs=[SM] * scalars + [block_of(a) for a in args[scalars:]],
        out_specs=jax.tree.map(block_of, outs),
        scratch_shapes=list(scratch),
        compiler_params=memory,
        cost_estimate=takes(cost),
        name=name,
    )(*args)


def feature_order(order_ref):
    place = lax.broadcasted_iota(jnp.int32, (1, 1024), 1)
    x, core, y, zh = place >> 8, (place >> 7) & 1, (place >> 5) & 3, (place >> 4) & 1
    feature = ((((x * 2 + zh) * 4 + y) * 2 + core) << 4) + (place & 15)
    for at in range(0, 1024, 256):
        rows = at + lax.broadcasted_iota(jnp.int32, (256, 1024), 0)
        order_ref[at : at + 256, :] = jnp.where(rows == feature, 1.0, 0.0).astype(bf16)


def core_lanes(side):
    core = lax.axis_index("c") ^ side
    return [pl.ds(pl.multiple_of(256 * x + 128 * core, 128), 128) for x in range(4)]


def of_core(ref, side):
    return jnp.concatenate([ref[:, lanes] for lanes in core_lanes(side)], axis=1)


def valid_rows(lengths_ref):
    ctx = (lax.axis_index("zh") * 4 + lax.axis_index("y")) * 2 + lax.axis_index("c")
    position = ctx * 256 + lax.broadcasted_iota(jnp.int32, (256, 1), 0)
    return jnp.where(position < lengths_ref[lax.axis_index("x")], 1.0, 0.0)


def norm_parts(values):
    center = values - jnp.mean(values, axis=-1, keepdims=True)
    inverse = lax.rsqrt(jnp.mean(center * center, axis=-1, keepdims=True) + NORM_EPS)
    return center * inverse, inverse


def norm_back(grad, gain, norm, inverse):
    scaled = grad * gain
    return inverse * (
        scaled
        - jnp.mean(scaled, axis=-1, keepdims=True)
        - norm * jnp.mean(scaled * norm, axis=-1, keepdims=True)
    )


def gelu_pair(u):
    k = 0.7978845608028654
    square = u * u
    t = jnp.tanh(u * (k + (k * 0.044715) * square))
    half = 0.5 + 0.5 * t
    value = u * half
    slope = half + (0.5 * u) * (1.0 - t * t) * (k + (3 * 0.044715 * k) * square)
    return value, slope


def prepare_kernel(qkv_ref, a_ref, b_ref, c_ref, d_ref, e_ref, g_ref, out_ref):
    rows = [r[...].astype(f32) for r in (a_ref, b_ref, c_ref, d_ref, e_ref, g_ref)]
    small = jnp.concatenate(rows + [jnp.zeros((2, 16), f32)], axis=0).T
    small = low(jnp.concatenate([small, jnp.zeros((16, 120), f32)], axis=1))

    def one(k, _):
        for c in range(3):
            out_ref[k, :, 512 * c : 512 * (c + 1)] = qkv_ref[:, c, :]
        out_ref[k, :, 1536:] = small
        return 0

    lax.fori_loop(0, 32, one, 0)


def prepare_rest_kernel(proj_ref, fc_ref, out_ref, rest_ref):
    rest_ref[:, :512] = proj_ref[...]
    rest_ref[:, 512:2560] = fc_ref[...]
    rest_ref[:, 2560:] = out_ref[...]


def pair_kernel(mine_ref, by_zh_ref, by_tp_ref, by_both_ref, out_ref):
    zh, tp = lax.axis_index("zh"), lax.axis_index("tp")
    here = pl.ds(pl.multiple_of(zh * 16, 16), 16)
    there = pl.ds(pl.multiple_of(16 - zh * 16, 16), 16)
    near = pl.ds(pl.multiple_of(tp * 512, 512), 512)
    far_off = pl.ds(pl.multiple_of(512 - tp * 512, 512), 512)
    for rows, ref, other_ref in ((here, mine_ref, by_tp_ref), (there, by_zh_ref, by_both_ref)):
        out_ref[rows, near] = ref[:, :512]
        out_ref[rows, far_off] = other_ref[...]
        out_ref[rows, 1024:] = ref[:, 512:]


def inputs_kernel(lengths_ref, tokens_ref, cotangent_ref, inputs_ref, grad_ref, order_ref):
    feature_order(order_ref)
    inputs_ref[...] = low(dot(tokens_ref[...], order_ref[...]))
    grad = dot(cotangent_ref[...], order_ref[...]) * valid_rows(lengths_ref)
    grad_ref[...] = low(grad)


def qkv_kernel(
    inputs_ref, own_ref, other_ref, bias_ref, heads_ref, own_n_ref, other_n_ref, vectors_ref, normed_ref
):
    for side, ref in ((0, own_ref), (1, other_ref)):
        small = ref[:, 1536:].astype(f32).T[:8]
        for x, lanes in enumerate(core_lanes(side)):
            vectors_ref[:, lanes] = small[:, 128 * x : 128 * (x + 1)]
    norm, _ = norm_parts(inputs_ref[...].astype(f32))
    normed_ref[...] = low(norm * vectors_ref[0:1, :] + vectors_ref[1:2, :])
    own_n_ref[...] = of_core(normed_ref, 0)
    other_n_ref[...] = of_core(normed_ref, 1)
    for c in range(3):
        cols = slice(512 * c, 512 * (c + 1))
        field = dot(own_n_ref[...], own_ref[:, cols]) + dot(other_n_ref[...], other_ref[:, cols])
        if c != 1:
            field = field + bias_ref[c // 2 : c // 2 + 1, :].astype(f32)
        field = low(field).T
        for h in range(8):
            heads_ref[h, 64 * c : 64 * (c + 1), :] = field[64 * h : 64 * (h + 1)]


def attn_end_kernel(heads_ref, weight_ref, inputs_ref, vectors_ref, middle_ref, n_ref, own_ref, wide_ref):
    tp = lax.axis_index("tp")
    for h in range(8):
        for t in range(2):
            at = 512 * t + 64 * h
            wide_ref[at : at + 64, :] = heads_ref[2 * h + t]
        own_ref[64 * h : 64 * (h + 1), :] = heads_ref[2 * h + tp]
    attn_out = contract(wide_ref[...].T, weight_ref[...], 1, 1) + vectors_ref[2:3, :]
    middle = inputs_ref[...].astype(f32) + attn_out
    middle_ref[...] = middle
    norm, _ = norm_parts(middle)
    n_ref[...] = low(norm * vectors_ref[3:4, :] + vectors_ref[4:5, :])


def attention_end(heads_all, rest, inputs, vectors):
    wide = pl.BlockSpec((256, 1024), lambda i: (0, 0))
    return pl.pallas_call(
        attn_end_kernel,
        grid=(1,),
        out_shape=(shape(256, 1024, kind=f32), shape(256, 1024), shape(512, 256)),
        in_specs=[
            pl.BlockSpec((16, 64, 256), lambda i: (0, 0, 0)),
            pl.BlockSpec((1024, 1024), lambda i: (0, 0)),
            wide,
            pl.BlockSpec((8, 1024), lambda i: (0, 0)),
        ],
        out_specs=(wide, wide, pl.BlockSpec((512, 256), lambda i: (0, 0))),
        scratch_shapes=[pltpu.VMEM((1024, 256), bf16)],
        compiler_params=ROOMY,
        cost_estimate=takes(3),
        name="attn_end",
    )(heads_all, far(rest), far(inputs), far(vectors))


def grad_act_kernel(gm_ref, weight_ref, out_ref):
    out_ref[...] = dot(gm_ref[...], weight_ref[...])


def grad_activated(grad_mlp, rest):
    return pl.pallas_call(
        grad_act_kernel,
        grid=(4,),
        out_shape=shape(256, 2048, kind=f32),
        in_specs=[
            pl.BlockSpec((256, 1024), lambda i: (0, 0)),
            pl.BlockSpec((1024, 512), lambda i: (0, 6 + i)),
        ],
        out_specs=pl.BlockSpec((256, 512), lambda i: (0, i)),
        compiler_params=ROOMY,
        cost_estimate=takes(3),
        name="grad_act",
    )(far(grad_mlp), far(rest))


def feed_kernel(n_ref, gact_ref, bias_ref, weight_ref, act_ref, gh_ref, part_ref, total_ref):
    i = pl.program_id(0)

    @pl.when(i == 0)
    def _():
        total_ref[...] = jnp.zeros_like(total_ref)

    halves = (slice(0, 256), slice(256, 512))
    hidden = [
        dot(n_ref[...], weight_ref[:, cols]) + bias_ref[:, cols].astype(f32) for cols in halves
    ]
    for cols, field in zip(halves, hidden):
        value, slope = gelu_pair(field)
        act_ref[:, cols] = low(value)
        gh_ref[:, cols] = low(gact_ref[:, cols] * slope)
    total_ref[...] += contract(gh_ref[...], weight_ref[...], 1, 1)

    @pl.when(i == 3)
    def _():
        part_ref[...] = low(total_ref[...])


def feed_forward(normed_two, grad_act, fc_bias, rest):
    def tile(rows, first):
        return pl.BlockSpec((rows, 512), lambda i: (0, first + i))

    wide = pl.BlockSpec((256, 1024), lambda i: (0, 0))
    return pl.pallas_call(
        feed_kernel,
        grid=(4,),
        out_shape=(shape(256, 2048), shape(256, 2048), shape(256, 1024)),
        in_specs=[wide, tile(256, 0), tile(1, 0), tile(1024, 2)],
        out_specs=(tile(256, 0), tile(256, 0), wide),
        scratch_shapes=[pltpu.VMEM((256, 1024), f32)],
        compiler_params=ROOMY,
        cost_estimate=takes(6),
        name="feed_forward",
    )(normed_two, grad_act, fc_bias, far(rest))


def wide_kernel(n_ref, gh_ref, gm_ref, act_ref, weight_ref, out_ref, part_ref, left_ref, total_ref):
    i = pl.program_id(0)

    @pl.when(i == 0)
    def _():
        left_ref[0] = n_ref[...].T
        left_ref[1] = gm_ref[...].T
        total_ref[...] = jnp.zeros_like(total_ref)

    @pl.when(i < 4)
    def _():
        out_ref[...] = low(dot(left_ref[0], gh_ref[...]))

    @pl.when(i >= 4)
    def _():
        out_ref[...] = low(dot(left_ref[1], act_ref[...]))
        total_ref[...] += contract(act_ref[...], weight_ref[...], 1, 1)

    @pl.when(i == 7)
    def _():
        part_ref[...] = low(total_ref[...])


def wide_grads(normed_two, grad_hidden, grad_mlp, activated, rest):
    whole = pl.BlockSpec((256, 1024), lambda i: (0, 0))
    return pl.pallas_call(
        wide_kernel,
        grid=(8,),
        out_shape=(shape(1024, 4096), shape(256, 1024)),
        in_specs=[
            whole,
            pl.BlockSpec((256, 512), lambda i: (0, jnp.minimum(i, 3))),
            whole,
            pl.BlockSpec((256, 512), lambda i: (0, jnp.maximum(i - 4, 0))),
            pl.BlockSpec((1024, 512), lambda i: (0, 6 + jnp.maximum(i - 4, 0))),
        ],
        out_specs=(pl.BlockSpec((1024, 512), lambda i: (0, i)), whole),
        scratch_shapes=[pltpu.VMEM((2, 1024, 256), bf16), pltpu.VMEM((256, 1024), f32)],
        compiler_params=WHOLE,
        cost_estimate=takes(8),
        name="wide_grads",
    )(normed_two, grad_hidden, far(grad_mlp), activated, far(rest))


def middle_back_kernel(
    middle_ref, mine_ref, swapped_ref, vectors_ref, gm_ref, weight_ref, out_ref, ga_ref, gheads_ref, cols_ref
):
    gm = gm_ref[...].astype(f32)
    norm, inverse = norm_parts(middle_ref[...])
    grad = mine_ref[...].astype(f32) + swapped_ref[...].astype(f32)
    out = gm + norm_back(grad, vectors_ref[3:4, :], norm, inverse)
    out_ref[...] = out
    low_out = low(out)
    ga_ref[...] = low_out
    tp = lax.axis_index("tp")
    field = low(dot(low_out, weight_ref[:, pl.ds(pl.multiple_of(tp * 512, 512), 512)])).T
    for h in range(8):
        gheads_ref[h] = field[64 * h : 64 * (h + 1)]
    rows = [low_out.astype(f32), grad * norm, grad, gm]
    rows = [jnp.sum(r, axis=0, keepdims=True) for r in rows]
    cols_ref[...] = jnp.concatenate(rows + [jnp.zeros((4, 1024), f32)], axis=0)


def middle_back(middle, mine, swapped, vectors, grad_mlp, rest):
    def whole(*dims):
        return pl.BlockSpec(dims, lambda i: (0,) * len(dims))

    wide = whole(256, 1024)
    return pl.pallas_call(
        middle_back_kernel,
        grid=(1,),
        out_shape=(
            shape(256, 1024, kind=f32),
            shape(256, 1024),
            shape(8, 64, 256),
            shape(8, 1024, kind=f32),
        ),
        in_specs=[wide, wide, wide, whole(8, 1024), wide, whole(1024, 1024)],
        out_specs=(wide, wide, whole(8, 64, 256), whole(8, 1024)),
        compiler_params=ALL,
        cost_estimate=takes(3),
        name="middle_back",
    )(*[far(x) for x in (middle, mine, swapped, vectors, grad_mlp, rest)])


def put_block(ref, at, block):
    for g in range(32):
        ref[16 * g : 16 * (g + 1), at : at + 128] = block


def merge_kernel(query_ref, own_ref, other_ref, out_ref):
    out_ref[:, :64, :] = query_ref[...]
    out_ref[:, 64:, :] = low(own_ref[...] + other_ref[...].astype(f32))


def final_kernel(
    lengths_ref, inputs_ref, middle_ref, mine_ref, swapped_ref, vectors_ref, out_ref, roots_ref, order_ref
):
    feature_order(order_ref)
    valid = valid_rows(lengths_ref)
    inputs = inputs_ref[...].astype(f32)
    middle = middle_ref[...]
    mlp_out = mine_ref[...].astype(f32) + swapped_ref[...].astype(f32) + vectors_ref[5:6, :]
    final = middle + mlp_out
    out_ref[...] = low(contract(low(final), order_ref[...], 1, 1))
    lane = lax.broadcasted_iota(jnp.int32, (1, 128), 1)
    total = jnp.zeros((1, 128), f32)
    for k, field in enumerate((inputs, middle - inputs, mlp_out, final)):
        total = jnp.where(lane == k, jnp.sum(valid * field * field), total)
    roots_ref[...] = total


def side_kernel(ga_ref, heads_ref, rows_ref, mine_ref, theirs_ref):
    for side, ref in ((0, mine_ref), (1, theirs_ref)):
        ref[:, :512] = low(contract(of_core(ga_ref, side).T, heads_ref[...], 1, 1))
        cols = jnp.concatenate([of_core(rows_ref, side), jnp.zeros((120, 512), f32)], axis=0)
        ref[:, 512:] = low(cols.T)


def grads_into(ref, normed, grads_ref, sums, rows):
    left = normed.T
    for c in range(3):
        cols = slice(512 * c, 512 * (c + 1))
        ref[:, cols] = low(contract(left, grads_ref[cols, :], 1, 1))
    put_block(ref, 1536, sums[0])
    put_block(ref, 1664, sums[1])
    cols = [jnp.zeros((4, 512), f32), rows[:2], jnp.zeros((122, 512), f32)]
    ref[:, 1792:] = low(jnp.concatenate(cols, axis=0).T)


def sum_rows(field, dim, count, extra):
    sums = contract(jnp.ones((8, 256), bf16), field, 1, dim)[0:1]
    sums = [sums[:, 128 * r : 128 * (r + 1)] for r in range(count)]
    return low(jnp.concatenate(sums + extra, axis=0))


def back_kernel(
    gback_ref,
    own_ref,
    other_ref,
    inputs_ref,
    other_n_ref,
    roots_ref,
    gh_ref,
    keep_ref,
    send_ref,
    rows_ref,
    theirs_ref,
    grads_ref,
    sums_ref,
    norm_ref,
    part_ref,
):
    for c in range(3):
        for h in range(8):
            at = 512 * c + 64 * h
            grads_ref[at : at + 64, :] = gback_ref[h, 64 * c : 64 * (c + 1), :]
    sides = [grads_ref[512 * c : 512 * (c + 1), :].T for c in range(3)]
    norm_ref[...], _ = norm_parts(inputs_ref[...].astype(f32))
    parts = []
    for side, ref in ((0, own_ref), (1, other_ref)):
        part = sum(contract(sides[c], ref[:, 512 * c : 512 * (c + 1)], 1, 1) for c in range(3))
        part = low(part)
        for x, lanes in enumerate(core_lanes(side)):
            part_ref[:, lanes] = part[:, 128 * x : 128 * (x + 1)]
        part = part.astype(f32)
        gain = jnp.sum(part * of_core(norm_ref, side), axis=0, keepdims=True)
        shift = jnp.sum(part, axis=0, keepdims=True)
        parts.append(jnp.concatenate([gain, shift, jnp.zeros((6, 512), f32)], axis=0))
    rows_ref[...] = parts[0]
    tp = lax.axis_index("tp")
    keep_ref[...] = part_ref[pl.ds(pl.multiple_of(tp * 128, 128), 128), :]
    send_ref[...] = part_ref[pl.ds(pl.multiple_of(128 - tp * 128, 128), 128), :]
    extra = [roots_ref[...], jnp.zeros((3, 128), f32)]
    sums_ref[0] = sum_rows(grads_ref[...], 1, 12, extra)
    sums_ref[1] = sum_rows(gh_ref[...], 0, 16, [])
    grads_into(theirs_ref, other_n_ref[...], grads_ref, sums_ref, parts[1])


def core_add_kernel(
    grads_ref, own_n_ref, sums_ref, b_ref, p_ref, q_ref, rows_ref, out_ref, left_ref
):
    i = pl.program_id(0)

    @pl.when(i == 0)
    def _():
        left_ref[...] = own_n_ref[...].T

    rows = pl.ds(pl.multiple_of(i * 128, 128), 128)
    for c in range(3):
        cols = slice(512 * c, 512 * (c + 1))
        mine = low(contract(left_ref[rows, :], grads_ref[cols, :], 1, 1)).astype(f32)
        out_ref[:, cols] = low(mine + b_ref[:, cols].astype(f32))
    for k in range(2):
        at = 1536 + 128 * k
        for g in range(8):
            theirs = b_ref[16 * g : 16 * (g + 1), at : at + 128].astype(f32)
            out_ref[16 * g : 16 * (g + 1), at : at + 128] = low(sums_ref[k].astype(f32) + theirs)
    side = p_ref[...].astype(f32) + q_ref[...].astype(f32)
    out_ref[:, 1792:2304] = low(side[:, :512])
    ln1 = jnp.concatenate([jnp.zeros((4, 128), f32), rows_ref[:2], jnp.zeros((122, 128), f32)], axis=0)
    both = low(ln1.T).astype(f32) + b_ref[:, 1792:].astype(f32)
    out_ref[:, 2304:] = low(side[:, 512:] + both)


def core_add(grads, own_n, sums, theirs, mine_p, theirs_p, rows):
    def tall(cols):
        return pl.BlockSpec((128, cols), lambda i: (i, 0))

    flat = pl.BlockSpec((8, 128), lambda i: (0, i))
    return pl.pallas_call(
        core_add_kernel,
        grid=(4,),
        out_shape=shape(512, 2432),
        in_specs=[
            block_of(grads),
            block_of(own_n),
            block_of(sums),
            tall(1920),
            tall(640),
            tall(640),
            flat,
        ],
        out_specs=tall(2432),
        scratch_shapes=[pltpu.VMEM((512, 256), bf16)],
        compiler_params=ALL,
        cost_estimate=takes(4),
        name="qkv_core_sum",
    )(*[far(x) for x in (grads, own_n, sums, theirs, mine_p, theirs_p, rows)])


def end_kernel(inputs_ref, gmid_ref, mine_ref, swapped_ref, vectors_ref, out_ref, order_ref):
    feature_order(order_ref)
    rows = pl.ds(pl.multiple_of(lax.axis_index("tp") * 128, 128), 128)
    norm, inverse = norm_parts(inputs_ref[rows, :].astype(f32))
    grad = mine_ref[...].astype(f32) + swapped_ref[...].astype(f32)
    grad = gmid_ref[rows, :] + norm_back(grad, vectors_ref[0:1, :], norm, inverse)
    out_ref[...] = low(contract(low(grad), order_ref[...], 1, 1))


def join_kernel(mine_ref, theirs_ref, out_ref):
    tp = lax.axis_index("tp")
    out_ref[pl.ds(pl.multiple_of(tp * 128, 128), 128), :] = mine_ref[...]
    out_ref[pl.ds(pl.multiple_of(128 - tp * 128, 128), 128), :] = theirs_ref[...]


def total_qkv_kernel(lengths_ref, got_ref, qkv_ref, proj_ref, bias_ref, fc_ref, roots_ref):
    total = got_ref[0].astype(f32)
    for k in range(1, 32):
        total = total + got_ref[k].astype(f32)
    for c in range(3):
        qkv_ref[c] = total[:, 512 * c : 512 * (c + 1)]
    for k in range(2):
        for r in range(4):
            row = 8 * k + r
            bias_ref[k : k + 1, 128 * r : 128 * (r + 1)] = total[row : row + 1, 1536:1664]
    count = lengths_ref[0] + lengths_ref[1] + lengths_ref[2] + lengths_ref[3]
    mean = total[12:13, 1536:1664] / (count.astype(f32) * 1024.0)
    roots_ref[...] = jnp.sqrt(mean + ROOT_EPS)
    fc_ref[...] = total[:, 1664:1792]
    proj_ref[...] = total[:, 1792:2304]


def total_cols_kernel(got_ref, cols_ref):
    total = got_ref[0].astype(f32)
    for k in range(1, 32):
        total = total + got_ref[k].astype(f32)
    cols_ref[...] = total.T[:8]


def total_cols(got):
    return pl.pallas_call(
        total_cols_kernel,
        grid=(1,),
        out_shape=shape(8, 16, kind=f32),
        in_specs=[pl.BlockSpec((32, 16, 128), lambda i: (0, 0, 18))],
        out_specs=pl.BlockSpec((8, 16), lambda i: (0, 0)),
        compiler_params=ROOMY,
        cost_estimate=takes(1),
        name="total_cols",
    )(got)


def total_wide_kernel(mine_ref, theirs_ref, fc_ref, out_ref):
    total = mine_ref[...].astype(f32) + theirs_ref[...].astype(f32)
    fc_ref[...] = total[:, :2048]
    out_ref[...] = total[:, 2048:]


def body(
    tokens,
    ln1_gain,
    ln1_bias,
    qkv_weight,
    qv_bias,
    proj_weight,
    proj_bias,
    ln2_gain,
    ln2_bias,
    fc_weight,
    fc_bias,
    out_weight,
    out_bias,
    piece_starts,
    seq_lengths,
    cotangent,
):
    vectors = (ln1_gain, ln1_bias, proj_bias, ln2_gain, ln2_bias, out_bias)
    pay_q = call(
        prepare_kernel,
        "weights_payload",
        shape(32, 16, 1664),
        qkv_weight,
        *[v.reshape(1, 16) for v in vectors],
    )
    own_q = exchange(pay_q, SPREAD).reshape(512, 1664)
    proj_rows = proj_weight.T
    pay_r = call(
        prepare_rest_kernel, "rest_payload", shape(16, 4608), proj_rows, fc_weight, out_weight.T
    )
    pair_r = call(
        pair_kernel,
        "rest_pair",
        shape(32, 5120),
        after(pay_r, pay_q),
        swap(pay_r, "zh"),
        swap(proj_rows, "tp"),
        lax.ppermute(proj_rows, ("zh", "tp"), [(i, 3 - i) for i in range(4)]),
    )
    rest = lax.all_gather(pair_r, ("x", "c", "y"), axis=0, tiled=True)

    inputs, grad_mlp = call(
        inputs_kernel,
        "inputs",
        (shape(256, 1024), shape(256, 1024)),
        seq_lengths,
        tokens[0],
        cotangent[0],
        scalars=1,
        cost=300,
        scratch=[pltpu.VMEM((1024, 1024), bf16)],
    )
    own_q = after(own_q, inputs)
    other_q = swap(own_q, "c")
    heads, own_n, other_n, vectors = call(
        qkv_kernel,
        "qkv",
        (shape(8, 192, 256), shape(256, 512), shape(256, 512), shape(8, 1024, kind=f32)),
        inputs,
        own_q,
        other_q,
        qv_bias,
        scratch=[pltpu.VMEM((256, 1024), bf16)],
        cost=3,
    )
    own = exchange(heads, LINE)
    other = swap(own[:, 64:], "c")
    attended, attended_low, log_sum = attn_forward(seq_lengths, piece_starts, own, other)
    heads_all = exchange(attended_low.reshape(16, 64, 256), ("zh", "y", "tp"))
    staged = attn_stage(own, other, log_sum)
    grad_act = grad_activated(grad_mlp, after(rest, attended_low))
    middle, normed_two, heads_out = attention_end(
        after(heads_all, staged[0], grad_act), rest, inputs, vectors
    )
    activated, grad_hidden, two_part = feed_forward(
        normed_two, grad_act, fc_bias.reshape(1, 2048), rest
    )
    two_swapped = swap(two_part, "tp")
    wide, mlp_part = wide_grads(normed_two, grad_hidden, grad_mlp, activated, rest)
    wide = lax.psum_scatter(
        after(wide, two_swapped), ("x", "c"), scatter_dimension=0, tiled=True
    )
    two_swapped = after(two_swapped, mlp_part)
    grad_middle, grad_attn, grad_heads, rows = middle_back(
        middle, two_part, two_swapped, vectors, grad_mlp, rest
    )
    grad_mine = exchange(grad_heads, LINE)

    mine_p, theirs_p = call(
        side_kernel,
        "proj_grads",
        (shape(512, 640), shape(512, 640)),
        far(grad_attn),
        far(heads_out),
        rows,
        cost=2,
    )
    grad_mine = after(grad_mine, mine_p)
    theirs_p = swap(after(theirs_p, grad_mine), "c")
    mlp_swapped = swap(after(mlp_part, grad_mine), "tp")

    grad_query, grad_own, grad_other = attn_backward(
        seq_lengths, piece_starts, staged, grad_mine, attended
    )
    grad_other, mlp_swapped = lax.optimization_barrier((grad_other, mlp_swapped))
    grad_back = call(
        merge_kernel, "merge", shape(8, 192, 256), grad_query, grad_own, swap(grad_other, "c")
    )
    grad_back = exchange(grad_back, LINE)
    layer_out, roots = call(
        final_kernel,
        "final",
        (shape(256, 1024), shape(1, 128, kind=f32)),
        seq_lengths,
        far(inputs),
        far(middle),
        after(mlp_part, grad_other),
        mlp_swapped,
        vectors,
        scalars=1,
        cost=3,
        scratch=[pltpu.VMEM((1024, 1024), bf16)],
    )
    one_keep, one_send, rows, theirs_q, grads, sums = call(
        back_kernel,
        "back",
        (
            shape(128, 1024),
            shape(128, 1024),
            shape(8, 512, kind=f32),
            shape(512, 1920),
            shape(1536, 256),
            shape(2, 16, 128),
        ),
        grad_back,
        far(own_q),
        far(other_q),
        far(inputs),
        far(other_n),
        roots,
        far(grad_hidden),
        cost=5,
        scratch=[pltpu.VMEM((256, 1024), f32), pltpu.VMEM((256, 1024), bf16)],
        memory=ALL,
    )
    one_swapped = swap(one_send, "tp")
    wide = lax.psum_scatter(after(wide, roots), "y", scatter_dimension=0, tiled=True)
    both = core_add(
        grads,
        own_n,
        sums,
        after(swap(theirs_q, "c"), one_swapped),
        mine_p,
        theirs_p,
        rows,
    )
    got_q = exchange(both.reshape(32, 16, 2432), SPREAD)
    half_tokens = call(
        end_kernel,
        "end",
        shape(128, 1024),
        far(inputs),
        far(grad_middle),
        one_keep,
        one_swapped,
        vectors,
        cost=2,
        scratch=[pltpu.VMEM((1024, 1024), bf16)],
    )
    half_swapped = swap(half_tokens, "tp")
    zh = lax.axis_index("zh")
    keep = lax.dynamic_slice_in_dim(wide, zh * 16, 16, 0)
    send = lax.dynamic_slice_in_dim(wide, 16 - zh * 16, 16, 0)
    grad_fc, grad_out = call(
        total_wide_kernel,
        "total_wide",
        (shape(16, 2048, kind=f32), shape(16, 2048, kind=f32)),
        keep,
        swap(send, "zh"),        cost=14,
    )
    got_q = after(got_q, grad_fc, half_swapped)
    cols = total_cols(got_q)
    ln1 = cols[4:6]
    grad_qkv, grad_proj, bias_sums, fc_sums, roots = call(
        total_qkv_kernel,
        "total_qkv",
        (
            shape(3, 16, 512, kind=f32),
            shape(16, 512, kind=f32),
            shape(2, 512, kind=f32),
            shape(16, 128, kind=f32),
            shape(1, 128, kind=f32),
        ),
        seq_lengths,
        after(got_q, cols),
        scalars=1,
    )
    ln1_swapped = swap(ln1, "tp")
    half_swapped = after(half_swapped, grad_qkv)
    grad_tokens = call(
        join_kernel, "join", shape(256, 1024), half_tokens, half_swapped
    )
    ln1 = ln1 + ln1_swapped
    return (
        layer_out[None],
        grad_tokens[None],
        ln1[0],
        ln1[1],
        grad_qkv.transpose(1, 0, 2),
        bias_sums,
        grad_proj.T,
        cols[0],
        cols[1],
        cols[2],
        grad_fc,
        fc_sums.reshape(2048),
        grad_out.T,
        cols[3],
        roots[0, :4],
    )


def solution(mesh):
    fine = Mesh(mesh.devices.reshape(4, 2, 4, 2, 2), ("x", "zh", "y", "c", "tp"))
    ctx = ("zh", "y", "c")
    every = ("x", "zh", "y", "c")
    in_specs = (
        P("x", ctx, None),
        P(every),
        P(every),
        P(every, None, "tp"),
        P(None, "tp"),
        P("tp", every),
        P(every),
        P(every),
        P(every),
        P(every, "tp"),
        P("tp"),
        P("tp", every),
        P(every),
        P("x", None),
        P(),
        P("x", ctx, None),
    )
    out_specs = (
        P("x", ctx, None),
        P("x", ctx, None),
        P(every),
        P(every),
        P(every, None, "tp"),
        P(None, "tp"),
        P("tp", every),
        P(every),
        P(every),
        P(every),
        P(every, "tp"),
        P("tp"),
        P("tp", every),
        P(every),
        P(),
    )
    return jax.shard_map(body, mesh=fine, in_specs=in_specs, out_specs=out_specs, check_vma=False)
```

```python
from functools import partial

import jax
import jax.numpy as jnp
from jax import lax
from jax.experimental import pallas as pl
from jax.experimental.pallas import tpu as pltpu
from jax.sharding import Mesh
from jax.sharding import PartitionSpec as P

f32 = jnp.float32
bf16 = jnp.bfloat16
NORM_EPS = 1e-05
ROOT_EPS = 1e-06
B=256; E=64; NB=16; MASKED=-1e30; PIECE=256

class Facts:
    def __init__(self, lengths_ref, starts_ref):
        self.core = lax.axis_index("c")
        self.items = (self.core, lengths_ref[lax.axis_index("x")], starts_ref[0, 0], starts_ref[0, 1])

    def __getitem__(self, at):
        return self.items[at]


def piece_of(pos, info_ref):
    n0=(pos>=info_ref[2])&(pos<info_ref[2]+PIECE)
    n1=(pos>=info_ref[3])&(pos<info_ref[3]+PIECE)
    return jnp.where(n0,1,0)+jnp.where(n1,2,0)

def allowed_block(key_block, query_block, info_ref):
    kpos=key_block*B+lax.broadcasted_iota(jnp.int32,(B,1),0)
    qpos=query_block*B+lax.broadcasted_iota(jnp.int32,(1,B),1)
    kp=piece_of(kpos,info_ref); qp=piece_of(qpos,info_ref)
    qp=jnp.where(qp==0,-1,qp)
    kp=jnp.where(kpos<info_ref[1],kp,-2)
    kpos=jnp.where(kpos<info_ref[1],kpos,1<<20)
    return (kpos<=qpos)|(kp==qp)

def extra_blocks(p, info_ref):
    edge=(2*p+2)*B
    crosses=((info_ref[2]<edge)&(edge<info_ref[2]+PIECE))|((info_ref[3]<edge)&(edge<info_ref[3]+PIECE))
    return jnp.where((info_ref[0]==1)&(p<NB//2-1)&crosses,1,0)

def dot(a,b): return jnp.dot(a,b,preferred_element_type=f32)

SAFE = 60.0


def split3(row):
    top = row.astype(bf16).astype(f32)
    mid = (row - top).astype(bf16).astype(f32)
    rows = jnp.concatenate([top, mid, row - top - mid, jnp.zeros((13, row.shape[1]), f32)], axis=0)
    return rows.astype(bf16)


def ones_beside(block):
    lane = lax.broadcasted_iota(jnp.int32, (B, 16), 1)
    return jnp.concatenate([block, jnp.where(lane < 3, 1.0, 0.0).astype(bf16)], axis=1)


CHUNK = 4 * B


def pair_allowed(m, info_ref):
    key = m * CHUNK + lax.broadcasted_iota(jnp.int32, (CHUNK, 1), 0)
    lane = lax.broadcasted_iota(jnp.int32, (1, 2 * B), 1)
    query = (4 * m + info_ref[0]) * B + lane + jnp.where(lane >= B, B, 0)
    key_piece, query_piece = piece_of(key, info_ref), piece_of(query, info_ref)
    query_piece = jnp.where(query_piece == 0, -1, query_piece)
    valid = key < info_ref[1]
    key_piece = jnp.where(valid, key_piece, -2)
    key = jnp.where(valid, key, 1 << 20)
    return (key <= query) | (key_piece == query_piece)


def pair_of(ref, m):
    return jnp.concatenate([ref[2 * m], ref[2 * m + 1]], axis=1)


def walk(m, extra, step, beyond, carry):
    def chunk(i, c):
        return step(pl.multiple_of(i * CHUNK, CHUNK), None, c)

    carry = lax.fori_loop(0, m, chunk, carry)
    first = pl.multiple_of(m * CHUNK, CHUNK)
    carry = step(first, m, carry)
    second = lax.fori_loop(
        0, extra, lambda i, c: beyond(pl.multiple_of(first + CHUNK, B), c), carry[:, B:]
    )
    return carry[:, :B], second


def masked_from(e, first, count, masked, query_block, info_ref):
    if not masked:
        return e
    keep = count - masked * B
    parts = [e[:keep]] if keep else []
    for at in range(keep, count, B):
        allowed = allowed_block((first >> 8) + at // B, query_block, info_ref)
        parts.append(jnp.where(allowed, e[at : at + B], 0.0))
    return jnp.concatenate(parts, axis=0)


def place(block):
    return pl.ds(pl.multiple_of(block * B, B), B)


def walk_all(p, extra, step, carry, chunk):
    end = 2 * B * (p + 1)
    for first in range(0, end, chunk):
        last = min(first + chunk, end)
        carry = step(first, last - first, max(0, last - (end - 2 * B)) // B, carry)
    if p == NB // 2 - 1:
        return carry
    return lax.fori_loop(0, extra, lambda i, c: step(end, B, 1, c), carry)


def forward_kernel(lengths_ref, starts_ref, own_ref, other_ref, out_ref, low_ref, lse_ref, key_ref, value_ref):
    info_ref = Facts(lengths_ref, starts_ref)
    core = info_ref[0]
    sublane = lax.broadcasted_iota(jnp.int32, (16, NB * B), 0)
    value_ref[E:, :] = jnp.where(sublane == 0, 1.0, 0.0).astype(bf16)

    def squares(block):
        field = block.astype(f32)
        return jnp.sum(field * field, axis=0, keepdims=True)

    query_top = jnp.zeros((1, B), f32)
    key_top = jnp.zeros((1, B), f32)
    for p in range(NB // 2):
        mine, theirs = own_ref[p, E : 2 * E, :], other_ref[p, :E, :]
        here, there = place(2 * p + core), place(2 * p + 1 - core)
        key_ref[here, :] = mine.T
        key_ref[there, :] = theirs.T
        value_ref[:E, here] = own_ref[p, 2 * E :, :]
        value_ref[:E, there] = other_ref[p, E:, :]
        query_top = jnp.maximum(query_top, squares(own_ref[p, :E, :]))
        key_top = jnp.maximum(key_top, jnp.maximum(squares(mine), squares(theirs)))
    bound = jnp.max(query_top) * jnp.max(key_top)

    def finish(p, top, acc):
        total = acc[E : E + 1]
        o = acc[:E] / total
        out_ref[p] = o
        low_ref[p, 0] = o.astype(bf16)
        low_ref[p, 1] = o.astype(bf16)
        lse_ref[p] = top + jnp.log(total)

    @pl.when(bound <= (8.0 * SAFE) ** 2)
    def _():
        def both(m, _):
            query = pair_of(own_ref.at[:, :E, :], m) * jnp.asarray(0.125, bf16)

            def step(first, masked, acc):
                at = pl.ds(first, CHUNK)
                e = jnp.exp(dot(key_ref[at, :], query))
                if masked is not None:
                    e = jnp.where(pair_allowed(masked, info_ref), e, 0.0)
                return acc + dot(value_ref[:, at], e.astype(bf16))

            def beyond(first, acc):
                at = pl.ds(first, B)
                e = jnp.exp(dot(key_ref[at, :], query[:, B:]))
                e = jnp.where(allowed_block(4 * m + 4, 4 * m + 2 + core, info_ref), e, 0.0)
                return acc + dot(value_ref[:, at], e.astype(bf16))

            accs = walk(
                m, extra_blocks(2 * m + 1, info_ref), step, beyond, jnp.zeros((E + 16, 2 * B), f32)
            )
            for odd in range(2):
                finish(2 * m + odd, 0.0, accs[odd])
            return 0

        lax.fori_loop(0, NB // 4, both, 0)

    @pl.when(bound > (8.0 * SAFE) ** 2)
    def _():
        def one(p, _):
            query = own_ref[p, :E, :] * jnp.asarray(0.125, bf16)
            qb = 2 * p + core

            def step(blocks, masked, carry):
                top, acc = carry
                scores = [dot(key_ref[place(j), :], query) for j in blocks]
                if masked:
                    scores = [
                        jnp.where(allowed_block(j, qb, info_ref), s, MASKED)
                        for j, s in zip(blocks, scores)
                    ]
                new = top
                for s in scores:
                    new = jnp.maximum(new, jnp.max(s, axis=0, keepdims=True))
                acc = acc * jnp.exp(top - new)
                for j, s in zip(blocks, scores):
                    acc = acc + dot(value_ref[:, place(j)], jnp.exp(s - new).astype(bf16))
                return new, acc

            carry = (jnp.full((1, B), MASKED, f32), jnp.zeros((E + 16, B), f32))
            carry = step((2 * p, 2 * p + 1), True, carry)
            carry = lax.fori_loop(0, p, lambda i, c: step((2 * i, 2 * i + 1), False, c), carry)
            carry = lax.fori_loop(
                0, extra_blocks(p, info_ref), lambda i, c: step((2 * p + 2,), True, c), carry
            )
            finish(p, *carry)
            return 0

        lax.fori_loop(0, NB // 2, one, 0)


def stage_kernel(own_ref, other_ref, lse_ref, key_ref, keyt_ref, value_ref, query_ref, rows_ref):
    core = lax.axis_index("c")
    blank = jnp.zeros((B, E), bf16)
    for p in range(NB // 2):
        mine, theirs = own_ref[p, E : 2 * E, :], other_ref[p, :E, :]
        here, there = place(2 * p + core), place(2 * p + 1 - core)
        keyt_ref[:, here] = mine
        keyt_ref[:, there] = theirs
        key_ref[here, :] = ones_beside(mine.T)
        key_ref[there, :] = ones_beside(theirs.T)
        value_ref[here, :] = ones_beside(own_ref[p, 2 * E :, :].T)
        value_ref[there, :] = ones_beside(other_ref[p, E:, :].T)
        query = own_ref[p, :E, :] * jnp.asarray(0.125, bf16)
        query_ref[p, :E, :] = query
        query_ref[p, E:, :] = split3(-lse_ref[p])
        rows_ref[p] = jnp.concatenate([blank, query.T], axis=1)


def backward_kernel(
    lengths_ref,
    starts_ref,
    key_ref,
    keyt_ref,
    value_ref,
    query_ref,
    rows_ref,
    gout_ref,
    out_ref,
    gq_ref,
    gown_ref,
    gother_ref,
    grad_ref,
    gouts_ref,
    grows_ref,
    sum_ref,
):
    info_ref = Facts(lengths_ref, starts_ref)
    core = info_ref[0]
    grad_ref[...] = jnp.zeros_like(grad_ref)
    blank = jnp.zeros((B, E), bf16)
    for p in range(NB // 2):
        gout = gout_ref[p]
        delta = jnp.sum(gout.astype(f32) * out_ref[p], axis=0, keepdims=True)
        gouts_ref[p, :E, :] = gout
        gouts_ref[p, E:, :] = split3(-delta)
        grows_ref[p] = jnp.concatenate([gout.T, blank], axis=1)
    sum_ref[...] = jnp.zeros_like(sum_ref)

    def chunk(p, first, count, masked):
        at = pl.ds(pl.multiple_of(first, B), count)
        e = jnp.exp(dot(key_ref[at, :], query_ref[p]))
        if masked:
            e = masked_from(e, first, count, masked, 2 * p + core, info_ref)
        gs = (e * dot(value_ref[at, :], gouts_ref[p])).astype(bf16)
        grad_ref[at, :] += dot(e.astype(bf16), grows_ref[p]) + dot(gs, rows_ref[p])
        sum_ref[p] += dot(keyt_ref[:, at], gs)

    def both(m, _):
        top = NB // 2 - 1 - m
        for k in range(NB // 2 - 1):
            late = k < top
            chunk(jnp.where(late, top, m), 2 * B * jnp.where(late, k, k - top), 2 * B, 0)
        chunk(top, 2 * B * top, 2 * B, 2)
        chunk(m, 2 * B * m, 2 * B, 2)
        return 0

    lax.fori_loop(0, NB // 4, both, 0)

    def beyond(p, _):
        def add(i, _):
            chunk(p, 2 * B * (p + 1), B, 1)
            return 0

        return lax.fori_loop(0, extra_blocks(p, info_ref), add, 0)

    lax.fori_loop(0, NB // 2 - 1, beyond, 0)
    for p in range(NB // 2):
        gq_ref[p] = (sum_ref[p] * 0.125).astype(bf16)
    for p in range(NB // 2):
        mine = grad_ref[place(2 * p + core), :].T
        theirs = grad_ref[place(2 * p + 1 - core), :].T.astype(bf16)
        gown_ref[p, :E, :] = mine[E:]
        gown_ref[p, E:, :] = mine[:E]
        gother_ref[p, :E, :] = theirs[E:]
        gother_ref[p, E:, :] = theirs[:E]


VM=pl.BlockSpec(memory_space=pltpu.VMEM); SM=pl.BlockSpec(memory_space=pltpu.SMEM)
LIMIT=40*1024*1024
def attn_forward(lengths,starts,own,other):
    H=NB//2
    return pl.pallas_call(forward_kernel,
        out_shape=(jax.ShapeDtypeStruct((H,E,B),f32),jax.ShapeDtypeStruct((H,2,E,B),bf16),jax.ShapeDtypeStruct((H,1,B),f32)),
        in_specs=[SM,SM,VM,VM],out_specs=(VM,VM,VM),
        scratch_shapes=[pltpu.VMEM((NB*B,E),bf16),pltpu.VMEM((E+16,NB*B),bf16)],
        compiler_params=pltpu.CompilerParams(vmem_limit_bytes=LIMIT),
        cost_estimate=takes(8),
        name="attention_forward")(lengths,starts,own,other)
def attn_stage(own, other, lse):
    half = NB // 2
    outs = (
        jax.ShapeDtypeStruct((NB * B, E + 16), bf16),
        jax.ShapeDtypeStruct((E, NB * B), bf16),
        jax.ShapeDtypeStruct((NB * B, E + 16), bf16),
        jax.ShapeDtypeStruct((half, E + 16, B), bf16),
        jax.ShapeDtypeStruct((half, B, 2 * E), bf16),
    )
    return pl.pallas_call(
        stage_kernel,
        out_shape=outs,
        in_specs=[VM] * 3,
        out_specs=(VM,) * 5,
        compiler_params=pltpu.CompilerParams(vmem_limit_bytes=LIMIT),
        cost_estimate=takes(1),
        name="attention_stage",
    )(own, other, lse)


def attn_backward(lengths, starts, staged, gout, out):
    half = NB // 2

    def full(array):
        return pl.BlockSpec(array.shape, lambda i: (0,) * len(array.shape))

    outs = (
        jax.ShapeDtypeStruct((half, E, B), bf16),
        jax.ShapeDtypeStruct((half, 2 * E, B), f32),
        jax.ShapeDtypeStruct((half, 2 * E, B), bf16),
    )
    return pl.pallas_call(
        backward_kernel,
        grid=(1,),
        out_shape=outs,
        in_specs=[SM, SM] + [full(x) for x in (*staged, gout, out)],
        out_specs=tuple(full(x) for x in outs),
        scratch_shapes=[
            pltpu.VMEM((NB * B, 2 * E), f32),
            pltpu.VMEM((half, E + 16, B), bf16),
            pltpu.VMEM((half, B, 2 * E), bf16),
            pltpu.VMEM((half, E, B), f32),
        ],
        compiler_params=pltpu.CompilerParams(vmem_limit_bytes=LIMIT),
        cost_estimate=takes(26),
        name="attention_backward",
    )(lengths, starts, *[far(x) for x in staged], gout, far(out))


SPREAD = ("x", "y", "zh")
LINE = ("zh", "y")
VM = pl.BlockSpec(memory_space=pltpu.VMEM)
SM = pl.BlockSpec(memory_space=pltpu.SMEM)
ANY = pl.BlockSpec(memory_space=pl.ANY)
ROOMY = pltpu.CompilerParams(vmem_limit_bytes=40 * 1024 * 1024)
WHOLE = pltpu.CompilerParams(vmem_limit_bytes=50 * 1024 * 1024)
ALL = pltpu.CompilerParams(vmem_limit_bytes=62 * 1024 * 1024)


def takes(microseconds):
    return pl.CostEstimate(
        flops=int(microseconds * 1.15e9), bytes_accessed=1 << 20, transcendentals=0
    )


def low(field):
    return field.astype(bf16)


def swap(field, axis):
    return lax.ppermute(field, axis, [(0, 1), (1, 0)])


def exchange(field, axes):
    return lax.all_to_all(field, axes, split_axis=0, concat_axis=0, tiled=True)


def after(field, *others):
    return lax.optimization_barrier((field, *others))[0]


def contract(a, b, dim_a, dim_b):
    return lax.dot_general(a, b, (((dim_a,), (dim_b,)), ((), ())), preferred_element_type=f32)


def shape(*dims, kind=bf16):
    return jax.ShapeDtypeStruct(dims, kind)


def far(field):
    return pltpu.with_memory_space_constraint(field, pltpu.HBM)


def block_of(array):
    dims = len(array.shape)
    return pl.BlockSpec(array.shape, lambda *_: (0,) * dims)


def call(kernel, name, outs, *args, scalars=0, cost=1, scratch=(), memory=ROOMY):
    return pl.pallas_call(
        kernel,
        grid=(1,),
        out_shape=outs,
        in_specs=[SM] * scalars + [block_of(a) for a in args[scalars:]],
        out_specs=jax.tree.map(block_of, outs),
        scratch_shapes=list(scratch),
        compiler_params=memory,
        cost_estimate=takes(cost),
        name=name,
    )(*args)


def feature_order(order_ref):
    place = lax.broadcasted_iota(jnp.int32, (1, 1024), 1)
    x, core, y, zh = place >> 8, (place >> 7) & 1, (place >> 5) & 3, (place >> 4) & 1
    feature = ((((x * 2 + zh) * 4 + y) * 2 + core) << 4) + (place & 15)
    for at in range(0, 1024, 256):
        rows = at + lax.broadcasted_iota(jnp.int32, (256, 1024), 0)
        order_ref[at : at + 256, :] = jnp.where(rows == feature, 1.0, 0.0).astype(bf16)


def core_lanes(side):
    core = lax.axis_index("c") ^ side
    return [pl.ds(pl.multiple_of(256 * x + 128 * core, 128), 128) for x in range(4)]


def of_core(ref, side):
    return jnp.concatenate([ref[:, lanes] for lanes in core_lanes(side)], axis=1)


def valid_rows(lengths_ref):
    ctx = (lax.axis_index("zh") * 4 + lax.axis_index("y")) * 2 + lax.axis_index("c")
    position = ctx * 256 + lax.broadcasted_iota(jnp.int32, (256, 1), 0)
    return jnp.where(position < lengths_ref[lax.axis_index("x")], 1.0, 0.0)


def norm_parts(values):
    center = values - jnp.mean(values, axis=-1, keepdims=True)
    inverse = lax.rsqrt(jnp.mean(center * center, axis=-1, keepdims=True) + NORM_EPS)
    return center * inverse, inverse


def norm_back(grad, gain, norm, inverse):
    scaled = grad * gain
    return inverse * (
        scaled
        - jnp.mean(scaled, axis=-1, keepdims=True)
        - norm * jnp.mean(scaled * norm, axis=-1, keepdims=True)
    )


def gelu_pair(u):
    k = 0.7978845608028654
    square = u * u
    t = jnp.tanh(u * (k + (k * 0.044715) * square))
    half = 0.5 + 0.5 * t
    value = u * half
    slope = half + (0.5 * u) * (1.0 - t * t) * (k + (3 * 0.044715 * k) * square)
    return value, slope


def prepare_kernel(qkv_ref, a_ref, b_ref, c_ref, d_ref, e_ref, g_ref, out_ref):
    rows = [r[...].astype(f32) for r in (a_ref, b_ref, c_ref, d_ref, e_ref, g_ref)]
    small = jnp.concatenate(rows + [jnp.zeros((2, 16), f32)], axis=0).T
    small = low(jnp.concatenate([small, jnp.zeros((16, 120), f32)], axis=1))

    def one(k, _):
        for c in range(3):
            out_ref[k, :, 512 * c : 512 * (c + 1)] = qkv_ref[:, c, :]
        out_ref[k, :, 1536:] = small
        return 0

    lax.fori_loop(0, 32, one, 0)


def prepare_rest_kernel(proj_ref, fc_ref, out_ref, rest_ref):
    rest_ref[:, :512] = proj_ref[...]
    rest_ref[:, 512:2560] = fc_ref[...]
    rest_ref[:, 2560:] = out_ref[...]


def pair_kernel(mine_ref, by_zh_ref, by_tp_ref, by_both_ref, out_ref):
    zh, tp = lax.axis_index("zh"), lax.axis_index("tp")
    here = pl.ds(pl.multiple_of(zh * 16, 16), 16)
    there = pl.ds(pl.multiple_of(16 - zh * 16, 16), 16)
    near = pl.ds(pl.multiple_of(tp * 512, 512), 512)
    far_off = pl.ds(pl.multiple_of(512 - tp * 512, 512), 512)
    for rows, ref, other_ref in ((here, mine_ref, by_tp_ref), (there, by_zh_ref, by_both_ref)):
        out_ref[rows, near] = ref[:, :512]
        out_ref[rows, far_off] = other_ref[...]
        out_ref[rows, 1024:] = ref[:, 512:]


def inputs_kernel(lengths_ref, tokens_ref, cotangent_ref, inputs_ref, grad_ref, order_ref):
    feature_order(order_ref)
    inputs_ref[...] = low(dot(tokens_ref[...], order_ref[...]))
    grad = dot(cotangent_ref[...], order_ref[...]) * valid_rows(lengths_ref)
    grad_ref[...] = low(grad)


def qkv_kernel(
    inputs_ref, own_ref, other_ref, bias_ref, heads_ref, own_n_ref, other_n_ref, vectors_ref, normed_ref
):
    for side, ref in ((0, own_ref), (1, other_ref)):
        small = ref[:, 1536:].astype(f32).T[:8]
        for x, lanes in enumerate(core_lanes(side)):
            vectors_ref[:, lanes] = small[:, 128 * x : 128 * (x + 1)]
    norm, _ = norm_parts(inputs_ref[...].astype(f32))
    normed_ref[...] = low(norm * vectors_ref[0:1, :] + vectors_ref[1:2, :])
    own_n_ref[...] = of_core(normed_ref, 0)
    other_n_ref[...] = of_core(normed_ref, 1)
    for c in range(3):
        cols = slice(512 * c, 512 * (c + 1))
        field = dot(own_n_ref[...], own_ref[:, cols]) + dot(other_n_ref[...], other_ref[:, cols])
        if c != 1:
            field = field + bias_ref[c // 2 : c // 2 + 1, :].astype(f32)
        field = low(field).T
        for h in range(8):
            heads_ref[h, 64 * c : 64 * (c + 1), :] = field[64 * h : 64 * (h + 1)]


def attn_end_kernel(heads_ref, weight_ref, inputs_ref, vectors_ref, middle_ref, n_ref, own_ref, wide_ref):
    tp = lax.axis_index("tp")
    for h in range(8):
        for t in range(2):
            at = 512 * t + 64 * h
            wide_ref[at : at + 64, :] = heads_ref[2 * h + t]
        own_ref[64 * h : 64 * (h + 1), :] = heads_ref[2 * h + tp]
    attn_out = contract(wide_ref[...].T, weight_ref[...], 1, 1) + vectors_ref[2:3, :]
    middle = inputs_ref[...].astype(f32) + attn_out
    middle_ref[...] = middle
    norm, _ = norm_parts(middle)
    n_ref[...] = low(norm * vectors_ref[3:4, :] + vectors_ref[4:5, :])


def attention_end(heads_all, rest, inputs, vectors):
    wide = pl.BlockSpec((256, 1024), lambda i: (0, 0))
    return pl.pallas_call(
        attn_end_kernel,
        grid=(1,),
        out_shape=(shape(256, 1024, kind=f32), shape(256, 1024), shape(512, 256)),
        in_specs=[
            pl.BlockSpec((16, 64, 256), lambda i: (0, 0, 0)),
            pl.BlockSpec((1024, 1024), lambda i: (0, 0)),
            wide,
            pl.BlockSpec((8, 1024), lambda i: (0, 0)),
        ],
        out_specs=(wide, wide, pl.BlockSpec((512, 256), lambda i: (0, 0))),
        scratch_shapes=[pltpu.VMEM((1024, 256), bf16)],
        compiler_params=ROOMY,
        cost_estimate=takes(3),
        name="attn_end",
    )(heads_all, far(rest), far(inputs), far(vectors))


def grad_act_kernel(gm_ref, weight_ref, out_ref):
    out_ref[...] = dot(gm_ref[...], weight_ref[...])


def grad_activated(grad_mlp, rest):
    return pl.pallas_call(
        grad_act_kernel,
        grid=(4,),
        out_shape=shape(256, 2048, kind=f32),
        in_specs=[
            pl.BlockSpec((256, 1024), lambda i: (0, 0)),
            pl.BlockSpec((1024, 512), lambda i: (0, 6 + i)),
        ],
        out_specs=pl.BlockSpec((256, 512), lambda i: (0, i)),
        compiler_params=ROOMY,
        cost_estimate=takes(3),
        name="grad_act",
    )(far(grad_mlp), far(rest))


def feed_kernel(n_ref, gact_ref, bias_ref, weight_ref, act_ref, gh_ref, part_ref, total_ref):
    i = pl.program_id(0)

    @pl.when(i == 0)
    def _():
        total_ref[...] = jnp.zeros_like(total_ref)

    halves = [slice(at, at + 256) for at in range(0, 1024, 256)]
    hidden = [
        dot(n_ref[...], weight_ref[:, cols]) + bias_ref[:, cols].astype(f32) for cols in halves
    ]
    for cols, field in zip(halves, hidden):
        value, slope = gelu_pair(field)
        act_ref[:, cols] = low(value)
        gh_ref[:, cols] = low(gact_ref[:, cols] * slope)
    total_ref[...] += contract(gh_ref[...], weight_ref[...], 1, 1)

    @pl.when(i == 1)
    def _():
        part_ref[...] = low(total_ref[...])


def feed_forward(normed_two, grad_act, fc_bias, rest):
    def tile(rows, first):
        return pl.BlockSpec((rows, 1024), lambda i: (0, first + i))

    wide = pl.BlockSpec((256, 1024), lambda i: (0, 0))
    return pl.pallas_call(
        feed_kernel,
        grid=(2,),
        out_shape=(shape(256, 2048), shape(256, 2048), shape(256, 1024)),
        in_specs=[wide, tile(256, 0), tile(1, 0), tile(1024, 1)],
        out_specs=(tile(256, 0), tile(256, 0), wide),
        scratch_shapes=[pltpu.VMEM((256, 1024), f32)],
        compiler_params=ROOMY,
        cost_estimate=takes(6),
        name="feed_forward",
    )(normed_two, grad_act, fc_bias, far(rest))


def wide_kernel(n_ref, gh_ref, gm_ref, act_ref, weight_ref, out_ref, part_ref, left_ref, total_ref):
    i = pl.program_id(0)

    @pl.when(i == 0)
    def _():
        left_ref[0] = n_ref[...].T
        left_ref[1] = gm_ref[...].T
        total_ref[...] = jnp.zeros_like(total_ref)

    @pl.when(i < 4)
    def _():
        out_ref[...] = low(dot(left_ref[0], gh_ref[...]))

    @pl.when(i >= 4)
    def _():
        out_ref[...] = low(dot(left_ref[1], act_ref[...]))
        total_ref[...] += contract(act_ref[...], weight_ref[...], 1, 1)

    @pl.when(i == 7)
    def _():
        part_ref[...] = low(total_ref[...])


def wide_grads(normed_two, grad_hidden, grad_mlp, activated, rest):
    whole = pl.BlockSpec((256, 1024), lambda i: (0, 0))
    return pl.pallas_call(
        wide_kernel,
        grid=(8,),
        out_shape=(shape(1024, 4096), shape(256, 1024)),
        in_specs=[
            whole,
            pl.BlockSpec((256, 512), lambda i: (0, jnp.minimum(i, 3))),
            whole,
            pl.BlockSpec((256, 512), lambda i: (0, jnp.maximum(i - 4, 0))),
            pl.BlockSpec((1024, 512), lambda i: (0, 6 + jnp.maximum(i - 4, 0))),
        ],
        out_specs=(pl.BlockSpec((1024, 512), lambda i: (0, i)), whole),
        scratch_shapes=[pltpu.VMEM((2, 1024, 256), bf16), pltpu.VMEM((256, 1024), f32)],
        compiler_params=WHOLE,
        cost_estimate=takes(8),
        name="wide_grads",
    )(normed_two, grad_hidden, far(grad_mlp), activated, far(rest))


def middle_back_kernel(
    middle_ref, mine_ref, swapped_ref, vectors_ref, gm_ref, weight_ref, out_ref, ga_ref, gheads_ref, cols_ref
):
    gm = gm_ref[...].astype(f32)
    norm, inverse = norm_parts(middle_ref[...])
    grad = mine_ref[...].astype(f32) + swapped_ref[...].astype(f32)
    out = gm + norm_back(grad, vectors_ref[3:4, :], norm, inverse)
    out_ref[...] = out
    low_out = low(out)
    ga_ref[...] = low_out
    tp = lax.axis_index("tp")
    field = low(dot(low_out, weight_ref[:, pl.ds(pl.multiple_of(tp * 512, 512), 512)])).T
    for h in range(8):
        gheads_ref[h] = field[64 * h : 64 * (h + 1)]
    rows = [low_out.astype(f32), grad * norm, grad, gm]
    rows = [jnp.sum(r, axis=0, keepdims=True) for r in rows]
    cols_ref[...] = jnp.concatenate(rows + [jnp.zeros((4, 1024), f32)], axis=0)


def middle_back(middle, mine, swapped, vectors, grad_mlp, rest):
    def whole(*dims):
        return pl.BlockSpec(dims, lambda i: (0,) * len(dims))

    wide = whole(256, 1024)
    return pl.pallas_call(
        middle_back_kernel,
        grid=(1,),
        out_shape=(
            shape(256, 1024, kind=f32),
            shape(256, 1024),
            shape(8, 64, 256),
            shape(8, 1024, kind=f32),
        ),
        in_specs=[wide, wide, wide, whole(8, 1024), wide, whole(1024, 1024)],
        out_specs=(wide, wide, whole(8, 64, 256), whole(8, 1024)),
        compiler_params=ALL,
        cost_estimate=takes(3),
        name="middle_back",
    )(*[far(x) for x in (middle, mine, swapped, vectors, grad_mlp, rest)])


def put_block(ref, at, block):
    for g in range(32):
        ref[16 * g : 16 * (g + 1), at : at + 128] = block


def merge_kernel(query_ref, own_ref, other_ref, out_ref):
    out_ref[:, :64, :] = query_ref[...]
    out_ref[:, 64:, :] = low(own_ref[...] + other_ref[...].astype(f32))


def final_kernel(
    lengths_ref, inputs_ref, middle_ref, mine_ref, swapped_ref, vectors_ref, out_ref, roots_ref, order_ref
):
    feature_order(order_ref)
    valid = valid_rows(lengths_ref)
    inputs = inputs_ref[...].astype(f32)
    middle = middle_ref[...]
    mlp_out = mine_ref[...].astype(f32) + swapped_ref[...].astype(f32) + vectors_ref[5:6, :]
    final = middle + mlp_out
    out_ref[...] = low(contract(low(final), order_ref[...], 1, 1))
    lane = lax.broadcasted_iota(jnp.int32, (1, 128), 1)
    total = jnp.zeros((1, 128), f32)
    for k, field in enumerate((inputs, middle - inputs, mlp_out, final)):
        total = jnp.where(lane == k, jnp.sum(valid * field * field), total)
    roots_ref[...] = total


def side_kernel(ga_ref, heads_ref, rows_ref, mine_ref, theirs_ref):
    for side, ref in ((0, mine_ref), (1, theirs_ref)):
        ref[:, :512] = low(contract(of_core(ga_ref, side).T, heads_ref[...], 1, 1))
        cols = jnp.concatenate([of_core(rows_ref, side), jnp.zeros((120, 512), f32)], axis=0)
        ref[:, 512:] = low(cols.T)


def grads_into(ref, normed, grads_ref, sums, rows):
    left = normed.T
    for c in range(3):
        cols = slice(512 * c, 512 * (c + 1))
        ref[:, cols] = low(contract(left, grads_ref[cols, :], 1, 1))
    put_block(ref, 1536, sums[0])
    put_block(ref, 1664, sums[1])
    cols = [jnp.zeros((4, 512), f32), rows[:2], jnp.zeros((122, 512), f32)]
    ref[:, 1792:] = low(jnp.concatenate(cols, axis=0).T)


def sum_rows(field, dim, count, extra):
    sums = contract(jnp.ones((8, 256), bf16), field, 1, dim)[0:1]
    sums = [sums[:, 128 * r : 128 * (r + 1)] for r in range(count)]
    return low(jnp.concatenate(sums + extra, axis=0))


def back_kernel(
    gback_ref,
    own_ref,
    other_ref,
    inputs_ref,
    other_n_ref,
    roots_ref,
    gh_ref,
    keep_ref,
    send_ref,
    rows_ref,
    theirs_ref,
    grads_ref,
    sums_ref,
    norm_ref,
    part_ref,
):
    for c in range(3):
        for h in range(8):
            at = 512 * c + 64 * h
            grads_ref[at : at + 64, :] = gback_ref[h, 64 * c : 64 * (c + 1), :]
    sides = [grads_ref[512 * c : 512 * (c + 1), :].T for c in range(3)]
    norm_ref[...], _ = norm_parts(inputs_ref[...].astype(f32))
    parts = []
    for side, ref in ((0, own_ref), (1, other_ref)):
        part = sum(contract(sides[c], ref[:, 512 * c : 512 * (c + 1)], 1, 1) for c in range(3))
        part = low(part)
        for x, lanes in enumerate(core_lanes(side)):
            part_ref[:, lanes] = part[:, 128 * x : 128 * (x + 1)]
        part = part.astype(f32)
        gain = jnp.sum(part * of_core(norm_ref, side), axis=0, keepdims=True)
        shift = jnp.sum(part, axis=0, keepdims=True)
        parts.append(jnp.concatenate([gain, shift, jnp.zeros((6, 512), f32)], axis=0))
    rows_ref[...] = parts[0]
    tp = lax.axis_index("tp")
    keep_ref[...] = part_ref[pl.ds(pl.multiple_of(tp * 128, 128), 128), :]
    send_ref[...] = part_ref[pl.ds(pl.multiple_of(128 - tp * 128, 128), 128), :]
    extra = [roots_ref[...], jnp.zeros((3, 128), f32)]
    sums_ref[0] = sum_rows(grads_ref[...], 1, 12, extra)
    sums_ref[1] = sum_rows(gh_ref[...], 0, 16, [])
    grads_into(theirs_ref, other_n_ref[...], grads_ref, sums_ref, parts[1])


def core_add_kernel(
    grads_ref, own_n_ref, sums_ref, b_ref, p_ref, q_ref, rows_ref, out_ref, left_ref
):
    i = pl.program_id(0)

    @pl.when(i == 0)
    def _():
        left_ref[...] = own_n_ref[...].T

    rows = pl.ds(pl.multiple_of(i * 128, 128), 128)
    for c in range(3):
        cols = slice(512 * c, 512 * (c + 1))
        mine = low(contract(left_ref[rows, :], grads_ref[cols, :], 1, 1)).astype(f32)
        out_ref[:, cols] = low(mine + b_ref[:, cols].astype(f32))
    for k in range(2):
        at = 1536 + 128 * k
        for g in range(8):
            theirs = b_ref[16 * g : 16 * (g + 1), at : at + 128].astype(f32)
            out_ref[16 * g : 16 * (g + 1), at : at + 128] = low(sums_ref[k].astype(f32) + theirs)
    side = p_ref[...].astype(f32) + q_ref[...].astype(f32)
    out_ref[:, 1792:2304] = low(side[:, :512])
    ln1 = jnp.concatenate([jnp.zeros((4, 128), f32), rows_ref[:2], jnp.zeros((122, 128), f32)], axis=0)
    both = low(ln1.T).astype(f32) + b_ref[:, 1792:].astype(f32)
    out_ref[:, 2304:] = low(side[:, 512:] + both)


def core_add(grads, own_n, sums, theirs, mine_p, theirs_p, rows):
    def tall(cols):
        return pl.BlockSpec((128, cols), lambda i: (i, 0))

    flat = pl.BlockSpec((8, 128), lambda i: (0, i))
    return pl.pallas_call(
        core_add_kernel,
        grid=(4,),
        out_shape=shape(512, 2432),
        in_specs=[
            block_of(grads),
            block_of(own_n),
            block_of(sums),
            tall(1920),
            tall(640),
            tall(640),
            flat,
        ],
        out_specs=tall(2432),
        scratch_shapes=[pltpu.VMEM((512, 256), bf16)],
        compiler_params=ALL,
        cost_estimate=takes(4),
        name="qkv_core_sum",
    )(*[far(x) for x in (grads, own_n, sums, theirs, mine_p, theirs_p, rows)])


def end_kernel(inputs_ref, gmid_ref, mine_ref, swapped_ref, vectors_ref, out_ref, order_ref):
    feature_order(order_ref)
    rows = pl.ds(pl.multiple_of(lax.axis_index("tp") * 128, 128), 128)
    norm, inverse = norm_parts(inputs_ref[rows, :].astype(f32))
    grad = mine_ref[...].astype(f32) + swapped_ref[...].astype(f32)
    grad = gmid_ref[rows, :] + norm_back(grad, vectors_ref[0:1, :], norm, inverse)
    out_ref[...] = low(contract(low(grad), order_ref[...], 1, 1))


def join_kernel(mine_ref, theirs_ref, out_ref):
    tp = lax.axis_index("tp")
    out_ref[pl.ds(pl.multiple_of(tp * 128, 128), 128), :] = mine_ref[...]
    out_ref[pl.ds(pl.multiple_of(128 - tp * 128, 128), 128), :] = theirs_ref[...]


def total_qkv_kernel(lengths_ref, got_ref, qkv_ref, proj_ref, bias_ref, fc_ref, roots_ref):
    total = got_ref[0].astype(f32)
    for k in range(1, 32):
        total = total + got_ref[k].astype(f32)
    for c in range(3):
        qkv_ref[c] = total[:, 512 * c : 512 * (c + 1)]
    for k in range(2):
        for r in range(4):
            row = 8 * k + r
            bias_ref[k : k + 1, 128 * r : 128 * (r + 1)] = total[row : row + 1, 1536:1664]
    count = lengths_ref[0] + lengths_ref[1] + lengths_ref[2] + lengths_ref[3]
    mean = total[12:13, 1536:1664] / (count.astype(f32) * 1024.0)
    roots_ref[...] = jnp.sqrt(mean + ROOT_EPS)
    fc_ref[...] = total[:, 1664:1792]
    proj_ref[...] = total[:, 1792:2304]


def total_cols_kernel(got_ref, cols_ref):
    total = got_ref[0].astype(f32)
    for k in range(1, 32):
        total = total + got_ref[k].astype(f32)
    cols_ref[...] = total.T[:8]


def total_cols(got):
    return pl.pallas_call(
        total_cols_kernel,
        grid=(1,),
        out_shape=shape(8, 16, kind=f32),
        in_specs=[pl.BlockSpec((32, 16, 128), lambda i: (0, 0, 18))],
        out_specs=pl.BlockSpec((8, 16), lambda i: (0, 0)),
        compiler_params=ROOMY,
        cost_estimate=takes(1),
        name="total_cols",
    )(got)


def total_wide_kernel(mine_ref, theirs_ref, fc_ref, out_ref):
    total = mine_ref[...].astype(f32) + theirs_ref[...].astype(f32)
    fc_ref[...] = total[:, :2048]
    out_ref[...] = total[:, 2048:]


def body(
    tokens,
    ln1_gain,
    ln1_bias,
    qkv_weight,
    qv_bias,
    proj_weight,
    proj_bias,
    ln2_gain,
    ln2_bias,
    fc_weight,
    fc_bias,
    out_weight,
    out_bias,
    piece_starts,
    seq_lengths,
    cotangent,
):
    vectors = (ln1_gain, ln1_bias, proj_bias, ln2_gain, ln2_bias, out_bias)
    pay_q = call(
        prepare_kernel,
        "weights_payload",
        shape(32, 16, 1664),
        qkv_weight,
        *[v.reshape(1, 16) for v in vectors],
    )
    own_q = exchange(pay_q, SPREAD).reshape(512, 1664)
    proj_rows = proj_weight.T
    pay_r = call(
        prepare_rest_kernel, "rest_payload", shape(16, 4608), proj_rows, fc_weight, out_weight.T
    )
    pair_r = call(
        pair_kernel,
        "rest_pair",
        shape(32, 5120),
        after(pay_r, pay_q),
        swap(pay_r, "zh"),
        swap(proj_rows, "tp"),
        lax.ppermute(proj_rows, ("zh", "tp"), [(i, 3 - i) for i in range(4)]),
    )
    rest = lax.all_gather(pair_r, ("x", "c", "y"), axis=0, tiled=True)

    inputs, grad_mlp = call(
        inputs_kernel,
        "inputs",
        (shape(256, 1024), shape(256, 1024)),
        seq_lengths,
        tokens[0],
        cotangent[0],
        scalars=1,
        cost=300,
        scratch=[pltpu.VMEM((1024, 1024), bf16)],
    )
    own_q = after(own_q, inputs)
    other_q = swap(own_q, "c")
    heads, own_n, other_n, vectors = call(
        qkv_kernel,
        "qkv",
        (shape(8, 192, 256), shape(256, 512), shape(256, 512), shape(8, 1024, kind=f32)),
        inputs,
        own_q,
        other_q,
        qv_bias,
        scratch=[pltpu.VMEM((256, 1024), bf16)],
        cost=3,
    )
    own = exchange(heads, LINE)
    other = swap(own[:, 64:], "c")
    attended, attended_low, log_sum = attn_forward(seq_lengths, piece_starts, own, other)
    heads_all = exchange(attended_low.reshape(16, 64, 256), ("zh", "y", "tp"))
    staged = attn_stage(own, other, log_sum)
    grad_act = grad_activated(grad_mlp, after(rest, attended_low))
    middle, normed_two, heads_out = attention_end(
        after(heads_all, staged[0], grad_act), rest, inputs, vectors
    )
    activated, grad_hidden, two_part = feed_forward(
        normed_two, grad_act, fc_bias.reshape(1, 2048), rest
    )
    two_swapped = swap(two_part, "tp")
    wide, mlp_part = wide_grads(normed_two, grad_hidden, grad_mlp, activated, rest)
    wide = lax.psum_scatter(
        after(wide, two_swapped), ("x", "c"), scatter_dimension=0, tiled=True
    )
    two_swapped = after(two_swapped, mlp_part)
    grad_middle, grad_attn, grad_heads, rows = middle_back(
        middle, two_part, two_swapped, vectors, grad_mlp, rest
    )
    grad_mine = exchange(grad_heads, LINE)

    mine_p, theirs_p = call(
        side_kernel,
        "proj_grads",
        (shape(512, 640), shape(512, 640)),
        far(grad_attn),
        far(heads_out),
        rows,
        cost=2,
    )
    grad_mine = after(grad_mine, mine_p)
    theirs_p = swap(after(theirs_p, grad_mine), "c")
    mlp_swapped = swap(after(mlp_part, grad_mine), "tp")

    grad_query, grad_own, grad_other = attn_backward(
        seq_lengths, piece_starts, staged, grad_mine, attended
    )
    grad_other, mlp_swapped = lax.optimization_barrier((grad_other, mlp_swapped))
    grad_back = call(
        merge_kernel, "merge", shape(8, 192, 256), grad_query, grad_own, swap(grad_other, "c")
    )
    grad_back = exchange(grad_back, LINE)
    layer_out, roots = call(
        final_kernel,
        "final",
        (shape(256, 1024), shape(1, 128, kind=f32)),
        seq_lengths,
        far(inputs),
        far(middle),
        after(mlp_part, grad_other),
        mlp_swapped,
        vectors,
        scalars=1,
        cost=3,
        scratch=[pltpu.VMEM((1024, 1024), bf16)],
    )
    one_keep, one_send, rows, theirs_q, grads, sums = call(
        back_kernel,
        "back",
        (
            shape(128, 1024),
            shape(128, 1024),
            shape(8, 512, kind=f32),
            shape(512, 1920),
            shape(1536, 256),
            shape(2, 16, 128),
        ),
        grad_back,
        far(own_q),
        far(other_q),
        far(inputs),
        far(other_n),
        roots,
        far(grad_hidden),
        cost=5,
        scratch=[pltpu.VMEM((256, 1024), f32), pltpu.VMEM((256, 1024), bf16)],
    )
    one_swapped = swap(one_send, "tp")
    wide = lax.psum_scatter(after(wide, roots), "y", scatter_dimension=0, tiled=True)
    both = core_add(
        grads,
        own_n,
        sums,
        after(swap(theirs_q, "c"), one_swapped),
        mine_p,
        theirs_p,
        rows,
    )
    got_q = exchange(both.reshape(32, 16, 2432), SPREAD)
    half_tokens = call(
        end_kernel,
        "end",
        shape(128, 1024),
        far(inputs),
        far(grad_middle),
        one_keep,
        one_swapped,
        vectors,
        cost=2,
        scratch=[pltpu.VMEM((1024, 1024), bf16)],
    )
    half_swapped = swap(half_tokens, "tp")
    zh = lax.axis_index("zh")
    keep = lax.dynamic_slice_in_dim(wide, zh * 16, 16, 0)
    send = lax.dynamic_slice_in_dim(wide, 16 - zh * 16, 16, 0)
    grad_fc, grad_out = call(
        total_wide_kernel,
        "total_wide",
        (shape(16, 2048, kind=f32), shape(16, 2048, kind=f32)),
        keep,
        swap(send, "zh"),        cost=14,
    )
    got_q = after(got_q, grad_fc, half_swapped)
    cols = total_cols(got_q)
    ln1 = cols[4:6]
    grad_qkv, grad_proj, bias_sums, fc_sums, roots = call(
        total_qkv_kernel,
        "total_qkv",
        (
            shape(3, 16, 512, kind=f32),
            shape(16, 512, kind=f32),
            shape(2, 512, kind=f32),
            shape(16, 128, kind=f32),
            shape(1, 128, kind=f32),
        ),
        seq_lengths,
        after(got_q, cols),
        scalars=1,
    )
    ln1_swapped = swap(ln1, "tp")
    half_swapped = after(half_swapped, grad_qkv)
    grad_tokens = call(
        join_kernel, "join", shape(256, 1024), half_tokens, half_swapped
    )
    ln1 = ln1 + ln1_swapped
    return (
        layer_out[None],
        grad_tokens[None],
        ln1[0],
        ln1[1],
        grad_qkv.transpose(1, 0, 2),
        bias_sums,
        grad_proj.T,
        cols[0],
        cols[1],
        cols[2],
        grad_fc,
        fc_sums.reshape(2048),
        grad_out.T,
        cols[3],
        roots[0, :4],
    )


def solution(mesh):
    fine = Mesh(mesh.devices.reshape(4, 2, 4, 2, 2), ("x", "zh", "y", "c", "tp"))
    ctx = ("zh", "y", "c")
    every = ("x", "zh", "y", "c")
    in_specs = (
        P("x", ctx, None),
        P(every),
        P(every),
        P(every, None, "tp"),
        P(None, "tp"),
        P("tp", every),
        P(every),
        P(every),
        P(every),
        P(every, "tp"),
        P("tp"),
        P("tp", every),
        P(every),
        P("x", None),
        P(),
        P("x", ctx, None),
    )
    out_specs = (
        P("x", ctx, None),
        P("x", ctx, None),
        P(every),
        P(every),
        P(every, None, "tp"),
        P(None, "tp"),
        P("tp", every),
        P(every),
        P(every),
        P(every),
        P(every, "tp"),
        P("tp"),
        P("tp", every),
        P(every),
        P(),
    )
    return jax.shard_map(body, mesh=fine, in_specs=in_specs, out_specs=out_specs, check_vma=False)
```

```python
from functools import partial

import jax
import jax.numpy as jnp
from jax import lax
from jax.experimental import pallas as pl
from jax.experimental.pallas import tpu as pltpu
from jax.sharding import Mesh
from jax.sharding import PartitionSpec as P

f32 = jnp.float32
bf16 = jnp.bfloat16
NORM_EPS = 1e-05
ROOT_EPS = 1e-06
B=256; E=64; NB=16; MASKED=-1e30; PIECE=256

class Facts:
    def __init__(self, lengths_ref, starts_ref):
        self.core = lax.axis_index("c")
        self.items = (self.core, lengths_ref[lax.axis_index("x")], starts_ref[0, 0], starts_ref[0, 1])

    def __getitem__(self, at):
        return self.items[at]


def piece_of(pos, info_ref):
    n0=(pos>=info_ref[2])&(pos<info_ref[2]+PIECE)
    n1=(pos>=info_ref[3])&(pos<info_ref[3]+PIECE)
    return jnp.where(n0,1,0)+jnp.where(n1,2,0)

def allowed_block(key_block, query_block, info_ref):
    kpos=key_block*B+lax.broadcasted_iota(jnp.int32,(B,1),0)
    qpos=query_block*B+lax.broadcasted_iota(jnp.int32,(1,B),1)
    kp=piece_of(kpos,info_ref); qp=piece_of(qpos,info_ref)
    qp=jnp.where(qp==0,-1,qp)
    kp=jnp.where(kpos<info_ref[1],kp,-2)
    kpos=jnp.where(kpos<info_ref[1],kpos,1<<20)
    return (kpos<=qpos)|(kp==qp)

def extra_blocks(p, info_ref):
    edge=(2*p+2)*B
    crosses=((info_ref[2]<edge)&(edge<info_ref[2]+PIECE))|((info_ref[3]<edge)&(edge<info_ref[3]+PIECE))
    return jnp.where((info_ref[0]==1)&(p<NB//2-1)&crosses,1,0)

def dot(a,b): return jnp.dot(a,b,preferred_element_type=f32)

SAFE = 60.0


def split3(row):
    top = row.astype(bf16).astype(f32)
    mid = (row - top).astype(bf16).astype(f32)
    rows = jnp.concatenate([top, mid, row - top - mid, jnp.zeros((13, row.shape[1]), f32)], axis=0)
    return rows.astype(bf16)


def ones_beside(block):
    lane = lax.broadcasted_iota(jnp.int32, (B, 16), 1)
    return jnp.concatenate([block, jnp.where(lane < 3, 1.0, 0.0).astype(bf16)], axis=1)


CHUNK = 4 * B


def pair_allowed(m, info_ref):
    key = m * CHUNK + lax.broadcasted_iota(jnp.int32, (CHUNK, 1), 0)
    lane = lax.broadcasted_iota(jnp.int32, (1, 2 * B), 1)
    query = (4 * m + info_ref[0]) * B + lane + jnp.where(lane >= B, B, 0)
    key_piece, query_piece = piece_of(key, info_ref), piece_of(query, info_ref)
    query_piece = jnp.where(query_piece == 0, -1, query_piece)
    valid = key < info_ref[1]
    key_piece = jnp.where(valid, key_piece, -2)
    key = jnp.where(valid, key, 1 << 20)
    return (key <= query) | (key_piece == query_piece)


def pair_of(ref, m):
    return jnp.concatenate([ref[2 * m], ref[2 * m + 1]], axis=1)


def walk(m, extra, step, beyond, carry):
    def chunk(i, c):
        return step(pl.multiple_of(i * CHUNK, CHUNK), None, c)

    carry = lax.fori_loop(0, m, chunk, carry)
    first = pl.multiple_of(m * CHUNK, CHUNK)
    carry = step(first, m, carry)
    second = lax.fori_loop(
        0, extra, lambda i, c: beyond(pl.multiple_of(first + CHUNK, B), c), carry[:, B:]
    )
    return carry[:, :B], second


def masked_from(e, first, count, masked, query_block, info_ref):
    if not masked:
        return e
    keep = count - masked * B
    parts = [e[:keep]] if keep else []
    for at in range(keep, count, B):
        allowed = allowed_block((first >> 8) + at // B, query_block, info_ref)
        parts.append(jnp.where(allowed, e[at : at + B], 0.0))
    return jnp.concatenate(parts, axis=0)


def place(block):
    return pl.ds(pl.multiple_of(block * B, B), B)


def walk_all(p, extra, step, carry, chunk):
    end = 2 * B * (p + 1)
    for first in range(0, end, chunk):
        last = min(first + chunk, end)
        carry = step(first, last - first, max(0, last - (end - 2 * B)) // B, carry)
    if p == NB // 2 - 1:
        return carry
    return lax.fori_loop(0, extra, lambda i, c: step(end, B, 1, c), carry)


def forward_kernel(lengths_ref, starts_ref, own_ref, other_ref, out_ref, low_ref, lse_ref, key_ref, value_ref):
    info_ref = Facts(lengths_ref, starts_ref)
    core = info_ref[0]
    sublane = lax.broadcasted_iota(jnp.int32, (16, NB * B), 0)
    value_ref[E:, :] = jnp.where(sublane == 0, 1.0, 0.0).astype(bf16)

    def squares(block):
        field = block.astype(f32)
        return jnp.sum(field * field, axis=0, keepdims=True)

    query_top = jnp.zeros((1, B), f32)
    key_top = jnp.zeros((1, B), f32)
    for p in range(NB // 2):
        mine, theirs = own_ref[p, E : 2 * E, :], other_ref[p, :E, :]
        here, there = place(2 * p + core), place(2 * p + 1 - core)
        key_ref[here, :] = mine.T
        key_ref[there, :] = theirs.T
        value_ref[:E, here] = own_ref[p, 2 * E :, :]
        value_ref[:E, there] = other_ref[p, E:, :]
        query_top = jnp.maximum(query_top, squares(own_ref[p, :E, :]))
        key_top = jnp.maximum(key_top, jnp.maximum(squares(mine), squares(theirs)))
    bound = jnp.max(query_top) * jnp.max(key_top)

    def finish(p, top, acc):
        total = acc[E : E + 1]
        o = acc[:E] / total
        out_ref[p] = o
        low_ref[p, 0] = o.astype(bf16)
        low_ref[p, 1] = o.astype(bf16)
        lse_ref[p] = top + jnp.log(total)

    @pl.when(bound <= (8.0 * SAFE) ** 2)
    def _():
        def both(m, _):
            query = pair_of(own_ref.at[:, :E, :], m) * jnp.asarray(0.125, bf16)

            def step(first, masked, acc):
                at = pl.ds(first, CHUNK)
                e = jnp.exp(dot(key_ref[at, :], query))
                if masked is not None:
                    e = jnp.where(pair_allowed(masked, info_ref), e, 0.0)
                return acc + dot(value_ref[:, at], e.astype(bf16))

            def beyond(first, acc):
                at = pl.ds(first, B)
                e = jnp.exp(dot(key_ref[at, :], query[:, B:]))
                e = jnp.where(allowed_block(4 * m + 4, 4 * m + 2 + core, info_ref), e, 0.0)
                return acc + dot(value_ref[:, at], e.astype(bf16))

            accs = walk(
                m, extra_blocks(2 * m + 1, info_ref), step, beyond, jnp.zeros((E + 16, 2 * B), f32)
            )
            for odd in range(2):
                finish(2 * m + odd, 0.0, accs[odd])
            return 0

        lax.fori_loop(0, NB // 4, both, 0)

    @pl.when(bound > (8.0 * SAFE) ** 2)
    def _():
        def one(p, _):
            query = own_ref[p, :E, :] * jnp.asarray(0.125, bf16)
            qb = 2 * p + core

            def step(blocks, masked, carry):
                top, acc = carry
                scores = [dot(key_ref[place(j), :], query) for j in blocks]
                if masked:
                    scores = [
                        jnp.where(allowed_block(j, qb, info_ref), s, MASKED)
                        for j, s in zip(blocks, scores)
                    ]
                new = top
                for s in scores:
                    new = jnp.maximum(new, jnp.max(s, axis=0, keepdims=True))
                acc = acc * jnp.exp(top - new)
                for j, s in zip(blocks, scores):
                    acc = acc + dot(value_ref[:, place(j)], jnp.exp(s - new).astype(bf16))
                return new, acc

            carry = (jnp.full((1, B), MASKED, f32), jnp.zeros((E + 16, B), f32))
            carry = step((2 * p, 2 * p + 1), True, carry)
            carry = lax.fori_loop(0, p, lambda i, c: step((2 * i, 2 * i + 1), False, c), carry)
            carry = lax.fori_loop(
                0, extra_blocks(p, info_ref), lambda i, c: step((2 * p + 2,), True, c), carry
            )
            finish(p, *carry)
            return 0

        lax.fori_loop(0, NB // 2, one, 0)


def stage_kernel(own_ref, other_ref, lse_ref, key_ref, keyt_ref, value_ref, query_ref, rows_ref):
    core = lax.axis_index("c")
    blank = jnp.zeros((B, E), bf16)
    for p in range(NB // 2):
        mine, theirs = own_ref[p, E : 2 * E, :], other_ref[p, :E, :]
        here, there = place(2 * p + core), place(2 * p + 1 - core)
        keyt_ref[:, here] = mine
        keyt_ref[:, there] = theirs
        key_ref[here, :] = ones_beside(mine.T)
        key_ref[there, :] = ones_beside(theirs.T)
        value_ref[here, :] = ones_beside(own_ref[p, 2 * E :, :].T)
        value_ref[there, :] = ones_beside(other_ref[p, E:, :].T)
        query = own_ref[p, :E, :] * jnp.asarray(0.125, bf16)
        query_ref[p, :E, :] = query
        query_ref[p, E:, :] = split3(-lse_ref[p])
        rows_ref[p] = jnp.concatenate([blank, query.T], axis=1)


def backward_kernel(
    lengths_ref,
    starts_ref,
    key_ref,
    keyt_ref,
    value_ref,
    query_ref,
    rows_ref,
    gout_ref,
    out_ref,
    gq_ref,
    gown_ref,
    gother_ref,
    grad_ref,
    gouts_ref,
    grows_ref,
    sum_ref,
):
    info_ref = Facts(lengths_ref, starts_ref)
    core = info_ref[0]
    grad_ref[...] = jnp.zeros_like(grad_ref)
    blank = jnp.zeros((B, E), bf16)
    for p in range(NB // 2):
        gout = gout_ref[p]
        delta = jnp.sum(gout.astype(f32) * out_ref[p], axis=0, keepdims=True)
        gouts_ref[p, :E, :] = gout
        gouts_ref[p, E:, :] = split3(-delta)
        grows_ref[p] = jnp.concatenate([gout.T, blank], axis=1)
    sum_ref[...] = jnp.zeros_like(sum_ref)

    def chunk(p, first, count, masked):
        at = pl.ds(pl.multiple_of(first, B), count)
        e = jnp.exp(dot(key_ref[at, :], query_ref[p]))
        if masked:
            e = masked_from(e, first, count, masked, 2 * p + core, info_ref)
        gs = (e * dot(value_ref[at, :], gouts_ref[p])).astype(bf16)
        grad_ref[at, :] += dot(e.astype(bf16), grows_ref[p]) + dot(gs, rows_ref[p])
        sum_ref[p] += dot(keyt_ref[:, at], gs)

    def both(m, _):
        top = NB // 2 - 1 - m
        for k in range(NB // 2 - 1):
            late = k < top
            chunk(jnp.where(late, top, m), 2 * B * jnp.where(late, k, k - top), 2 * B, 0)
        chunk(top, 2 * B * top, 2 * B, 2)
        chunk(m, 2 * B * m, 2 * B, 2)
        return 0

    lax.fori_loop(0, NB // 4, both, 0)

    def beyond(p, _):
        def add(i, _):
            chunk(p, 2 * B * (p + 1), B, 1)
            return 0

        return lax.fori_loop(0, extra_blocks(p, info_ref), add, 0)

    lax.fori_loop(0, NB // 2 - 1, beyond, 0)
    for p in range(NB // 2):
        gq_ref[p] = (sum_ref[p] * 0.125).astype(bf16)
    for p in range(NB // 2):
        mine = grad_ref[place(2 * p + core), :].T
        theirs = grad_ref[place(2 * p + 1 - core), :].T.astype(bf16)
        gown_ref[p, :E, :] = mine[E:]
        gown_ref[p, E:, :] = mine[:E]
        gother_ref[p, :E, :] = theirs[E:]
        gother_ref[p, E:, :] = theirs[:E]


VM=pl.BlockSpec(memory_space=pltpu.VMEM); SM=pl.BlockSpec(memory_space=pltpu.SMEM)
LIMIT=40*1024*1024
def attn_forward(lengths,starts,own,other):
    H=NB//2
    return pl.pallas_call(forward_kernel,
        out_shape=(jax.ShapeDtypeStruct((H,E,B),f32),jax.ShapeDtypeStruct((H,2,E,B),bf16),jax.ShapeDtypeStruct((H,1,B),f32)),
        in_specs=[SM,SM,VM,VM],out_specs=(VM,VM,VM),
        scratch_shapes=[pltpu.VMEM((NB*B,E),bf16),pltpu.VMEM((E+16,NB*B),bf16)],
        compiler_params=pltpu.CompilerParams(vmem_limit_bytes=LIMIT),
        cost_estimate=takes(8),
        name="attention_forward")(lengths,starts,own,other)
def attn_stage(own, other, lse):
    half = NB // 2
    outs = (
        jax.ShapeDtypeStruct((NB * B, E + 16), bf16),
        jax.ShapeDtypeStruct((E, NB * B), bf16),
        jax.ShapeDtypeStruct((NB * B, E + 16), bf16),
        jax.ShapeDtypeStruct((half, E + 16, B), bf16),
        jax.ShapeDtypeStruct((half, B, 2 * E), bf16),
    )
    return pl.pallas_call(
        stage_kernel,
        out_shape=outs,
        in_specs=[VM] * 3,
        out_specs=(VM,) * 5,
        compiler_params=pltpu.CompilerParams(vmem_limit_bytes=LIMIT),
        cost_estimate=takes(1),
        name="attention_stage",
    )(own, other, lse)


def attn_backward(lengths, starts, staged, gout, out):
    half = NB // 2

    def full(array):
        return pl.BlockSpec(array.shape, lambda i: (0,) * len(array.shape))

    outs = (
        jax.ShapeDtypeStruct((half, E, B), bf16),
        jax.ShapeDtypeStruct((half, 2 * E, B), f32),
        jax.ShapeDtypeStruct((half, 2 * E, B), bf16),
    )
    return pl.pallas_call(
        backward_kernel,
        grid=(1,),
        out_shape=outs,
        in_specs=[SM, SM] + [full(x) for x in (*staged, gout, out)],
        out_specs=tuple(full(x) for x in outs),
        scratch_shapes=[
            pltpu.VMEM((NB * B, 2 * E), f32),
            pltpu.VMEM((half, E + 16, B), bf16),
            pltpu.VMEM((half, B, 2 * E), bf16),
            pltpu.VMEM((half, E, B), f32),
        ],
        compiler_params=pltpu.CompilerParams(vmem_limit_bytes=LIMIT),
        cost_estimate=takes(26),
        name="attention_backward",
    )(lengths, starts, *[far(x) for x in staged], gout, far(out))


SPREAD = ("x", "y", "zh")
LINE = ("zh", "y")
VM = pl.BlockSpec(memory_space=pltpu.VMEM)
SM = pl.BlockSpec(memory_space=pltpu.SMEM)
ANY = pl.BlockSpec(memory_space=pl.ANY)
ROOMY = pltpu.CompilerParams(vmem_limit_bytes=40 * 1024 * 1024)
WHOLE = pltpu.CompilerParams(vmem_limit_bytes=50 * 1024 * 1024)
ALL = pltpu.CompilerParams(vmem_limit_bytes=62 * 1024 * 1024)


def takes(microseconds):
    return pl.CostEstimate(
        flops=int(microseconds * 1.15e9), bytes_accessed=1 << 20, transcendentals=0
    )


def low(field):
    return field.astype(bf16)


def swap(field, axis):
    return lax.ppermute(field, axis, [(0, 1), (1, 0)])


def exchange(field, axes):
    return lax.all_to_all(field, axes, split_axis=0, concat_axis=0, tiled=True)


def after(field, *others):
    return lax.optimization_barrier((field, *others))[0]


def contract(a, b, dim_a, dim_b):
    return lax.dot_general(a, b, (((dim_a,), (dim_b,)), ((), ())), preferred_element_type=f32)


def shape(*dims, kind=bf16):
    return jax.ShapeDtypeStruct(dims, kind)


def far(field):
    return pltpu.with_memory_space_constraint(field, pltpu.HBM)


def block_of(array):
    dims = len(array.shape)
    return pl.BlockSpec(array.shape, lambda *_: (0,) * dims)


def call(kernel, name, outs, *args, scalars=0, cost=1, scratch=(), memory=ROOMY):
    return pl.pallas_call(
        kernel,
        grid=(1,),
        out_shape=outs,
        in_specs=[SM] * scalars + [block_of(a) for a in args[scalars:]],
        out_specs=jax.tree.map(block_of, outs),
        scratch_shapes=list(scratch),
        compiler_params=memory,
        cost_estimate=takes(cost),
        name=name,
    )(*args)


def feature_order(order_ref):
    place = lax.broadcasted_iota(jnp.int32, (1, 1024), 1)
    x, core, y, zh = place >> 8, (place >> 7) & 1, (place >> 5) & 3, (place >> 4) & 1
    feature = ((((x * 2 + zh) * 4 + y) * 2 + core) << 4) + (place & 15)
    for at in range(0, 1024, 256):
        rows = at + lax.broadcasted_iota(jnp.int32, (256, 1024), 0)
        order_ref[at : at + 256, :] = jnp.where(rows == feature, 1.0, 0.0).astype(bf16)


def core_lanes(side):
    core = lax.axis_index("c") ^ side
    return [pl.ds(pl.multiple_of(256 * x + 128 * core, 128), 128) for x in range(4)]


def of_core(ref, side):
    return jnp.concatenate([ref[:, lanes] for lanes in core_lanes(side)], axis=1)


def valid_rows(lengths_ref):
    ctx = (lax.axis_index("zh") * 4 + lax.axis_index("y")) * 2 + lax.axis_index("c")
    position = ctx * 256 + lax.broadcasted_iota(jnp.int32, (256, 1), 0)
    return jnp.where(position < lengths_ref[lax.axis_index("x")], 1.0, 0.0)


def norm_parts(values):
    center = values - jnp.mean(values, axis=-1, keepdims=True)
    inverse = lax.rsqrt(jnp.mean(center * center, axis=-1, keepdims=True) + NORM_EPS)
    return center * inverse, inverse


def norm_back(grad, gain, norm, inverse):
    scaled = grad * gain
    return inverse * (
        scaled
        - jnp.mean(scaled, axis=-1, keepdims=True)
        - norm * jnp.mean(scaled * norm, axis=-1, keepdims=True)
    )


def gelu_pair(u):
    k = 0.7978845608028654
    square = u * u
    t = jnp.tanh(u * (k + (k * 0.044715) * square))
    half = 0.5 + 0.5 * t
    value = u * half
    slope = half + (0.5 * u) * (1.0 - t * t) * (k + (3 * 0.044715 * k) * square)
    return value, slope


def prepare_kernel(qkv_ref, a_ref, b_ref, c_ref, d_ref, e_ref, g_ref, out_ref):
    rows = [r[...].astype(f32) for r in (a_ref, b_ref, c_ref, d_ref, e_ref, g_ref)]
    small = jnp.concatenate(rows + [jnp.zeros((2, 16), f32)], axis=0).T
    small = low(jnp.concatenate([small, jnp.zeros((16, 120), f32)], axis=1))

    def one(k, _):
        for c in range(3):
            out_ref[k, :, 512 * c : 512 * (c + 1)] = qkv_ref[c]
        out_ref[k, :, 1536:] = small
        return 0

    lax.fori_loop(0, 32, one, 0)


def prepare_rest_kernel(proj_ref, fc_ref, out_ref, rest_ref):
    rest_ref[:, :512] = proj_ref[...]
    rest_ref[:, 512:2560] = fc_ref[...]
    rest_ref[:, 2560:] = out_ref[...]


def pair_kernel(mine_ref, by_zh_ref, by_tp_ref, by_both_ref, out_ref):
    zh, tp = lax.axis_index("zh"), lax.axis_index("tp")
    here = pl.ds(pl.multiple_of(zh * 16, 16), 16)
    there = pl.ds(pl.multiple_of(16 - zh * 16, 16), 16)
    near = pl.ds(pl.multiple_of(tp * 512, 512), 512)
    far_off = pl.ds(pl.multiple_of(512 - tp * 512, 512), 512)
    for rows, ref, other_ref in ((here, mine_ref, by_tp_ref), (there, by_zh_ref, by_both_ref)):
        out_ref[rows, near] = ref[:, :512]
        out_ref[rows, far_off] = other_ref[...]
        out_ref[rows, 1024:] = ref[:, 512:]


def inputs_kernel(lengths_ref, tokens_ref, cotangent_ref, inputs_ref, grad_ref, order_ref):
    feature_order(order_ref)
    inputs_ref[...] = low(dot(tokens_ref[...], order_ref[...]))
    grad = dot(cotangent_ref[...], order_ref[...]) * valid_rows(lengths_ref)
    grad_ref[...] = low(grad)


def qkv_kernel(
    inputs_ref, own_ref, other_ref, bias_ref, heads_ref, own_n_ref, other_n_ref, vectors_ref, normed_ref
):
    for side, ref in ((0, own_ref), (1, other_ref)):
        small = ref[:, 1536:].astype(f32).T[:8]
        for x, lanes in enumerate(core_lanes(side)):
            vectors_ref[:, lanes] = small[:, 128 * x : 128 * (x + 1)]
    norm, _ = norm_parts(inputs_ref[...].astype(f32))
    normed_ref[...] = low(norm * vectors_ref[0:1, :] + vectors_ref[1:2, :])
    own_n_ref[...] = of_core(normed_ref, 0)
    other_n_ref[...] = of_core(normed_ref, 1)
    for c in range(3):
        cols = slice(512 * c, 512 * (c + 1))
        field = dot(own_n_ref[...], own_ref[:, cols]) + dot(other_n_ref[...], other_ref[:, cols])
        if c != 1:
            field = field + bias_ref[c // 2 : c // 2 + 1, :].astype(f32)
        field = low(field).T
        for h in range(8):
            heads_ref[h, 64 * c : 64 * (c + 1), :] = field[64 * h : 64 * (h + 1)]


def attn_end_kernel(heads_ref, weight_ref, inputs_ref, vectors_ref, middle_ref, n_ref, own_ref, wide_ref):
    tp = lax.axis_index("tp")
    for h in range(8):
        for t in range(2):
            at = 512 * t + 64 * h
            wide_ref[at : at + 64, :] = heads_ref[2 * h + t]
        own_ref[64 * h : 64 * (h + 1), :] = heads_ref[2 * h + tp]
    attn_out = contract(wide_ref[...].T, weight_ref[...], 1, 1) + vectors_ref[2:3, :]
    middle = inputs_ref[...].astype(f32) + attn_out
    middle_ref[...] = middle
    norm, _ = norm_parts(middle)
    n_ref[...] = low(norm * vectors_ref[3:4, :] + vectors_ref[4:5, :])


def attention_end(heads_all, rest, inputs, vectors):
    wide = pl.BlockSpec((256, 1024), lambda i: (0, 0))
    return pl.pallas_call(
        attn_end_kernel,
        grid=(1,),
        out_shape=(shape(256, 1024, kind=f32), shape(256, 1024), shape(512, 256)),
        in_specs=[
            pl.BlockSpec((16, 64, 256), lambda i: (0, 0, 0)),
            pl.BlockSpec((1024, 1024), lambda i: (0, 0)),
            wide,
            pl.BlockSpec((8, 1024), lambda i: (0, 0)),
        ],
        out_specs=(wide, wide, pl.BlockSpec((512, 256), lambda i: (0, 0))),
        scratch_shapes=[pltpu.VMEM((1024, 256), bf16)],
        compiler_params=ROOMY,
        cost_estimate=takes(3),
        name="attn_end",
    )(heads_all, far(rest), far(inputs), far(vectors))


def grad_act_kernel(gm_ref, weight_ref, out_ref):
    out_ref[...] = dot(gm_ref[...], weight_ref[...])


def grad_activated(grad_mlp, rest):
    return pl.pallas_call(
        grad_act_kernel,
        grid=(4,),
        out_shape=shape(256, 2048, kind=f32),
        in_specs=[
            pl.BlockSpec((256, 1024), lambda i: (0, 0)),
            pl.BlockSpec((1024, 512), lambda i: (0, 6 + i)),
        ],
        out_specs=pl.BlockSpec((256, 512), lambda i: (0, i)),
        compiler_params=ROOMY,
        cost_estimate=takes(3),
        name="grad_act",
    )(far(grad_mlp), far(rest))


def feed_kernel(n_ref, gact_ref, bias_ref, weight_ref, act_ref, gh_ref, part_ref, total_ref):
    i = pl.program_id(0)

    @pl.when(i == 0)
    def _():
        total_ref[...] = jnp.zeros_like(total_ref)

    halves = [slice(at, at + 256) for at in range(0, 1024, 256)]
    hidden = [
        dot(n_ref[...], weight_ref[:, cols]) + bias_ref[:, cols].astype(f32) for cols in halves
    ]
    for cols, field in zip(halves, hidden):
        value, slope = gelu_pair(field)
        act_ref[:, cols] = low(value)
        gh_ref[:, cols] = low(gact_ref[:, cols] * slope)
    total_ref[...] += contract(gh_ref[...], weight_ref[...], 1, 1)

    @pl.when(i == 1)
    def _():
        part_ref[...] = low(total_ref[...])


def feed_forward(normed_two, grad_act, fc_bias, rest):
    def tile(rows, first):
        return pl.BlockSpec((rows, 1024), lambda i: (0, first + i))

    wide = pl.BlockSpec((256, 1024), lambda i: (0, 0))
    return pl.pallas_call(
        feed_kernel,
        grid=(2,),
        out_shape=(shape(256, 2048), shape(256, 2048), shape(256, 1024)),
        in_specs=[wide, tile(256, 0), tile(1, 0), tile(1024, 1)],
        out_specs=(tile(256, 0), tile(256, 0), wide),
        scratch_shapes=[pltpu.VMEM((256, 1024), f32)],
        compiler_params=ROOMY,
        cost_estimate=takes(6),
        name="feed_forward",
    )(normed_two, grad_act, fc_bias, far(rest))


def wide_kernel(n_ref, gh_ref, gm_ref, act_ref, weight_ref, out_ref, part_ref, left_ref, total_ref):
    i = pl.program_id(0)

    @pl.when(i == 0)
    def _():
        left_ref[0] = n_ref[...].T
        left_ref[1] = gm_ref[...].T
        total_ref[...] = jnp.zeros_like(total_ref)

    @pl.when(i < 4)
    def _():
        out_ref[...] = low(dot(left_ref[0], gh_ref[...]))

    @pl.when(i >= 4)
    def _():
        out_ref[...] = low(dot(left_ref[1], act_ref[...]))
        total_ref[...] += contract(act_ref[...], weight_ref[...], 1, 1)

    @pl.when(i == 7)
    def _():
        part_ref[...] = low(total_ref[...])


def wide_grads(normed_two, grad_hidden, grad_mlp, activated, rest):
    whole = pl.BlockSpec((256, 1024), lambda i: (0, 0))
    return pl.pallas_call(
        wide_kernel,
        grid=(8,),
        out_shape=(shape(1024, 4096), shape(256, 1024)),
        in_specs=[
            whole,
            pl.BlockSpec((256, 512), lambda i: (0, jnp.minimum(i, 3))),
            whole,
            pl.BlockSpec((256, 512), lambda i: (0, jnp.maximum(i - 4, 0))),
            pl.BlockSpec((1024, 512), lambda i: (0, 6 + jnp.maximum(i - 4, 0))),
        ],
        out_specs=(pl.BlockSpec((1024, 512), lambda i: (0, i)), whole),
        scratch_shapes=[pltpu.VMEM((2, 1024, 256), bf16), pltpu.VMEM((256, 1024), f32)],
        compiler_params=WHOLE,
        cost_estimate=takes(8),
        name="wide_grads",
    )(normed_two, grad_hidden, far(grad_mlp), activated, far(rest))


def middle_back_kernel(
    middle_ref, mine_ref, swapped_ref, vectors_ref, gm_ref, weight_ref, out_ref, ga_ref, gheads_ref, cols_ref
):
    gm = gm_ref[...].astype(f32)
    norm, inverse = norm_parts(middle_ref[...])
    grad = mine_ref[...].astype(f32) + swapped_ref[...].astype(f32)
    out = gm + norm_back(grad, vectors_ref[3:4, :], norm, inverse)
    out_ref[...] = out
    low_out = low(out)
    ga_ref[...] = low_out
    tp = lax.axis_index("tp")
    field = low(dot(low_out, weight_ref[:, pl.ds(pl.multiple_of(tp * 512, 512), 512)])).T
    for h in range(8):
        gheads_ref[h] = field[64 * h : 64 * (h + 1)]
    rows = [low_out.astype(f32), grad * norm, grad, gm]
    rows = [jnp.sum(r, axis=0, keepdims=True) for r in rows]
    cols_ref[...] = jnp.concatenate(rows + [jnp.zeros((4, 1024), f32)], axis=0)


def middle_back(middle, mine, swapped, vectors, grad_mlp, rest):
    def whole(*dims):
        return pl.BlockSpec(dims, lambda i: (0,) * len(dims))

    wide = whole(256, 1024)
    return pl.pallas_call(
        middle_back_kernel,
        grid=(1,),
        out_shape=(
            shape(256, 1024, kind=f32),
            shape(256, 1024),
            shape(8, 64, 256),
            shape(8, 1024, kind=f32),
        ),
        in_specs=[wide, wide, wide, whole(8, 1024), wide, whole(1024, 1024)],
        out_specs=(wide, wide, whole(8, 64, 256), whole(8, 1024)),
        compiler_params=ALL,
        cost_estimate=takes(3),
        name="middle_back",
    )(*[far(x) for x in (middle, mine, swapped, vectors, grad_mlp, rest)])


def put_block(ref, at, block):
    for g in range(32):
        ref[16 * g : 16 * (g + 1), at : at + 128] = block


def merge_kernel(query_ref, own_ref, other_ref, out_ref):
    out_ref[:, :64, :] = query_ref[...]
    out_ref[:, 64:, :] = low(own_ref[...] + other_ref[...].astype(f32))


def final_kernel(
    lengths_ref, inputs_ref, middle_ref, mine_ref, swapped_ref, vectors_ref, out_ref, roots_ref, order_ref
):
    feature_order(order_ref)
    valid = valid_rows(lengths_ref)
    inputs = inputs_ref[...].astype(f32)
    middle = middle_ref[...]
    mlp_out = mine_ref[...].astype(f32) + swapped_ref[...].astype(f32) + vectors_ref[5:6, :]
    final = middle + mlp_out
    out_ref[...] = low(contract(low(final), order_ref[...], 1, 1))
    lane = lax.broadcasted_iota(jnp.int32, (1, 128), 1)
    total = jnp.zeros((1, 128), f32)
    for k, field in enumerate((inputs, middle - inputs, mlp_out, final)):
        total = jnp.where(lane == k, jnp.sum(valid * field * field), total)
    roots_ref[...] = total


def side_kernel(ga_ref, heads_ref, rows_ref, mine_ref, theirs_ref):
    for side, ref in ((0, mine_ref), (1, theirs_ref)):
        ref[:, :512] = low(contract(of_core(ga_ref, side).T, heads_ref[...], 1, 1))
        cols = jnp.concatenate([of_core(rows_ref, side), jnp.zeros((120, 512), f32)], axis=0)
        ref[:, 512:] = low(cols.T)


def grads_into(ref, normed, grads_ref, sums, rows):
    left = normed.T
    for c in range(3):
        cols = slice(512 * c, 512 * (c + 1))
        ref[:, cols] = low(contract(left, grads_ref[cols, :], 1, 1))
    put_block(ref, 1536, sums[0])
    put_block(ref, 1664, sums[1])
    cols = [jnp.zeros((4, 512), f32), rows[:2], jnp.zeros((122, 512), f32)]
    ref[:, 1792:] = low(jnp.concatenate(cols, axis=0).T)


def sum_rows(field, dim, count, extra):
    sums = contract(jnp.ones((8, 256), bf16), field, 1, dim)[0:1]
    sums = [sums[:, 128 * r : 128 * (r + 1)] for r in range(count)]
    return low(jnp.concatenate(sums + extra, axis=0))


def back_kernel(
    gback_ref,
    own_ref,
    other_ref,
    inputs_ref,
    other_n_ref,
    roots_ref,
    gh_ref,
    keep_ref,
    send_ref,
    rows_ref,
    theirs_ref,
    grads_ref,
    sums_ref,
    norm_ref,
    part_ref,
):
    for c in range(3):
        for h in range(8):
            at = 512 * c + 64 * h
            grads_ref[at : at + 64, :] = gback_ref[h, 64 * c : 64 * (c + 1), :]
    sides = [grads_ref[512 * c : 512 * (c + 1), :].T for c in range(3)]
    norm_ref[...], _ = norm_parts(inputs_ref[...].astype(f32))
    parts = []
    for side, ref in ((0, own_ref), (1, other_ref)):
        part = sum(contract(sides[c], ref[:, 512 * c : 512 * (c + 1)], 1, 1) for c in range(3))
        part = low(part)
        for x, lanes in enumerate(core_lanes(side)):
            part_ref[:, lanes] = part[:, 128 * x : 128 * (x + 1)]
        part = part.astype(f32)
        gain = jnp.sum(part * of_core(norm_ref, side), axis=0, keepdims=True)
        shift = jnp.sum(part, axis=0, keepdims=True)
        parts.append(jnp.concatenate([gain, shift, jnp.zeros((6, 512), f32)], axis=0))
    rows_ref[...] = parts[0]
    tp = lax.axis_index("tp")
    keep_ref[...] = part_ref[pl.ds(pl.multiple_of(tp * 128, 128), 128), :]
    send_ref[...] = part_ref[pl.ds(pl.multiple_of(128 - tp * 128, 128), 128), :]
    extra = [roots_ref[...], jnp.zeros((3, 128), f32)]
    sums_ref[0] = sum_rows(grads_ref[...], 1, 12, extra)
    sums_ref[1] = sum_rows(gh_ref[...], 0, 16, [])
    grads_into(theirs_ref, other_n_ref[...], grads_ref, sums_ref, parts[1])


def core_add_kernel(
    grads_ref, own_n_ref, sums_ref, b_ref, p_ref, q_ref, rows_ref, out_ref, left_ref
):
    i = pl.program_id(0)

    @pl.when(i == 0)
    def _():
        left_ref[...] = own_n_ref[...].T

    rows = pl.ds(pl.multiple_of(i * 128, 128), 128)
    for c in range(3):
        cols = slice(512 * c, 512 * (c + 1))
        mine = low(contract(left_ref[rows, :], grads_ref[cols, :], 1, 1)).astype(f32)
        out_ref[:, cols] = low(mine + b_ref[:, cols].astype(f32))
    for k in range(2):
        at = 1536 + 128 * k
        for g in range(8):
            theirs = b_ref[16 * g : 16 * (g + 1), at : at + 128].astype(f32)
            out_ref[16 * g : 16 * (g + 1), at : at + 128] = low(sums_ref[k].astype(f32) + theirs)
    side = p_ref[...].astype(f32) + q_ref[...].astype(f32)
    out_ref[:, 1792:2304] = low(side[:, :512])
    ln1 = jnp.concatenate([jnp.zeros((4, 128), f32), rows_ref[:2], jnp.zeros((122, 128), f32)], axis=0)
    both = low(ln1.T).astype(f32) + b_ref[:, 1792:].astype(f32)
    out_ref[:, 2304:] = low(side[:, 512:] + both)


def core_add(grads, own_n, sums, theirs, mine_p, theirs_p, rows):
    def tall(cols):
        return pl.BlockSpec((128, cols), lambda i: (i, 0))

    flat = pl.BlockSpec((8, 128), lambda i: (0, i))
    return pl.pallas_call(
        core_add_kernel,
        grid=(4,),
        out_shape=shape(512, 2432),
        in_specs=[
            block_of(grads),
            block_of(own_n),
            block_of(sums),
            tall(1920),
            tall(640),
            tall(640),
            flat,
        ],
        out_specs=tall(2432),
        scratch_shapes=[pltpu.VMEM((512, 256), bf16)],
        compiler_params=ALL,
        cost_estimate=takes(4),
        name="qkv_core_sum",
    )(*[far(x) for x in (grads, own_n, sums, theirs, mine_p, theirs_p, rows)])


def end_kernel(inputs_ref, gmid_ref, mine_ref, swapped_ref, vectors_ref, out_ref, order_ref):
    feature_order(order_ref)
    rows = pl.ds(pl.multiple_of(lax.axis_index("tp") * 128, 128), 128)
    norm, inverse = norm_parts(inputs_ref[rows, :].astype(f32))
    grad = mine_ref[...].astype(f32) + swapped_ref[...].astype(f32)
    grad = gmid_ref[rows, :] + norm_back(grad, vectors_ref[0:1, :], norm, inverse)
    out_ref[...] = low(contract(low(grad), order_ref[...], 1, 1))


def join_kernel(mine_ref, theirs_ref, out_ref):
    tp = lax.axis_index("tp")
    out_ref[pl.ds(pl.multiple_of(tp * 128, 128), 128), :] = mine_ref[...]
    out_ref[pl.ds(pl.multiple_of(128 - tp * 128, 128), 128), :] = theirs_ref[...]


def total_qkv_kernel(lengths_ref, got_ref, qkv_ref, proj_ref, bias_ref, fc_ref, roots_ref):
    total = got_ref[0].astype(f32)
    for k in range(1, 32):
        total = total + got_ref[k].astype(f32)
    for c in range(3):
        qkv_ref[c] = total[:, 512 * c : 512 * (c + 1)]
    for k in range(2):
        for r in range(4):
            row = 8 * k + r
            bias_ref[k : k + 1, 128 * r : 128 * (r + 1)] = total[row : row + 1, 1536:1664]
    count = lengths_ref[0] + lengths_ref[1] + lengths_ref[2] + lengths_ref[3]
    mean = total[12:13, 1536:1664] / (count.astype(f32) * 1024.0)
    roots_ref[...] = jnp.sqrt(mean + ROOT_EPS)
    fc_ref[...] = total[:, 1664:1792]
    proj_ref[...] = total[:, 1792:2304]


def total_cols_kernel(got_ref, cols_ref):
    total = got_ref[0].astype(f32)
    for k in range(1, 32):
        total = total + got_ref[k].astype(f32)
    cols_ref[...] = total.T[:8]


def total_cols(got):
    return pl.pallas_call(
        total_cols_kernel,
        grid=(1,),
        out_shape=shape(8, 16, kind=f32),
        in_specs=[pl.BlockSpec((32, 16, 128), lambda i: (0, 0, 18))],
        out_specs=pl.BlockSpec((8, 16), lambda i: (0, 0)),
        compiler_params=ROOMY,
        cost_estimate=takes(1),
        name="total_cols",
    )(got)


def total_wide_kernel(mine_ref, theirs_ref, fc_ref, out_ref):
    total = mine_ref[...].astype(f32) + theirs_ref[...].astype(f32)
    fc_ref[...] = total[:, :2048]
    out_ref[...] = total[:, 2048:]


def body(
    tokens,
    ln1_gain,
    ln1_bias,
    qkv_weight,
    qv_bias,
    proj_weight,
    proj_bias,
    ln2_gain,
    ln2_bias,
    fc_weight,
    fc_bias,
    out_weight,
    out_bias,
    piece_starts,
    seq_lengths,
    cotangent,
):
    vectors = (ln1_gain, ln1_bias, proj_bias, ln2_gain, ln2_bias, out_bias)
    pay_q = call(
        prepare_kernel,
        "weights_payload",
        shape(32, 16, 1664),
        qkv_weight.transpose(1, 0, 2),
        *[v.reshape(1, 16) for v in vectors],
    )
    own_q = exchange(pay_q, SPREAD).reshape(512, 1664)
    proj_rows = proj_weight.T
    pay_r = call(
        prepare_rest_kernel,
        "rest_payload",
        shape(16, 4608),
        *[far(x) for x in (proj_rows, fc_weight, out_weight.T)],
    )
    pair_r = call(
        pair_kernel,
        "rest_pair",
        shape(32, 5120),
        after(pay_r, pay_q),
        swap(pay_r, "zh"),
        swap(proj_rows, "tp"),
        lax.ppermute(proj_rows, ("zh", "tp"), [(i, 3 - i) for i in range(4)]),
    )
    rest = lax.all_gather(pair_r, ("x", "c", "y"), axis=0, tiled=True)

    inputs, grad_mlp = call(
        inputs_kernel,
        "inputs",
        (shape(256, 1024), shape(256, 1024)),
        seq_lengths,
        tokens[0],
        cotangent[0],
        scalars=1,
        cost=300,
        scratch=[pltpu.VMEM((1024, 1024), bf16)],
    )
    own_q = after(own_q, inputs)
    other_q = swap(own_q, "c")
    heads, own_n, other_n, vectors = call(
        qkv_kernel,
        "qkv",
        (shape(8, 192, 256), shape(256, 512), shape(256, 512), shape(8, 1024, kind=f32)),
        inputs,
        own_q,
        other_q,
        qv_bias,
        scratch=[pltpu.VMEM((256, 1024), bf16)],
        cost=3,
    )
    own = exchange(heads, LINE)
    other = swap(own[:, 64:], "c")
    attended, attended_low, log_sum = attn_forward(seq_lengths, piece_starts, own, other)
    heads_all = exchange(attended_low.reshape(16, 64, 256), ("zh", "y", "tp"))
    staged = attn_stage(own, other, log_sum)
    grad_act = grad_activated(grad_mlp, after(rest, attended_low))
    middle, normed_two, heads_out = attention_end(
        after(heads_all, staged[0], grad_act), rest, inputs, vectors
    )
    activated, grad_hidden, two_part = feed_forward(
        normed_two, grad_act, fc_bias.reshape(1, 2048), rest
    )
    two_swapped = swap(two_part, "tp")
    wide, mlp_part = wide_grads(normed_two, grad_hidden, grad_mlp, activated, rest)
    wide = lax.psum_scatter(
        after(wide, two_swapped), ("x", "c"), scatter_dimension=0, tiled=True
    )
    two_swapped = after(two_swapped, mlp_part)
    grad_middle, grad_attn, grad_heads, rows = middle_back(
        middle, two_part, two_swapped, vectors, grad_mlp, rest
    )
    grad_mine = exchange(grad_heads, LINE)

    mine_p, theirs_p = call(
        side_kernel,
        "proj_grads",
        (shape(512, 640), shape(512, 640)),
        far(grad_attn),
        far(heads_out),
        rows,
        cost=2,
    )
    grad_mine = after(grad_mine, mine_p)
    theirs_p = swap(after(theirs_p, grad_mine), "c")
    mlp_swapped = swap(after(mlp_part, grad_mine), "tp")

    grad_query, grad_own, grad_other = attn_backward(
        seq_lengths, piece_starts, staged, grad_mine, attended
    )
    grad_other, mlp_swapped = lax.optimization_barrier((grad_other, mlp_swapped))
    grad_back = call(
        merge_kernel, "merge", shape(8, 192, 256), grad_query, grad_own, swap(grad_other, "c")
    )
    grad_back = exchange(grad_back, LINE)
    layer_out, roots = call(
        final_kernel,
        "final",
        (shape(256, 1024), shape(1, 128, kind=f32)),
        seq_lengths,
        far(inputs),
        far(middle),
        after(mlp_part, grad_other),
        mlp_swapped,
        vectors,
        scalars=1,
        cost=3,
        scratch=[pltpu.VMEM((1024, 1024), bf16)],
    )
    one_keep, one_send, rows, theirs_q, grads, sums = call(
        back_kernel,
        "back",
        (
            shape(128, 1024),
            shape(128, 1024),
            shape(8, 512, kind=f32),
            shape(512, 1920),
            shape(1536, 256),
            shape(2, 16, 128),
        ),
        grad_back,
        far(own_q),
        far(other_q),
        far(inputs),
        far(other_n),
        roots,
        far(grad_hidden),
        cost=5,
        scratch=[pltpu.VMEM((256, 1024), f32), pltpu.VMEM((256, 1024), bf16)],
    )
    one_swapped = swap(one_send, "tp")
    wide = lax.psum_scatter(after(wide, roots), "y", scatter_dimension=0, tiled=True)
    both = core_add(
        grads,
        own_n,
        sums,
        after(swap(theirs_q, "c"), one_swapped),
        mine_p,
        theirs_p,
        rows,
    )
    got_q = exchange(both.reshape(32, 16, 2432), SPREAD)
    half_tokens = call(
        end_kernel,
        "end",
        shape(128, 1024),
        far(inputs),
        far(grad_middle),
        one_keep,
        one_swapped,
        vectors,
        cost=2,
        scratch=[pltpu.VMEM((1024, 1024), bf16)],
    )
    half_swapped = swap(half_tokens, "tp")
    zh = lax.axis_index("zh")
    keep = lax.dynamic_slice_in_dim(wide, zh * 16, 16, 0)
    send = lax.dynamic_slice_in_dim(wide, 16 - zh * 16, 16, 0)
    grad_fc, grad_out = call(
        total_wide_kernel,
        "total_wide",
        (shape(16, 2048, kind=f32), shape(16, 2048, kind=f32)),
        keep,
        swap(send, "zh"),        cost=14,
    )
    got_q = after(got_q, grad_fc, half_swapped)
    cols = total_cols(got_q)
    ln1 = cols[4:6]
    grad_qkv, grad_proj, bias_sums, fc_sums, roots = call(
        total_qkv_kernel,
        "total_qkv",
        (
            shape(3, 16, 512, kind=f32),
            shape(16, 512, kind=f32),
            shape(2, 512, kind=f32),
            shape(16, 128, kind=f32),
            shape(1, 128, kind=f32),
        ),
        seq_lengths,
        after(got_q, cols),
        scalars=1,
    )
    ln1_swapped = swap(ln1, "tp")
    half_swapped = after(half_swapped, grad_qkv)
    grad_tokens = call(
        join_kernel, "join", shape(256, 1024), half_tokens, half_swapped
    )
    ln1 = ln1 + ln1_swapped
    return (
        layer_out[None],
        grad_tokens[None],
        ln1[0],
        ln1[1],
        grad_qkv.transpose(1, 0, 2),
        bias_sums,
        grad_proj.T,
        cols[0],
        cols[1],
        cols[2],
        grad_fc,
        fc_sums.reshape(2048),
        grad_out.T,
        cols[3],
        roots[0, :4],
    )


def solution(mesh):
    fine = Mesh(mesh.devices.reshape(4, 2, 4, 2, 2), ("x", "zh", "y", "c", "tp"))
    ctx = ("zh", "y", "c")
    every = ("x", "zh", "y", "c")
    in_specs = (
        P("x", ctx, None),
        P(every),
        P(every),
        P(every, None, "tp"),
        P(None, "tp"),
        P("tp", every),
        P(every),
        P(every),
        P(every),
        P(every, "tp"),
        P("tp"),
        P("tp", every),
        P(every),
        P("x", None),
        P(),
        P("x", ctx, None),
    )
    out_specs = (
        P("x", ctx, None),
        P("x", ctx, None),
        P(every),
        P(every),
        P(every, None, "tp"),
        P(None, "tp"),
        P("tp", every),
        P(every),
        P(every),
        P(every),
        P(every, "tp"),
        P("tp"),
        P("tp", every),
        P(every),
        P(),
    )
    return jax.shard_map(body, mesh=fine, in_specs=in_specs, out_specs=out_specs, check_vma=False)
```
